512 devices in a mesh: dp: 32 (over x_lo, y, core), tensor: 16 (over x_hi, z).
Axes of the slice: x: 4 (x_hi: 2, x_lo: 2; x = x_hi * 2 + x_lo), y: 8, z: 8, core: 2. Of those that a mesh axis runs over, the one named last changes fastest.
Arguments:
- hidden_rows: bfloat16 [4096, 4096], P(('dp', 'tensor')), may hold values from -3 to 3
- queries: bfloat16 [4096, 8192], P('dp', 'tensor'), may hold values from -8 to 8
- keys: bfloat16 [36864, 2048], P('dp', 'tensor'), may hold values from -8 to 8, as said below
- values: bfloat16 [36864, 2048], P('dp', 'tensor'), may hold values from -6 to 6, as said below
- slab_start: int32 [32], P('dp'), may hold values from 512 to 1024
- out_weight: bfloat16 [8192, 4096], P('tensor', 'dp'), may hold values from -0.1875 to 0.1875
- norm_gain: bfloat16 [4096], replicated, may hold values from 0.5 to 1.5
- route_ids: int32 [4096, 8], P('dp'), may hold values from 0 to 127, as said below
- route_weights: int32 [4096, 8], P('dp'), may hold values from 4096 to 32767
- flight_experts: int32 [4], replicated, may hold values from 0 to 127, as said below
- gate_weight: bfloat16 [4096, 6144], P('dp', 'tensor'), may hold values from -0.09375 to 0.09375
- up_weight: bfloat16 [4096, 6144], P('dp', 'tensor'), may hold values from -0.09375 to 0.09375
- down_weight: bfloat16 [6144, 4096], P('tensor', 'dp'), may hold values from -0.3125 to 0.3125
Outputs:
- mixed: bfloat16 [4096, 4096], P(('dp', 'tensor'))
The draws below stay inside these ranges and needn't reach their ends.
Inputs may be any that keep to these rules, and one draw needn't show every extreme that they name: Column blocks t and u of keys are equal where t // 4 == u // 4. Column blocks t and u of values are equal where t // 4 == u // 4. `flight_experts`: 4 different expert numbers. `route_ids`: each row names 8 different experts. In the 8 rows of one tensor index (aligned blocks of each slab), each expert of flight_experts is named by at most 4 rows; in every slab some expert of flight_experts is named by exactly 4 rows in every block. `route_weights`: gate weights in units of 1/65536.
All inputs are finite; a program needn't handle non-finite values.
Results may differ from the reference program's by a relative error of at most 0.022.
Values may be sent and summed in bfloat16 or wider, within the bound.
No kernel may reach another device: no remote copies, remote signals or barrier semaphores. Data moves between devices by JAX's collectives and lax.ppermute only.
A program may use at most 64 MiB of HBM per device.

```python
import jax
import jax.numpy as jnp
from jax import lax

D = 4096
HEADS = 64
HD = 128
KV_HEADS = 4
EXPERTS = 128
TOPK = 8
FF = 1536
SLAB = 128
PREFIX = 1024
FLIGHT = 4
CTX = 1152
HEADS_DEV = 4
COPIES = 4
HID_DEV = 384
GROUP = 4
CAP = 4
N_DP = 32
N_TENSOR = 16


def flight_plan(base_key):
    key = jax.random.fold_in(base_key, 101)
    middle = jax.random.permutation(key, EXPERTS - 2)[:FLIGHT - 2].astype(jnp.int32) + 1
    listed = jnp.concatenate([jnp.array([0, EXPERTS - 1], jnp.int32), middle])
    order = jax.random.permutation(jax.random.fold_in(key, 1), FLIGHT)
    return listed[order].astype(jnp.int32)


def draw_queries(key, part):
    key = jax.random.fold_in(key, 3)
    drawn = jnp.clip(1.7 * jax.random.normal(key, (N_DP, SLAB, HEADS, HD), jnp.float32), -8.0, 8.0)
    return drawn.reshape(N_DP * SLAB, HEADS * HD).astype(jnp.bfloat16)


def draw_keys(key, part):
    key = jax.random.fold_in(key, 5)
    drawn = jnp.clip(1.7 * jax.random.normal(key, (N_DP, CTX, KV_HEADS, HD), jnp.float32), -8.0, 8.0)
    drawn = jnp.repeat(drawn, COPIES, axis=2)
    return drawn.reshape(N_DP * CTX, KV_HEADS * COPIES * HD).astype(jnp.bfloat16)


def draw_values(key, part):
    key = jax.random.fold_in(key, 7)
    drawn = jnp.clip(jax.random.normal(key, (N_DP, CTX, KV_HEADS, HD), jnp.float32), -6.0, 6.0)
    drawn = jnp.repeat(drawn, COPIES, axis=2)
    return drawn.reshape(N_DP * CTX, KV_HEADS * COPIES * HD).astype(jnp.bfloat16)


def draw_slab_start(key, part):
    key = jax.random.fold_in(key, 9)
    offsets = jax.random.randint(key, (N_DP,), PREFIX // 2, PREFIX + 1, dtype=jnp.int32)
    chosen = jax.random.randint(jax.random.fold_in(key, 1), (), 0, N_DP, dtype=jnp.int32)
    return offsets.at[chosen].set(PREFIX).astype(jnp.int32)


def draw_flight_experts(key, part):
    return flight_plan(key)


def draw_route_ids(key, part):
    flights = flight_plan(key)
    key = jax.random.fold_in(key, 13)
    rows_dev = SLAB // N_TENSOR
    most = min(4, rows_dev)
    blocks = N_DP * N_TENSOR
    all_rows = N_DP * SLAB
    subkeys = jax.random.split(key, 5)
    counts = jax.random.randint(subkeys[0], (blocks, FLIGHT), most - most // 2, most + 1, dtype=jnp.int32)
    full_slot = jnp.repeat(jax.random.randint(subkeys[1], (N_DP,), 0, FLIGHT, dtype=jnp.int32), N_TENSOR)
    counts = jnp.where(jnp.arange(FLIGHT, dtype=jnp.int32)[None, :] == full_slot[:, None], most, counts)
    raw = jax.random.randint(subkeys[2], (blocks, FLIGHT, rows_dev), 0, 65536, dtype=jnp.int32) * rows_dev + jnp.arange(rows_dev, dtype=jnp.int32)
    ranking = jnp.argsort(jnp.argsort(raw, axis=2), axis=2).astype(jnp.int32)
    picked = (ranking < counts[:, :, None]).transpose(0, 2, 1).reshape(all_rows, FLIGHT)
    others_count = EXPERTS - FLIGHT
    scores = jax.random.randint(subkeys[3], (all_rows, others_count), 0, 65536, dtype=jnp.int32) * 256 + jnp.arange(others_count, dtype=jnp.int32)
    chosen = jax.lax.top_k(scores, TOPK)[1].astype(jnp.int32)
    ordered = jnp.sort(flights)
    for slot in range(FLIGHT):
        chosen = chosen + (chosen >= ordered[slot]).astype(jnp.int32)
    for slot in range(FLIGHT):
        chosen = chosen.at[:, slot].set(jnp.where(picked[:, slot], flights[slot], chosen[:, slot]))
    mixing = jax.random.randint(subkeys[4], (all_rows, TOPK), 0, 65536, dtype=jnp.int32) * TOPK + jnp.arange(TOPK, dtype=jnp.int32)
    shuffle = jnp.argsort(mixing, axis=1)
    return jnp.take_along_axis(chosen, shuffle, axis=1).astype(jnp.int32)


def plant(values, key, smallest, high):
    dims = values.shape
    spot = [jax.random.randint(jax.random.fold_in(key, axis), (), 0, dims[axis]) for axis in range(len(dims))]
    values = values.at[tuple(spot)].set(smallest)
    longest = dims.index(max(dims))
    spot[longest] = (spot[longest] + 1) % dims[longest]
    return values.at[tuple(spot)].set(high)


def block_scale(key, dims, pieces, low, high):
    gain, own = 1.0, jax.random.fold_in(key, 6)
    for axis_at, shards_of in pieces:
        steps = jnp.exp(jax.random.uniform(jax.random.fold_in(own, axis_at), (shards_of,), jnp.float32, low / len(pieces), high / len(pieces)))
        gain = gain * jnp.repeat(steps, dims[axis_at] // shards_of).reshape([-1 if axis == axis_at else 1 for axis in range(len(dims))])
    return gain


def centred(own_key, extent, spread, most, cuts=(), held_as=jnp.bfloat16):
    factor_of = block_scale(own_key, extent, cuts, -0.22, 0.18) if cuts else 1.0
    values = jax.random.normal(own_key, extent, jnp.float32) * spread * factor_of
    return jnp.minimum(jnp.maximum(values, -most), most).astype(held_as)


def setup_inputs(seed: int = 0) -> dict:
    splits = jax.random.split(jax.random.key(seed), 14)
    return {
        "hidden_rows": centred(splits[0], (N_DP * SLAB, D), 0.5, 3.0, ((0, 512),)),
        "queries": draw_queries(jax.random.fold_in(splits[13], 71), 0),
        "keys": draw_keys(jax.random.fold_in(splits[13], 71), 0),
        "values": draw_values(jax.random.fold_in(splits[13], 71), 0),
        "slab_start": draw_slab_start(jax.random.fold_in(splits[13], 71), 0),
        "out_weight": centred(splits[5], (HEADS * HD, D), (HD * 8) ** -0.5, 0.1875, ((0, 16), (1, 32))),
        "norm_gain": jnp.clip(1.0 + 0.1 * jax.random.normal(splits[6], (D,), jnp.float32), 0.5, 1.5).astype(jnp.bfloat16),
        "route_ids": draw_route_ids(jax.random.fold_in(splits[13], 71), 0),
        "route_weights": plant(jax.random.randint(splits[8], (N_DP * SLAB, TOPK), 4096, 32768), jax.random.fold_in(splits[8], 1), 4096, 32767).astype(jnp.int32),
        "flight_experts": draw_flight_experts(jax.random.fold_in(splits[13], 71), 0),
        "gate_weight": centred(splits[10], (D, FLIGHT * FF), D ** -0.5, 0.09375, ((0, 32), (1, 16))),
        "up_weight": centred(splits[11], (D, FLIGHT * FF), D ** -0.5, 0.09375, ((0, 32), (1, 16))),
        "down_weight": centred(splits[12], (FLIGHT * FF, D), (FF // 4) ** -0.5, 0.3125, ((0, 16), (1, 32))),
    }


def attend(q_dev, keys_dev, values_dev, first_pos):
    slab_rows = q_dev.shape[0]
    head_size = keys_dev.shape[1]
    head_count = q_dev.shape[1] // head_size
    pair_count = head_count // 2
    grouped = q_dev.reshape(slab_rows, pair_count, 2, head_size).transpose(1, 2, 0, 3).reshape(pair_count, 2 * slab_rows, head_size)
    position = first_pos + jnp.arange(2 * slab_rows, dtype=jnp.int32) % slab_rows
    visible = jnp.arange(keys_dev.shape[0], dtype=jnp.int32)[None, :] <= position[:, None]

    def one_pair(q_block):
        scores = lax.dot_general(q_block, keys_dev, (((1,), (1,)), ((), ())), preferred_element_type=jnp.float32) * head_size ** (-0.5)
        scores = jnp.where(visible, scores, -1e+30)
        maxima = lax.optimization_barrier(jnp.max(scores, axis=1, keepdims=True))
        exp_scores = jnp.exp(scores - maxima)
        totals = lax.optimization_barrier(jnp.sum(exp_scores, axis=1, keepdims=True))
        context = jnp.dot(exp_scores.astype(jnp.bfloat16), values_dev, preferred_element_type=jnp.float32) / totals
        return context.astype(jnp.bfloat16)
    result = lax.map(one_pair, grouped)
    return result.reshape(pair_count, 2, slab_rows, head_size).transpose(2, 0, 1, 3).reshape(slab_rows, head_count * head_size)

def rms_norm(residual, norm_gain):
    values32 = residual.astype(jnp.float32)
    inverse = lax.rsqrt(lax.optimization_barrier(jnp.mean(values32 * values32, axis=1, keepdims=True)) + 1e-06)
    return (values32 * inverse * norm_gain.astype(jnp.float32)).astype(jnp.bfloat16)

def reference(hidden_rows, queries, keys, values, slab_start, out_weight, norm_gain, route_ids, route_weights, flight_experts, gate_weight, up_weight, down_weight):
    q_all = queries.reshape(N_DP, SLAB, N_TENSOR, HEADS_DEV * HD).transpose(0, 2, 1, 3)
    k_all = keys.reshape(N_DP, CTX, N_TENSOR, HD).transpose(0, 2, 1, 3)
    v_all = values.reshape(N_DP, CTX, N_TENSOR, HD).transpose(0, 2, 1, 3)
    wo_all = out_weight.reshape(N_TENSOR, HEADS_DEV * HD, D)

    def one_slab(inputs):
        q_slab, k_slab, v_slab, first_pos = inputs

        def one_device(parts):
            q_dev, k_dev, v_dev, w_dev = parts
            context = attend(q_dev, k_dev, v_dev, first_pos)
            partial_sum = jnp.dot(context, w_dev, preferred_element_type=jnp.float32).astype(jnp.bfloat16)
            return lax.optimization_barrier(partial_sum)
        head_parts = lax.map(one_device, (q_slab, k_slab, v_slab, wo_all))
        return lax.optimization_barrier(jnp.sum(head_parts.astype(jnp.float32), axis=0))
    attention = lax.map(one_slab, (q_all, k_all, v_all, slab_start)).reshape(N_DP * SLAB, D)
    residual = (hidden_rows.astype(jnp.float32) + attention).astype(jnp.bfloat16)
    normed = rms_norm(residual, norm_gain)
    matches = route_ids[:, None, :] == flight_experts[None, :, None]
    hits = lax.optimization_barrier(jnp.sum(matches.astype(jnp.int32), axis=2, dtype=jnp.int32))
    gate_coef = lax.optimization_barrier(jnp.sum(jnp.where(matches, route_weights[:, None, :], 0), axis=2, dtype=jnp.int32)).astype(jnp.float32) / 65536.0
    limit = N_DP * N_TENSOR * CAP
    gate_cols = gate_weight.reshape(D, N_TENSOR, HID_DEV).transpose(1, 0, 2)
    up_cols = up_weight.reshape(D, N_TENSOR, HID_DEV).transpose(1, 0, 2)
    down_rows = down_weight.reshape(N_TENSOR, HID_DEV, D)
    expert_sum = jnp.zeros((N_DP * SLAB, D), jnp.float32)
    for expert_slot in range(FLIGHT):
        order = jnp.argsort(1 - hits[:, expert_slot], stable=True)[:limit].astype(jnp.int32)
        chosen = jnp.take(normed, order, axis=0)

        def one_slice(parts):
            w_gate, w_up, w_down = parts
            gate_pre = jnp.dot(chosen, w_gate, preferred_element_type=jnp.float32)
            up_pre = jnp.dot(chosen, w_up, preferred_element_type=jnp.float32)
            activated = (jax.nn.silu(gate_pre) * up_pre).astype(jnp.bfloat16)
            return lax.optimization_barrier(jnp.dot(activated, w_down, preferred_element_type=jnp.float32).astype(jnp.bfloat16))
        first = expert_slot * GROUP
        slice_parts = lax.map(one_slice, (gate_cols[first:first + GROUP], up_cols[first:first + GROUP], down_rows[first:first + GROUP]))
        combined = lax.optimization_barrier(jnp.sum(slice_parts.astype(jnp.float32), axis=0))
        coef = jnp.take(gate_coef[:, expert_slot], order, axis=0)
        expert_sum = expert_sum.at[order].add(coef[:, None] * combined)
    return (residual.astype(jnp.float32) + expert_sum).astype(jnp.bfloat16)
```

```python
import jax
import jax.numpy as jnp
from jax import lax
from jax.experimental import pallas as pl
from jax.experimental.pallas import tpu as pltpu
from jax.sharding import Mesh
from jax.sharding import PartitionSpec as P

DP = ("xl", "y", "core")
TENSOR = ("xh", "z")
RING = 8
FIRST = (0, -1, 1, -2, 2)
SECOND = (-3, 3, 4)
VMEM_BYTES = 48 * 1024 * 1024


def attend(q_dev, keys_dev, values_dev, first_pos):
    slab_rows = q_dev.shape[0]
    head_size = keys_dev.shape[1]
    head_count = q_dev.shape[1] // head_size
    pair_count = head_count // 2
    grouped = (
        q_dev.reshape(slab_rows, pair_count, 2, head_size)
        .transpose(1, 2, 0, 3)
        .reshape(pair_count, 2 * slab_rows, head_size)
    )
    position = first_pos + jnp.arange(2 * slab_rows, dtype=jnp.int32) % slab_rows
    visible = jnp.arange(keys_dev.shape[0], dtype=jnp.int32)[None, :] <= position[:, None]

    def one_pair(q_block):
        scores = lax.dot_general(
            q_block, keys_dev, (((1,), (1,)), ((), ())), preferred_element_type=jnp.float32
        ) * head_size ** (-0.5)
        scores = jnp.where(visible, scores, -1e30)
        maxima = jnp.max(scores, axis=1, keepdims=True)
        exp_scores = jnp.exp(scores - maxima)
        totals = jnp.sum(exp_scores, axis=1, keepdims=True)
        context = (
            jnp.dot(exp_scores.astype(jnp.bfloat16), values_dev, preferred_element_type=jnp.float32)
            / totals
        )
        return context.astype(jnp.bfloat16)

    result = lax.map(one_pair, grouped)
    return (
        result.reshape(pair_count, 2, slab_rows, head_size)
        .transpose(2, 0, 1, 3)
        .reshape(slab_rows, head_count * head_size)
    )


def rms_norm(residual, norm_gain):
    values32 = residual.astype(jnp.float32)
    inverse = lax.rsqrt(jnp.mean(values32 * values32, axis=1, keepdims=True) + 1e-06)
    return (values32 * inverse * norm_gain.astype(jnp.float32)).astype(jnp.bfloat16)


def along_y(block, step):
    return lax.ppermute(block, "y", [(i, (i + step) % RING) for i in range(RING)])


def swap(block, axis):
    return lax.ppermute(block, axis, [(0, 1), (1, 0)])


def ring_gather(weight):
    pair = jnp.stack([weight, swap(weight, "xl")])
    up1, down1 = along_y(pair, 1), along_y(pair, -1)
    up2, down2 = along_y(up1, 1), along_y(down1, -1)
    first = jnp.stack([pair, up1, down1, up2, down2])
    up3, down3 = along_y(up2, 1), along_y(down2, -1)
    other_first = swap(first, "core")
    up4, down4 = along_y(up3[:1], 1), along_y(down3[1:], -1)
    second = jnp.stack([up3, down3, jnp.concatenate([up4, down4])])
    other_second = swap(second, "core")
    return first, second, other_first, other_second


def project_kernel(place_ref, context_ref, first_ref, second_ref, other_first_ref, other_second_ref, out_ref):
    xl, y, core = place_ref[0], place_ref[1], place_ref[2]
    context = context_ref[...]
    for blocks_ref, steps, own in (
        (first_ref, FIRST, 0),
        (other_first_ref, FIRST, 1),
        (second_ref, SECOND, 0),
        (other_second_ref, SECOND, 1),
    ):
        for k, step in enumerate(steps):
            for side in range(2):
                chip = (xl ^ side) * RING + ((y + (step + RING)) & (RING - 1))
                column = pl.multiple_of((chip * 2 + (core ^ own)) * 128, 128)
                out_ref[:, pl.ds(column, 128)] = jnp.dot(
                    context, blocks_ref[k, side], preferred_element_type=jnp.float32
                ).astype(out_ref.dtype)


def project(context, blocks, width):
    place = jnp.stack([lax.axis_index("xl"), lax.axis_index("y"), lax.axis_index("core")]).astype(jnp.int32)
    rows = context.shape[0]
    vmem = pl.BlockSpec(memory_space=pltpu.VMEM)
    return pl.pallas_call(
        project_kernel,
        out_shape=jax.ShapeDtypeStruct((rows, width), jnp.bfloat16),
        in_specs=[pl.BlockSpec(memory_space=pltpu.SMEM)] + [vmem] * 5,
        out_specs=vmem,
        compiler_params=pltpu.CompilerParams(vmem_limit_bytes=VMEM_BYTES),
        cost_estimate=pl.CostEstimate(
            flops=2 * rows * context.shape[1] * width,
            bytes_accessed=2 * context.shape[1] * width,
            transcendentals=0,
        ),
        name="project",
    )(place, context, *blocks)


CHUNKS = 8


def expert_kernel(rows_ref, weights_hbm, out_ref, weights, sems):
    width, hidden = rows_ref.shape[1], weights.shape[1] // 3
    part = width // CHUNKS

    def copy(i):
        at = pl.ds(i * part, part)
        return pltpu.make_async_copy(weights_hbm.at[at], weights.at[at], sems.at[i])

    for i in range(CHUNKS):
        copy(i).start()
    total = jnp.zeros((rows_ref.shape[0], 2 * hidden), jnp.float32)
    for i in range(CHUNKS):
        copy(i).wait()
        total += jnp.dot(
            rows_ref[:, i * part : (i + 1) * part],
            weights[i * part : (i + 1) * part, : 2 * hidden],
            preferred_element_type=jnp.float32,
        )
    gate, up = total[:, :hidden], total[:, hidden:]
    activated = (gate / (1.0 + jnp.exp(-gate)) * up).astype(jnp.bfloat16)
    for d in range(width // 128):
        down = jnp.concatenate(
            [
                weights[d * 128 : (d + 1) * 128, 2 * hidden + j * 128 : 2 * hidden + (j + 1) * 128]
                for j in range(hidden // 128)
            ]
        )
        out_ref[:, d * 128 : (d + 1) * 128] = jnp.dot(
            activated, down, preferred_element_type=jnp.float32
        ).astype(out_ref.dtype)


def expert(rows, weights):
    vmem = pl.BlockSpec(memory_space=pltpu.VMEM)
    return pl.pallas_call(
        expert_kernel,
        out_shape=jax.ShapeDtypeStruct(rows.shape, jnp.bfloat16),
        in_specs=[vmem, pl.BlockSpec(memory_space=pl.ANY)],
        out_specs=vmem,
        scratch_shapes=[
            pltpu.VMEM(weights.shape, jnp.bfloat16),
            pltpu.SemaphoreType.DMA((CHUNKS,)),
        ],
        compiler_params=pltpu.CompilerParams(vmem_limit_bytes=VMEM_BYTES),
        cost_estimate=pl.CostEstimate(
            flops=2 * rows.shape[0] * weights.size, bytes_accessed=2 * weights.size, transcendentals=0
        ),
        name="expert",
    )(rows, weights)


def per_device(
    hidden_rows,
    queries,
    keys,
    values,
    slab_start,
    out_weight,
    norm_gain,
    route_ids,
    route_weights,
    flight_experts,
    gate_weight,
    up_weight,
    down_weight,
):
    tensor_idx = lax.axis_index(TENSOR)
    groups = lax.axis_size(TENSOR)
    own_rows = hidden_rows.shape[0]
    width = hidden_rows.shape[1]
    flight = flight_experts.shape[0]
    per_expert = groups // flight
    capacity = min(4, own_rows)
    hidden = gate_weight.shape[1]

    down_wide = down_weight.reshape(hidden // 128, 128, 128).transpose(1, 0, 2).reshape(128, hidden)
    expert_weights = lax.all_gather(
        jnp.concatenate([gate_weight, up_weight, down_wide], axis=1), DP, axis=0, tiled=True
    )
    blocks = ring_gather(out_weight)
    context = attend(queries, keys, values, slab_start[0])

    matches = route_ids[:, None, :] == flight_experts[None, :, None]
    hits = jnp.sum(matches.astype(jnp.int32), axis=2, dtype=jnp.int32).reshape(
        groups, own_rows, flight
    )
    gate_coef = (
        jnp.sum(jnp.where(matches, route_weights[:, None, :], 0), axis=2, dtype=jnp.int32).astype(
            jnp.float32
        )
        / 65536.0
    )
    own_hits = lax.dynamic_index_in_dim(hits, tensor_idx, 0, keepdims=False)
    slot_number = jnp.cumsum(own_hits, axis=0) - 1
    own_place = jnp.logical_and(
        own_hits[..., None] == 1, slot_number[..., None] == jnp.arange(capacity, dtype=jnp.int32)
    )
    own_coef = lax.dynamic_slice_in_dim(gate_coef, tensor_idx * own_rows, own_rows, 0)

    projected = project(context, blocks, width)
    head_parts = lax.all_to_all(
        projected.reshape(groups, own_rows, width), TENSOR, split_axis=0, concat_axis=0, tiled=True
    )
    attention = jnp.sum(head_parts.astype(jnp.float32), axis=0)
    residual = (hidden_rows.astype(jnp.float32) + attention).astype(jnp.bfloat16)
    normed = rms_norm(residual, norm_gain)
    packed = jnp.einsum(
        "rfc,rd->fcd", own_place.astype(jnp.bfloat16), normed, preferred_element_type=jnp.float32
    ).astype(jnp.bfloat16)
    rows_in = lax.all_to_all(
        jnp.repeat(packed, per_expert, axis=0), TENSOR, split_axis=0, concat_axis=0, tiled=True
    )
    expert_out = expert(rows_in.reshape(groups * capacity, width), expert_weights)
    slice_parts = expert_out.reshape(groups, capacity, width)
    returned = lax.all_to_all(slice_parts, TENSOR, split_axis=0, concat_axis=0, tiled=True)
    weighted = own_place.astype(jnp.float32) * own_coef[:, :, None]
    weighted = jnp.repeat(weighted, per_expert, axis=1)
    expert_sum = jnp.einsum(
        "rtc,tcd->rd", weighted, returned.astype(jnp.float32), precision=lax.Precision.HIGHEST
    )
    return (residual.astype(jnp.float32) + expert_sum).astype(jnp.bfloat16)


def solution(mesh):
    fine = Mesh(mesh.devices.reshape(2, RING, 2, 2, 8), DP + TENSOR)
    placed = (
        P(DP + TENSOR, None),
        P(DP, TENSOR),
        P(DP, TENSOR),
        P(DP, TENSOR),
        P(DP),
        P(TENSOR, DP),
        P(),
        P(DP, None),
        P(DP, None),
        P(),
        P(DP, TENSOR),
        P(DP, TENSOR),
        P(TENSOR, DP),
    )
    return jax.shard_map(
        per_device, mesh=fine, in_specs=placed, out_specs=P(DP + TENSOR, None), check_vma=False
    )
```

```python
import jax
import jax.numpy as jnp
from jax import lax
from jax.experimental import pallas as pl
from jax.experimental.pallas import tpu as pltpu
from jax.sharding import Mesh
from jax.sharding import PartitionSpec as P

DP = ("xl", "y", "core")
TENSOR = ("xh", "z")
RING = 8
STEPS = (0, -1, 1, -2, 2, -3, 3)
SLAB = 128
HALF = 2048
COLS = 256
HIDDEN = 384
HEADS_WIDE = 512
CAP = 4
FLIGHT = 4
GROUP = 4
BLOCKS = 16
ROWS = 8
VMEM_BYTES = 48 * 1024 * 1024
F32, BF16 = jnp.float32, jnp.bfloat16


def attend(q_dev, keys_dev, values_dev, first_pos):
    slab_rows = q_dev.shape[0]
    head_size = keys_dev.shape[1]
    head_count = q_dev.shape[1] // head_size
    pair_count = head_count // 2
    grouped = (
        q_dev.reshape(slab_rows, pair_count, 2, head_size)
        .transpose(1, 2, 0, 3)
        .reshape(pair_count, 2 * slab_rows, head_size)
    )
    position = first_pos + jnp.arange(2 * slab_rows, dtype=jnp.int32) % slab_rows
    visible = jnp.arange(keys_dev.shape[0], dtype=jnp.int32)[None, :] <= position[:, None]

    def one_pair(q_block):
        scores = lax.dot_general(
            q_block, keys_dev, (((1,), (1,)), ((), ())), preferred_element_type=jnp.float32
        ) * head_size ** (-0.5)
        scores = jnp.where(visible, scores, -1e30)
        maxima = jnp.max(scores, axis=1, keepdims=True)
        exp_scores = jnp.exp(scores - maxima)
        totals = jnp.sum(exp_scores, axis=1, keepdims=True)
        context = (
            jnp.dot(exp_scores.astype(jnp.bfloat16), values_dev, preferred_element_type=jnp.float32)
            / totals
        )
        return context.astype(jnp.bfloat16)

    result = lax.map(one_pair, grouped)
    return (
        result.reshape(pair_count, 2, slab_rows, head_size)
        .transpose(2, 0, 1, 3)
        .reshape(slab_rows, head_count * head_size)
    )


def swap(block, axis):
    return lax.ppermute(block, axis, [(0, 1), (1, 0)])


def along_z(block, step):
    return lax.ppermute(block, "z", [(i, (i + step) % RING) for i in range(RING)])


def by_slab(own, other, xl):
    return jnp.where(xl == 0, jnp.stack([own, other]), jnp.stack([other, own]))


def kernel_call(body, out_shapes, operands, spaces, flops, moved, name, scratch=()):
    kinds = {
        "v": pl.BlockSpec(memory_space=pltpu.VMEM),
        "s": pl.BlockSpec(memory_space=pltpu.SMEM),
        "h": pl.BlockSpec(memory_space=pl.ANY),
    }
    return pl.pallas_call(
        body,
        out_shape=[jax.ShapeDtypeStruct(shape, dtype) for shape, dtype in out_shapes],
        in_specs=[kinds[s] for s in spaces],
        out_specs=[kinds["v"]] * len(out_shapes),
        scratch_shapes=list(scratch),
        compiler_params=pltpu.CompilerParams(vmem_limit_bytes=VMEM_BYTES),
        cost_estimate=pl.CostEstimate(flops=flops, bytes_accessed=moved, transcendentals=0),
        name=name,
    )(*operands)


def pack_weights_kernel(gate_ref, up_ref, down_ref, out_weight_ref, packed_ref):
    packed_ref[:, :HIDDEN] = gate_ref[...]
    packed_ref[:, HIDDEN : 2 * HIDDEN] = up_ref[...]
    at = 2 * HIDDEN
    for ref in (down_ref, out_weight_ref):
        for j in range(ref.shape[0] // 128):
            packed_ref[:, at : at + 128] = ref[j * 128 : (j + 1) * 128, :]
            at += 128


def project_kernel(place_ref, hidden_ref, *refs):
    contexts, (weights_hbm, keep_ref, send_ref, weights, sems) = refs[:9], refs[9:]
    xh, z = place_ref[3], place_ref[4]

    def copy(k):
        at = pl.ds(k * 2 * 128, 2 * 128)
        return pltpu.make_async_copy(
            weights_hbm.at[at, pl.ds(3 * HIDDEN, HEADS_WIDE)], weights.at[at], sems.at[k]
        )

    for k in range(RING):
        copy(k).start()
    for k in range(RING):
        copy(k).wait()
    total = jnp.zeros((2 * SLAB, COLS), F32)
    for k in range(RING):
        if k < len(STEPS):
            step, context = STEPS[k], contexts[k][...]
        else:
            step, context = 4, jnp.concatenate([contexts[k][...], contexts[k + 1][...]])
        first = pl.multiple_of(((z + (step + RING)) & (RING - 1)) * 256, 256)
        block = weights[pl.ds(first, 256), :]
        for half in range(2):
            rhs = jnp.concatenate(
                [
                    jnp.concatenate([block[:128, q * 128 : (q + 1) * 128], block[128:, q * 128 : (q + 1) * 128]], axis=1)
                    for q in (2 * half, 2 * half + 1)
                ]
            )
            total += jnp.dot(context[:, half * 256 : (half + 1) * 256], rhs, preferred_element_type=F32)
    low, high = total[:SLAB], total[SLAB:]
    keep_ref[...] = jnp.where(xh == 0, low, high) + hidden_ref[...].astype(F32)
    send_ref[...] = jnp.where(xh == 0, high, low).astype(BF16)


def residual_kernel(keep_ref, recv_ref, place_ref, residual_ref, rows_ref):
    residual = (keep_ref[...] + recv_ref[...].astype(F32)).astype(BF16)
    residual_ref[...] = residual
    picked = jnp.dot(place_ref[...], residual, preferred_element_type=F32).astype(BF16)
    per_expert = BLOCKS * CAP
    for f in range(FLIGHT):
        for j in range(GROUP):
            at = (f * GROUP + j) * per_expert
            rows_ref[at : at + per_expert, :] = picked[f * per_expert : (f + 1) * per_expert]


def gate_up_kernel(rows_ref, gain_ref, weights_hbm, own_ref, send_ref, weights, sems):
    part = HALF // RING

    def copy(k):
        at = pl.ds(k * part, part)
        return pltpu.make_async_copy(
            weights_hbm.at[at, pl.ds(0, 2 * HIDDEN)], weights.at[at], sems.at[k]
        )

    for k in range(RING):
        copy(k).start()
    slots = BLOCKS * CAP
    total = jnp.zeros((2 * slots, 2 * HIDDEN), F32)
    squares = jnp.zeros((2 * slots, 1), F32)
    for k in range(RING):
        rows = jnp.concatenate(
            [rows_ref[k * slots : (k + 1) * slots, :], rows_ref[(RING + k) * slots : (RING + k + 1) * slots, :]]
        ).astype(F32)
        squares += jnp.sum(rows * rows, axis=1, keepdims=True)
        scaled = (rows * gain_ref[:, k * part : (k + 1) * part].astype(F32)).astype(BF16)
        copy(k).wait()
        total += jnp.dot(scaled, weights[k * part : (k + 1) * part, :], preferred_element_type=F32)
    own_ref[:, : 2 * HIDDEN] = total
    own_ref[:, 2 * HIDDEN :] = jnp.broadcast_to(squares, (2 * slots, 128))
    send_ref[:, : 2 * HIDDEN] = total.astype(BF16)
    high = squares.astype(BF16)
    rest = squares - high.astype(F32)
    middle = rest.astype(BF16)
    low = (rest - middle.astype(F32)).astype(BF16)
    lane = lax.broadcasted_iota(jnp.int32, (2 * slots, 128), 1)
    tail = jnp.where(lane == 0, high.astype(F32), 0.0)
    tail = jnp.where(lane == 1, middle.astype(F32), tail)
    tail = jnp.where(lane == 2, low.astype(F32), tail)
    send_ref[:, 2 * HIDDEN :] = tail.astype(BF16)


def down_kernel(own_ref, recv_ref, residual_ref, weights_hbm, out_ref, weights, sem):
    copy = pltpu.make_async_copy(weights_hbm.at[:, pl.ds(2 * HIDDEN, HIDDEN)], weights, sem)
    copy.start()
    slots = 2 * BLOCKS * CAP
    other = recv_ref[:, 2 * HIDDEN :].astype(F32)
    squares = own_ref[:, 2 * HIDDEN : 2 * HIDDEN + 1] + jnp.sum(other, axis=1, keepdims=True)
    inverse = lax.rsqrt(squares / (2 * HALF) + 1e-06)
    total = (own_ref[:, : 2 * HIDDEN] + recv_ref[:, : 2 * HIDDEN].astype(F32)) * inverse
    gate, up = total[:, :HIDDEN], total[:, HIDDEN:]
    activated = (gate / (1.0 + jnp.exp(-gate)) * up).astype(BF16)
    to = lax.broadcasted_iota(jnp.int32, (slots, slots), 0)
    source = lax.broadcasted_iota(jnp.int32, (slots, slots), 1)
    wanted = ((to >> 2) & 1) * (BLOCKS * CAP) + (to >> 3) * CAP + (to & 3)
    order = jnp.where(source == wanted, 1.0, 0.0).astype(BF16)
    activated = jnp.dot(order, activated, preferred_element_type=F32).astype(BF16)
    copy.wait()
    for d in range(HALF // 256):
        rhs = jnp.concatenate(
            [
                jnp.concatenate(
                    [
                        weights[(2 * d + e) * 128 : (2 * d + e + 1) * 128, j * 128 : (j + 1) * 128]
                        for j in range(HIDDEN // 128)
                    ]
                )
                for e in range(2)
            ],
            axis=1,
        )
        out_ref[:, d * 256 : (d + 1) * 256] = jnp.dot(
            activated, rhs, preferred_element_type=F32
        ).astype(BF16)
    out_ref[:, HALF:] = residual_ref[...]


def combine_kernel(place_ref, coefs_ref, returned_ref, keep_ref, send_ref):
    xl = place_ref[0]
    coefs = coefs_ref[...]
    high = coefs.astype(BF16)
    rest = coefs - high.astype(F32)
    middle = rest.astype(BF16)
    low = (rest - middle.astype(F32)).astype(BF16)
    slots = BLOCKS * ROWS
    to = lax.broadcasted_iota(jnp.int32, (slots, slots), 0)
    source = lax.broadcasted_iota(jnp.int32, (slots, slots), 1)
    wanted = ((to >> 3) & 1) * (RING * ROWS) + (to >> 4) * ROWS + (to & 7)
    order = jnp.where(source == wanted, 1.0, 0.0).astype(BF16)
    residual = jnp.dot(order, returned_ref[:, HALF:], preferred_element_type=F32)
    for k in range(RING):
        at = slice(k * COLS, (k + 1) * COLS)
        parts = returned_ref[:, at]
        mixed = (
            residual[k * 16 : (k + 1) * 16]
            + jnp.dot(high, parts, preferred_element_type=F32)
            + (
                jnp.dot(middle, parts, preferred_element_type=F32)
                + jnp.dot(low, parts, preferred_element_type=F32)
            )
        )
        keep_ref[:, at] = jnp.where(xl == 0, mixed[:ROWS], mixed[ROWS:]).astype(BF16)
        send_ref[:, at] = jnp.where(xl == 0, mixed[ROWS:], mixed[:ROWS]).astype(BF16)


def per_device(
    hidden_rows,
    queries,
    keys,
    values,
    slab_start,
    out_weight,
    norm_gain,
    route_ids,
    route_weights,
    flight_experts,
    gate_weight,
    up_weight,
    down_weight,
):
    xl, xh = lax.axis_index("xl"), lax.axis_index("xh")
    tensor_idx = lax.axis_index(TENSOR)
    place = jnp.stack([lax.axis_index(a) for a in DP + TENSOR]).astype(jnp.int32)

    swapped = lax.ppermute(
        out_weight, ("y", "z"), [(a * RING + b, b * RING + a) for a in range(RING) for b in range(RING)]
    )
    context = attend(queries, keys, values, slab_start[0])
    swapped, context = lax.optimization_barrier((swapped, context))
    (packed,) = kernel_call(
        pack_weights_kernel,
        [((128, 3 * HIDDEN + HEADS_WIDE), BF16)],
        (gate_weight, up_weight, down_weight, swapped),
        "vvvv",
        0,
        4 * 128 * 1664,
        "pack_weights",
    )
    weights = lax.all_gather(packed, ("y", "core"), axis=0, tiled=True)

    hidden_own = lax.dynamic_slice(hidden_rows, (0, xl * HALF), (ROWS, HALF))
    hidden_other = swap(lax.dynamic_slice(hidden_rows, (0, (1 - xl) * HALF), (ROWS, HALF)), "xl")
    hidden_both = by_slab(hidden_own, hidden_other, xl)
    hidden_cols = lax.all_to_all(
        hidden_both.reshape(2, ROWS, RING, COLS).transpose(0, 2, 1, 3).reshape(BLOCKS, ROWS, COLS),
        TENSOR,
        split_axis=0,
        concat_axis=0,
        tiled=True,
    ).reshape(SLAB, COLS)

    matches = route_ids[:, None, :] == flight_experts[None, :, None]
    hits = jnp.sum(matches.astype(jnp.int32), axis=2, dtype=jnp.int32)
    units = jnp.sum(jnp.where(matches, route_weights[:, None, :], 0), axis=2, dtype=jnp.int32)
    table = jnp.concatenate([hits, units], axis=1).T
    tables = by_slab(table, swap(table, "xl"), xl)
    tables = tables.transpose(0, 2, 1).reshape(2, BLOCKS, ROWS, 2 * FLIGHT)
    hits, units = tables[..., :FLIGHT], tables[..., FLIGHT:]
    slot = jnp.cumsum(hits, axis=2) - 1
    placing = jnp.logical_and(
        hits[..., None] == 1, slot[..., None] == jnp.arange(CAP, dtype=jnp.int32)
    )
    coef = units.astype(F32) / 65536.0
    here = lax.dynamic_index_in_dim(placing, xh, 0, keepdims=False).astype(BF16)
    same = jnp.eye(BLOCKS, dtype=BF16)
    picker = (
        here.transpose(2, 0, 3, 1)[:, :, :, None, :] * same[None, :, None, :, None]
    ).reshape(FLIGHT * BLOCKS * CAP, SLAB)
    mine = lax.dynamic_index_in_dim(placing, tensor_idx, 1, keepdims=False).astype(F32)
    mine = mine * lax.dynamic_index_in_dim(coef, tensor_idx, 1, keepdims=False)[..., None]
    coefs = mine[:, :, :, None, None, :] * jnp.eye(2, dtype=F32)[:, None, None, None, :, None]
    coefs = jnp.broadcast_to(coefs, (2, ROWS, FLIGHT, GROUP, 2, CAP)).reshape(
        2 * ROWS, BLOCKS * 2 * CAP
    )

    both = by_slab(context, swap(context, "xl"), xl).reshape(2 * SLAB, HEADS_WIDE)
    up1, down1 = along_z(both, 1), along_z(both, -1)
    up2, down2 = along_z(up1, 1), along_z(down1, -1)
    up3, down3 = along_z(up2, 1), along_z(down2, -1)
    up4, down4 = along_z(up3[:SLAB], 1), along_z(down3[SLAB:], -1)

    keep, send = kernel_call(
        project_kernel,
        [((SLAB, COLS), F32), ((SLAB, COLS), BF16)],
        (place, hidden_cols, both, up1, down1, up2, down2, up3, down3, up4, down4, weights),
        "sv" + "v" * 9 + "h",
        2 * 256 * 4096 * 256,
        2 * 2048 * 1024,
        "project",
        [pltpu.VMEM((HALF, HEADS_WIDE), BF16), pltpu.SemaphoreType.DMA((RING,))],
    )
    residual, rows_out = kernel_call(
        residual_kernel,
        [((SLAB, COLS), BF16), ((FLIGHT * GROUP * BLOCKS * CAP, COLS), BF16)],
        (keep, swap(send, "xh"), picker),
        "vvv",
        2 * 256 * 128 * 256,
        1 << 20,
        "residual",
    )
    rows_in = lax.all_to_all(
        rows_out.reshape(BLOCKS, BLOCKS * CAP, COLS), TENSOR, split_axis=0, concat_axis=0, tiled=True
    ).reshape(BLOCKS * BLOCKS * CAP, COLS)
    gain = lax.dynamic_slice(norm_gain, (xl * HALF,), (HALF,)).reshape(1, HALF)
    own, part = kernel_call(
        gate_up_kernel,
        [((2 * BLOCKS * CAP, 2 * HIDDEN + 128), F32), ((2 * BLOCKS * CAP, 2 * HIDDEN + 128), BF16)],
        (rows_in, gain, weights),
        "vvh",
        2 * 128 * 2048 * 768,
        3 << 20,
        "gate_up",
        [pltpu.VMEM((HALF, 2 * HIDDEN), BF16), pltpu.SemaphoreType.DMA((RING,))],
    )
    (outward,) = kernel_call(
        down_kernel,
        [((2 * BLOCKS * CAP, HALF + COLS), BF16)],
        (own, swap(part, "xl"), residual, weights),
        "vvvh",
        2 * 128 * 384 * 2048,
        2 << 20,
        "down",
        [pltpu.VMEM((HALF, HIDDEN), BF16), pltpu.SemaphoreType.DMA],
    )
    returned = lax.all_to_all(
        outward.reshape(BLOCKS, 2 * CAP, HALF + COLS), TENSOR, split_axis=0, concat_axis=0, tiled=True
    ).reshape(BLOCKS * 2 * CAP, HALF + COLS)
    kept, sent = kernel_call(
        combine_kernel,
        [((ROWS, HALF), BF16), ((ROWS, HALF), BF16)],
        (place, coefs, returned),
        "svv",
        2 * 48 * 128 * 2304,
        1 << 20,
        "combine",
    )
    arrived = swap(sent, "xl")
    return jnp.where(
        xl == 0, jnp.concatenate([kept, arrived], axis=1), jnp.concatenate([arrived, kept], axis=1)
    )


def solution(mesh):
    fine = Mesh(mesh.devices.reshape(2, RING, 2, 2, RING), DP + TENSOR)
    placed = (
        P(DP + TENSOR, None),
        P(DP, TENSOR),
        P(DP, TENSOR),
        P(DP, TENSOR),
        P(DP),
        P(TENSOR, DP),
        P(),
        P(DP, None),
        P(DP, None),
        P(),
        P(DP, TENSOR),
        P(DP, TENSOR),
        P(TENSOR, DP),
    )
    return jax.shard_map(
        per_device, mesh=fine, in_specs=placed, out_specs=P(DP + TENSOR, None), check_vma=False
    )
```

```python
import jax
import jax.numpy as jnp
from jax import lax
from jax.experimental import pallas as pl
from jax.experimental.pallas import tpu as pltpu
from jax.sharding import Mesh
from jax.sharding import PartitionSpec as P

DP = ("xl", "y", "core")
TENSOR = ("xh", "z")
PAIR_TENSOR = ("xl",) + TENSOR
RING = 8
STEPS = (0, -1, 1, -2, 2, -3, 3)
SLAB = 128
HALF = 2048
QUARTER = 1024
COLS = 256
HIDDEN = 384
HEADS_WIDE = 512
CAP = 4
FLIGHT = 4
GROUP = 4
BLOCKS = 16
ROWS = 8
TABLE = 16
VMEM_BYTES = 48 * 1024 * 1024
F32, BF16 = jnp.float32, jnp.bfloat16


def attend(q_dev, keys_dev, values_dev, first_pos):
    slab_rows = q_dev.shape[0]
    head_size = keys_dev.shape[1]
    head_count = q_dev.shape[1] // head_size
    pair_count = head_count // 2
    grouped = (
        q_dev.reshape(slab_rows, pair_count, 2, head_size)
        .transpose(1, 2, 0, 3)
        .reshape(pair_count, 2 * slab_rows, head_size)
    )
    position = first_pos + jnp.arange(2 * slab_rows, dtype=jnp.int32) % slab_rows
    visible = jnp.arange(keys_dev.shape[0], dtype=jnp.int32)[None, :] <= position[:, None]

    def one_pair(q_block):
        scores = lax.dot_general(
            q_block, keys_dev, (((1,), (1,)), ((), ())), preferred_element_type=jnp.float32
        ) * head_size ** (-0.5)
        scores = jnp.where(visible, scores, -1e30)
        maxima = jnp.max(scores, axis=1, keepdims=True)
        exp_scores = jnp.exp(scores - maxima)
        totals = jnp.sum(exp_scores, axis=1, keepdims=True)
        context = (
            jnp.dot(exp_scores.astype(jnp.bfloat16), values_dev, preferred_element_type=jnp.float32)
            / totals
        )
        return context.astype(jnp.bfloat16)

    result = lax.map(one_pair, grouped)
    return (
        result.reshape(pair_count, 2, slab_rows, head_size)
        .transpose(2, 0, 1, 3)
        .reshape(slab_rows, head_count * head_size)
    )


def swap(block, axis):
    return lax.ppermute(block, axis, [(0, 1), (1, 0)])


def along_z(block, step):
    return lax.ppermute(block, "z", [(i, (i + step) % RING) for i in range(RING)])


def by_slab(own, other, xl):
    return jnp.where(xl == 0, jnp.stack([own, other]), jnp.stack([other, own]))


def kernel_call(body, out_shapes, operands, spaces, flops, moved, name, scratch=()):
    kinds = {
        "v": pl.BlockSpec(memory_space=pltpu.VMEM),
        "s": pl.BlockSpec(memory_space=pltpu.SMEM),
        "h": pl.BlockSpec(memory_space=pl.ANY),
    }
    return pl.pallas_call(
        body,
        out_shape=[jax.ShapeDtypeStruct(shape, dtype) for shape, dtype in out_shapes],
        in_specs=[kinds[s] for s in spaces],
        out_specs=[kinds["v"]] * len(out_shapes),
        scratch_shapes=list(scratch),
        compiler_params=pltpu.CompilerParams(vmem_limit_bytes=VMEM_BYTES),
        cost_estimate=pl.CostEstimate(flops=flops, bytes_accessed=moved, transcendentals=0),
        name=name,
    )(*operands)


def pack_weights_kernel(gate_ref, up_ref, down_ref, out_weight_ref, packed_ref):
    packed_ref[:, :HIDDEN] = gate_ref[...]
    packed_ref[:, HIDDEN : 2 * HIDDEN] = up_ref[...]
    at = 2 * HIDDEN
    for ref in (down_ref, out_weight_ref):
        for j in range(ref.shape[0] // 128):
            packed_ref[:, at : at + 128] = ref[j * 128 : (j + 1) * 128, :]
            at += 128


def project_kernel(place_ref, hidden_ref, *refs):
    contexts, (weights_hbm, keep_ref, send_ref, weights, sems) = refs[:9], refs[9:]
    xh, z = place_ref[3], place_ref[4]

    def copy(k):
        at = pl.ds(k * 2 * 128, 2 * 128)
        return pltpu.make_async_copy(
            weights_hbm.at[at, pl.ds(3 * HIDDEN, HEADS_WIDE)], weights.at[at], sems.at[k]
        )

    for k in range(RING):
        copy(k).start()
    for k in range(RING):
        copy(k).wait()
    total = jnp.zeros((2 * SLAB, COLS), F32)
    for k in range(RING):
        if k < len(STEPS):
            step, context = STEPS[k], contexts[k][...]
        else:
            step, context = 4, jnp.concatenate([contexts[k][...], contexts[k + 1][...]])
        first = pl.multiple_of(((z + (step + RING)) & (RING - 1)) * 256, 256)
        block = weights[pl.ds(first, 256), :]
        for half in range(2):
            rhs = jnp.concatenate(
                [
                    jnp.concatenate([block[:128, q * 128 : (q + 1) * 128], block[128:, q * 128 : (q + 1) * 128]], axis=1)
                    for q in (2 * half, 2 * half + 1)
                ]
            )
            total += jnp.dot(context[:, half * 256 : (half + 1) * 256], rhs, preferred_element_type=F32)
    low, high = total[:SLAB], total[SLAB:]
    keep_ref[...] = jnp.where(xh == 0, low, high) + hidden_ref[...].astype(F32)
    send_ref[...] = jnp.where(xh == 0, high, low).astype(BF16)


def residual_kernel(keep_ref, recv_ref, place_ref, residual_ref, rows_ref):
    residual = (keep_ref[...] + recv_ref[...].astype(F32)).astype(BF16)
    residual_ref[...] = residual
    picked = jnp.dot(place_ref[...], residual, preferred_element_type=F32).astype(BF16)
    per_expert = BLOCKS * CAP
    for f in range(FLIGHT):
        for j in range(GROUP):
            at = (f * GROUP + j) * per_expert
            rows_ref[at : at + per_expert, :] = picked[f * per_expert : (f + 1) * per_expert]


def gate_up_kernel(rows_ref, gain_ref, weights_hbm, own_ref, send_ref, weights, sems):
    part = HALF // RING

    def copy(k):
        at = pl.ds(k * part, part)
        return pltpu.make_async_copy(
            weights_hbm.at[at, pl.ds(0, 2 * HIDDEN)], weights.at[at], sems.at[k]
        )

    for k in range(RING):
        copy(k).start()
    slots = BLOCKS * CAP
    total = jnp.zeros((2 * slots, 2 * HIDDEN), F32)
    squares = jnp.zeros((2 * slots, 1), F32)
    for k in range(RING):
        rows = jnp.concatenate(
            [rows_ref[k * slots : (k + 1) * slots, :], rows_ref[(RING + k) * slots : (RING + k + 1) * slots, :]]
        ).astype(F32)
        squares += jnp.sum(rows * rows, axis=1, keepdims=True)
        scaled = (rows * gain_ref[:, k * part : (k + 1) * part].astype(F32)).astype(BF16)
        copy(k).wait()
        total += jnp.dot(scaled, weights[k * part : (k + 1) * part, :], preferred_element_type=F32)
    own_ref[:, : 2 * HIDDEN] = total
    own_ref[:, 2 * HIDDEN :] = jnp.broadcast_to(squares, (2 * slots, 128))
    send_ref[:, : 2 * HIDDEN] = total.astype(BF16)
    high = squares.astype(BF16)
    rest = squares - high.astype(F32)
    middle = rest.astype(BF16)
    low = (rest - middle.astype(F32)).astype(BF16)
    lane = lax.broadcasted_iota(jnp.int32, (2 * slots, 128), 1)
    tail = jnp.where(lane == 0, high.astype(F32), 0.0)
    tail = jnp.where(lane == 1, middle.astype(F32), tail)
    tail = jnp.where(lane == 2, low.astype(F32), tail)
    send_ref[:, 2 * HIDDEN :] = tail.astype(BF16)


def down_kernel(place_ref, own_ref, recv_ref, residual_ref, weights_hbm, out_ref, weights, sem):
    copy = pltpu.make_async_copy(weights_hbm.at[:, pl.ds(2 * HIDDEN, HIDDEN)], weights, sem)
    copy.start()
    xh = place_ref[3]
    slots = 2 * BLOCKS * CAP
    other = recv_ref[:, 2 * HIDDEN :].astype(F32)
    squares = own_ref[:, 2 * HIDDEN : 2 * HIDDEN + 1] + jnp.sum(other, axis=1, keepdims=True)
    inverse = lax.rsqrt(squares / (2 * HALF) + 1e-06)
    total = (own_ref[:, : 2 * HIDDEN] + recv_ref[:, : 2 * HIDDEN].astype(F32)) * inverse
    gate, up = total[:, :HIDDEN], total[:, HIDDEN:]
    activated = (gate / (1.0 + jnp.exp(-gate)) * up).astype(BF16)
    to = lax.broadcasted_iota(jnp.int32, (2 * slots, slots), 0)
    source = lax.broadcasted_iota(jnp.int32, (2 * slots, slots), 1)
    twice = jnp.where(source == (to >> 3) * CAP + (to & 3), 1.0, 0.0).astype(BF16)
    activated = jnp.dot(twice, activated, preferred_element_type=F32).astype(BF16)
    first = (lax.broadcasted_iota(jnp.int32, (2 * slots, COLS), 0) & 4) == 0

    def columns(d):
        rhs = jnp.concatenate(
            [
                jnp.concatenate(
                    [
                        weights[(2 * d + e) * 128 : (2 * d + e + 1) * 128, j * 128 : (j + 1) * 128]
                        for j in range(HIDDEN // 128)
                    ]
                )
                for e in range(2)
            ],
            axis=1,
        )
        return jnp.dot(activated, rhs, preferred_element_type=F32)

    copy.wait()
    chunks = QUARTER // COLS
    for d in range(chunks):
        out_ref[:, d * COLS : (d + 1) * COLS] = jnp.where(first, columns(d), columns(d + chunks)).astype(BF16)
    residual = residual_ref[...].astype(F32)
    out_ref[:SLAB, QUARTER:] = jnp.where(xh == 0, residual, 0.0).astype(BF16)
    out_ref[SLAB:, QUARTER:] = jnp.where(xh == 1, residual, 0.0).astype(BF16)


def combine_kernel(place_ref, coefs_ref, returned_ref, out_ref):
    xl = place_ref[0]
    coefs = coefs_ref[...]
    high = coefs.astype(BF16)
    rest = coefs - high.astype(F32)
    middle = rest.astype(BF16)
    low = (rest - middle.astype(F32)).astype(BF16)
    rows, slots = 4 * ROWS, 2 * BLOCKS * ROWS
    to = lax.broadcasted_iota(jnp.int32, (rows, slots), 0)
    source = lax.broadcasted_iota(jnp.int32, (rows, slots), 1)
    half, quarter, row = to >> 4, (to >> 3) & 1, to & 7
    for k in range(QUARTER // COLS):
        at = slice(k * COLS, (k + 1) * COLS)
        wanted = (half * BLOCKS + xl * RING + quarter * (RING // 2) + k) * ROWS + row
        picker = jnp.where(source == wanted, 1.0, 0.0).astype(BF16)
        parts = returned_ref[:, at]
        mixed = (
            jnp.dot(picker, returned_ref[:, QUARTER:], preferred_element_type=F32)
            + jnp.dot(high, parts, preferred_element_type=F32)
            + (
                jnp.dot(middle, parts, preferred_element_type=F32)
                + jnp.dot(low, parts, preferred_element_type=F32)
            )
        )
        for q in range(4):
            out_ref[:, q * QUARTER + k * COLS : q * QUARTER + (k + 1) * COLS] = mixed[
                q * ROWS : (q + 1) * ROWS
            ].astype(BF16)


def per_device(
    hidden_rows,
    queries,
    keys,
    values,
    slab_start,
    out_weight,
    norm_gain,
    route_ids,
    route_weights,
    flight_experts,
    gate_weight,
    up_weight,
    down_weight,
):
    xl, xh = lax.axis_index("xl"), lax.axis_index("xh")
    tensor_idx = lax.axis_index(TENSOR)
    place = jnp.stack([lax.axis_index(a) for a in DP + TENSOR]).astype(jnp.int32)

    swapped = lax.ppermute(
        out_weight, ("y", "z"), [(a * RING + b, b * RING + a) for a in range(RING) for b in range(RING)]
    )
    context = attend(queries, keys, values, slab_start[0])
    matches = route_ids[:, None, :] == flight_experts[None, :, None]
    hits = jnp.sum(matches.astype(jnp.int32), axis=2, dtype=jnp.int32)
    units = jnp.sum(jnp.where(matches, route_weights[:, None, :], 0), axis=2, dtype=jnp.int32)

    hit_rows = jnp.pad(hits.T.astype(BF16), ((0, TABLE - FLIGHT), (0, HEADS_WIDE - SLAB)))
    extended = jnp.concatenate([context, hit_rows])
    other = swap(extended, "xl")
    swapped, _ = lax.optimization_barrier((swapped, context))
    (packed,) = kernel_call(
        pack_weights_kernel,
        [((128, 3 * HIDDEN + HEADS_WIDE), BF16)],
        (gate_weight, up_weight, down_weight, swapped),
        "vvvv",
        0,
        4 * 128 * 1664,
        "pack_weights",
    )
    weights = lax.all_gather(packed, ("y", "core"), axis=0, tiled=True)

    slabs = by_slab(extended, other, xl)
    both = slabs[:, :SLAB].reshape(2 * SLAB, HEADS_WIDE)
    up1, down1 = along_z(both, 1), along_z(both, -1)
    up2, down2 = along_z(up1, 1), along_z(down1, -1)
    up3, down3 = along_z(up2, 1), along_z(down2, -1)
    up4, down4 = along_z(up3[:SLAB], 1), along_z(down3[SLAB:], -1)

    hidden_later, _ = lax.optimization_barrier((hidden_rows, up1))
    wanted = jnp.arange(2, dtype=jnp.int32)[None, :, None, None, None] == xl
    hidden_out = jnp.where(
        wanted, hidden_later.reshape(ROWS, 2, 1, RING, COLS).transpose(1, 2, 3, 0, 4), 0
    ).astype(BF16)
    hidden_in = lax.all_to_all(
        hidden_out.reshape(2 * BLOCKS, ROWS, COLS), PAIR_TENSOR, split_axis=0, concat_axis=0, tiled=True
    )
    hidden_cols = lax.dynamic_slice_in_dim(hidden_in, xh * BLOCKS, BLOCKS, 0).reshape(SLAB, COLS)

    hits_here = lax.dynamic_index_in_dim(slabs, xh, 0, keepdims=False)[SLAB : SLAB + FLIGHT, :SLAB]
    hits_here = hits_here.astype(jnp.int32).reshape(FLIGHT, BLOCKS, ROWS)
    slot_here = jnp.cumsum(hits_here, axis=2) - 1
    here = jnp.logical_and(
        hits_here[:, :, None, :] == 1,
        slot_here[:, :, None, :] == jnp.arange(CAP, dtype=jnp.int32)[:, None],
    ).astype(BF16)
    same = jnp.eye(BLOCKS, dtype=BF16)
    picker = (here[:, :, :, None, :] * same[None, :, None, :, None]).reshape(
        FLIGHT * BLOCKS * CAP, SLAB
    )
    hits_mine = lax.dynamic_slice_in_dim(hits, tensor_idx * ROWS, ROWS, 0)
    coef = lax.dynamic_slice_in_dim(units, tensor_idx * ROWS, ROWS, 0).astype(F32) / 65536.0
    slot_mine = jnp.cumsum(hits_mine, axis=0) - 1
    mine = jnp.where(
        jnp.logical_and(
            hits_mine[..., None] == 1, slot_mine[..., None] == jnp.arange(CAP, dtype=jnp.int32)
        ),
        coef[..., None],
        0.0,
    )
    two = jnp.eye(2, dtype=F32)
    coefs = (
        mine[None, None, :, None, :, None, None, :]
        * two[:, None, None, :, None, None, None, None]
        * two[None, :, None, None, None, None, :, None]
    )
    coefs = jnp.broadcast_to(coefs, (2, 2, ROWS, 2, FLIGHT, GROUP, 2, CAP)).reshape(
        4 * ROWS, 2 * BLOCKS * 2 * CAP
    )
    gain = lax.dynamic_slice(norm_gain, (xl * HALF,), (HALF,)).reshape(1, HALF)
    weights, picker, coefs, gain = lax.optimization_barrier((weights, picker, coefs, gain))

    keep, send = kernel_call(
        project_kernel,
        [((SLAB, COLS), F32), ((SLAB, COLS), BF16)],
        (place, hidden_cols, both, up1, down1, up2, down2, up3, down3, up4, down4, weights),
        "sv" + "v" * 9 + "h",
        2 * 256 * 4096 * 256,
        2 * 2048 * 1024,
        "project",
        [pltpu.VMEM((HALF, HEADS_WIDE), BF16), pltpu.SemaphoreType.DMA((RING,))],
    )
    residual, rows_out = kernel_call(
        residual_kernel,
        [((SLAB, COLS), BF16), ((FLIGHT * GROUP * BLOCKS * CAP, COLS), BF16)],
        (keep, swap(send, "xh"), picker),
        "vvv",
        2 * 256 * 128 * 256,
        1 << 20,
        "residual",
    )
    rows_in = lax.all_to_all(
        rows_out.reshape(BLOCKS, BLOCKS * CAP, COLS), TENSOR, split_axis=0, concat_axis=0, tiled=True
    ).reshape(BLOCKS * BLOCKS * CAP, COLS)
    own, part = kernel_call(
        gate_up_kernel,
        [((2 * BLOCKS * CAP, 2 * HIDDEN + 128), F32), ((2 * BLOCKS * CAP, 2 * HIDDEN + 128), BF16)],
        (rows_in, gain, weights),
        "vvh",
        2 * 128 * 2048 * 768,
        3 << 20,
        "gate_up",
        [pltpu.VMEM((HALF, 2 * HIDDEN), BF16), pltpu.SemaphoreType.DMA((RING,))],
    )
    (outward,) = kernel_call(
        down_kernel,
        [((4 * BLOCKS * CAP, QUARTER + COLS), BF16)],
        (place, own, swap(part, "xl"), residual, weights),
        "svvvh",
        2 * 256 * 384 * 2048,
        2 << 20,
        "down",
        [pltpu.VMEM((HALF, HIDDEN), BF16), pltpu.SemaphoreType.DMA],
    )
    returned = lax.all_to_all(
        outward.reshape(2 * BLOCKS, 2 * CAP, QUARTER + COLS),
        PAIR_TENSOR,
        split_axis=0,
        concat_axis=0,
        tiled=True,
    ).reshape(4 * BLOCKS * CAP, QUARTER + COLS)
    (mixed,) = kernel_call(
        combine_kernel,
        [((ROWS, 2 * HALF), BF16)],
        (place, coefs, returned),
        "svv",
        2 * 128 * 256 * 1024,
        1 << 20,
        "combine",
    )
    return mixed


def solution(mesh):
    fine = Mesh(mesh.devices.reshape(2, RING, 2, 2, RING), DP + TENSOR)
    placed = (
        P(DP + TENSOR, None),
        P(DP, TENSOR),
        P(DP, TENSOR),
        P(DP, TENSOR),
        P(DP),
        P(TENSOR, DP),
        P(),
        P(DP, None),
        P(DP, None),
        P(),
        P(DP, TENSOR),
        P(DP, TENSOR),
        P(TENSOR, DP),
    )
    return jax.shard_map(
        per_device, mesh=fine, in_specs=placed, out_specs=P(DP + TENSOR, None), check_vma=False
    )
```

```python
import jax
import jax.numpy as jnp
from jax import lax
from jax.experimental import pallas as pl
from jax.experimental.pallas import tpu as pltpu
from jax.sharding import Mesh
from jax.sharding import PartitionSpec as P

DP = ("xl", "y", "core")
TENSOR = ("xh", "z")
PAIR_TENSOR = ("xl",) + TENSOR
RING = 8
STEPS = (0, -1, 1, -2, 2, -3, 3)
SLAB = 128
HALF = 2048
QUARTER = 1024
COLS = 256
HIDDEN = 384
HEADS_WIDE = 512
CAP = 4
FLIGHT = 4
GROUP = 4
BLOCKS = 16
ROWS = 8
TABLE = 16
VMEM_BYTES = 48 * 1024 * 1024
F32, BF16 = jnp.float32, jnp.bfloat16


def attend_kernel(start_ref, queries_ref, keys_ref, values_ref, hits_ref, out_ref):
    keys, values = keys_ref[...], values_ref[...]
    size = keys.shape[1]
    shape = (2 * SLAB, keys.shape[0])
    position = start_ref[0] + (lax.broadcasted_iota(jnp.int32, shape, 0) & (SLAB - 1))
    visible = lax.broadcasted_iota(jnp.int32, shape, 1) <= position
    for pair in range(HEADS_WIDE // size // 2):
        first, second = (slice((2 * pair + i) * size, (2 * pair + i + 1) * size) for i in range(2))
        block = jnp.concatenate([queries_ref[:, first], queries_ref[:, second]])
        scores = lax.dot_general(
            block, keys, (((1,), (1,)), ((), ())), preferred_element_type=F32
        ) * size ** (-0.5)
        scores = jnp.where(visible, scores, -1e30)
        exp_scores = jnp.exp(scores - jnp.max(scores, axis=1, keepdims=True))
        totals = jnp.sum(exp_scores, axis=1, keepdims=True)
        context = (jnp.dot(exp_scores.astype(BF16), values, preferred_element_type=F32) / totals).astype(BF16)
        out_ref[:SLAB, first] = context[:SLAB]
        out_ref[:SLAB, second] = context[SLAB:]
    out_ref[SLAB:, :] = hits_ref[...]


def swap(block, axis):
    return lax.ppermute(block, axis, [(0, 1), (1, 0)])


def along_z(block, step):
    return lax.ppermute(block, "z", [(i, (i + step) % RING) for i in range(RING)])


def kernel_call(body, out_shapes, operands, spaces, flops, moved, name, scratch=()):
    kinds = {
        "v": pl.BlockSpec(memory_space=pltpu.VMEM),
        "s": pl.BlockSpec(memory_space=pltpu.SMEM),
        "h": pl.BlockSpec(memory_space=pl.ANY),
    }
    return pl.pallas_call(
        body,
        out_shape=[jax.ShapeDtypeStruct(shape, dtype) for shape, dtype in out_shapes],
        in_specs=[kinds[s] for s in spaces],
        out_specs=[kinds["v"]] * len(out_shapes),
        scratch_shapes=list(scratch),
        compiler_params=pltpu.CompilerParams(vmem_limit_bytes=VMEM_BYTES),
        cost_estimate=pl.CostEstimate(flops=flops, bytes_accessed=moved, transcendentals=0),
        name=name,
    )(*operands)


def pack_weights_kernel(gate_ref, up_ref, *refs):
    wide, packed_ref = refs[:-1], refs[-1]
    packed_ref[:, :HIDDEN] = gate_ref[...]
    packed_ref[:, HIDDEN : 2 * HIDDEN] = up_ref[...]
    at = 2 * HIDDEN
    for ref in wide:
        for j in range(ref.shape[0] // 128):
            packed_ref[:, at : at + 128] = ref[j * 128 : (j + 1) * 128, :]
            at += 128


def pack_down_kernel(down_ref, packed_ref):
    for j in range(HIDDEN // 128):
        packed_ref[:, j * 128 : (j + 1) * 128] = down_ref[j * 128 : (j + 1) * 128, :]


def project_kernel(place_ref, *refs):
    contexts, (weights_hbm, keep_ref, send_ref, weights, sems) = refs[:9], refs[9:]
    z = place_ref[4]

    def copy(k):
        at = pl.ds(k * 2 * 128, 2 * 128)
        return pltpu.make_async_copy(
            weights_hbm.at[at, pl.ds(2 * HIDDEN, HEADS_WIDE)], weights.at[at], sems.at[k]
        )

    for k in range(RING):
        copy(k).start()
    for k in range(RING):
        copy(k).wait()
    total = jnp.zeros((2 * SLAB, COLS), F32)
    for k in range(RING):
        if k < len(STEPS):
            step, context = STEPS[k], contexts[k][...]
        else:
            step, context = 4, jnp.concatenate([contexts[k][...], contexts[k + 1][...]])
        for half in range(2):
            first = pl.multiple_of(((z + (step + RING + half * 4)) & (RING - 1)) * 256, 256)
            lanes = slice(half * 256, half * 256 + 256)
            block = weights[pl.ds(first, 256), lanes]
            rhs = jnp.concatenate(
                [
                    jnp.concatenate([block[:128, q * 128 : (q + 1) * 128], block[128:, q * 128 : (q + 1) * 128]], axis=1)
                    for q in range(2)
                ]
            )
            total += jnp.dot(context[:, lanes], rhs, preferred_element_type=F32)
    keep_ref[...] = total
    send_ref[...] = total.astype(BF16)


def residual_kernel(place_ref, keep_ref, recv_ref, hidden_ref, pickers_ref, residual_ref, rows_ref):
    xl, xh = place_ref[0], place_ref[3]
    attention = keep_ref[...] + recv_ref[...].astype(F32)
    own, other = attention[:SLAB], attention[SLAB:]
    per_expert = BLOCKS * CAP
    held = jnp.zeros((SLAB, COLS), F32)
    for slab in range(2):
        at = slice(slab * SLAB, (slab + 1) * SLAB)
        residual = (jnp.where(xl == slab, own, other) + hidden_ref[at, :].astype(F32)).astype(BF16)
        held = jnp.where(xh == slab, residual.astype(F32), held)
        picked = jnp.dot(pickers_ref[at, :], residual, preferred_element_type=F32).astype(BF16)
        for f in range(FLIGHT // 2):
            for j in range(GROUP):
                to = ((f * GROUP + j) * 2 + slab) * per_expert
                rows_ref[to : to + per_expert, :] = picked[f * per_expert : (f + 1) * per_expert]
    residual_ref[...] = held.astype(BF16)


def gate_up_kernel(rows_ref, gain_ref, weights_hbm, own_ref, send_ref, weights, sems):
    part = HALF // RING

    def copy(k):
        at = pl.ds(k * part, part)
        return pltpu.make_async_copy(
            weights_hbm.at[at, pl.ds(0, 2 * HIDDEN)], weights.at[at], sems.at[k]
        )

    for k in range(RING):
        copy(k).start()
    slots = BLOCKS * CAP
    total = jnp.zeros((2 * slots, 2 * HIDDEN), F32)
    squares = jnp.zeros((2 * slots, 1), F32)
    for k in range(RING):
        rows = rows_ref[2 * k * slots : 2 * (k + 1) * slots, :].astype(F32)
        squares += jnp.sum(rows * rows, axis=1, keepdims=True)
        scaled = (rows * gain_ref[:, k * part : (k + 1) * part].astype(F32)).astype(BF16)
        copy(k).wait()
        total += jnp.dot(scaled, weights[k * part : (k + 1) * part, :], preferred_element_type=F32)
    own_ref[:, : 2 * HIDDEN] = total
    own_ref[:, 2 * HIDDEN :] = jnp.broadcast_to(squares, (2 * slots, 128))
    send_ref[:, : 2 * HIDDEN] = total.astype(BF16)
    high = squares.astype(BF16)
    rest = squares - high.astype(F32)
    middle = rest.astype(BF16)
    low = (rest - middle.astype(F32)).astype(BF16)
    lane = lax.broadcasted_iota(jnp.int32, (2 * slots, 128), 1)
    tail = jnp.where(lane == 0, high.astype(F32), 0.0)
    tail = jnp.where(lane == 1, middle.astype(F32), tail)
    tail = jnp.where(lane == 2, low.astype(F32), tail)
    send_ref[:, 2 * HIDDEN :] = tail.astype(BF16)


def down_kernel(place_ref, own_ref, recv_ref, residual_ref, weights_hbm, out_ref, weights, sem):
    copy = pltpu.make_async_copy(weights_hbm, weights, sem)
    copy.start()
    xh = place_ref[3]
    slots = 2 * BLOCKS * CAP
    other = recv_ref[:, 2 * HIDDEN :].astype(F32)
    squares = own_ref[:, 2 * HIDDEN : 2 * HIDDEN + 1] + jnp.sum(other, axis=1, keepdims=True)
    inverse = lax.rsqrt(squares / (2 * HALF) + 1e-06)
    total = (own_ref[:, : 2 * HIDDEN] + recv_ref[:, : 2 * HIDDEN].astype(F32)) * inverse
    gate, up = total[:, :HIDDEN], total[:, HIDDEN:]
    activated = (gate / (1.0 + jnp.exp(-gate)) * up).astype(BF16)
    to = lax.broadcasted_iota(jnp.int32, (2 * slots, slots), 0)
    source = lax.broadcasted_iota(jnp.int32, (2 * slots, slots), 1)
    twice = jnp.where(source == (to >> 3) * CAP + (to & 3), 1.0, 0.0).astype(BF16)
    activated = jnp.dot(twice, activated, preferred_element_type=F32).astype(BF16)
    first = (lax.broadcasted_iota(jnp.int32, (2 * slots, COLS), 0) & 4) == 0

    def columns(d):
        rhs = jnp.concatenate(
            [
                jnp.concatenate(
                    [
                        weights[(2 * d + e) * 128 : (2 * d + e + 1) * 128, j * 128 : (j + 1) * 128]
                        for j in range(HIDDEN // 128)
                    ]
                )
                for e in range(2)
            ],
            axis=1,
        )
        return jnp.dot(activated, rhs, preferred_element_type=F32)

    copy.wait()
    chunks = QUARTER // COLS
    for d in range(chunks):
        out_ref[:, d * COLS : (d + 1) * COLS] = jnp.where(first, columns(d), columns(d + chunks)).astype(BF16)
    residual = residual_ref[...].astype(F32)
    out_ref[:SLAB, QUARTER:] = jnp.where(xh == 0, residual, 0.0).astype(BF16)
    out_ref[SLAB:, QUARTER:] = jnp.where(xh == 1, residual, 0.0).astype(BF16)


def combine_kernel(place_ref, coefs_ref, returned_ref, out_ref):
    xl = place_ref[0]
    coefs = coefs_ref[...]
    high = coefs.astype(BF16)
    rest = coefs - high.astype(F32)
    middle = rest.astype(BF16)
    low = (rest - middle.astype(F32)).astype(BF16)
    rows, slots = 4 * ROWS, 2 * BLOCKS * ROWS
    to = lax.broadcasted_iota(jnp.int32, (rows, slots), 0)
    source = lax.broadcasted_iota(jnp.int32, (rows, slots), 1)
    half, quarter, row = to >> 4, (to >> 3) & 1, to & 7
    for k in range(QUARTER // COLS):
        at = slice(k * COLS, (k + 1) * COLS)
        wanted = (half * BLOCKS + xl * RING + quarter * (RING // 2) + k) * ROWS + row
        picker = jnp.where(source == wanted, 1.0, 0.0).astype(BF16)
        parts = returned_ref[:, at]
        mixed = (
            jnp.dot(picker, returned_ref[:, QUARTER:], preferred_element_type=F32)
            + jnp.dot(high, parts, preferred_element_type=F32)
            + (
                jnp.dot(middle, parts, preferred_element_type=F32)
                + jnp.dot(low, parts, preferred_element_type=F32)
            )
        )
        for q in range(4):
            out_ref[:, q * QUARTER + k * COLS : q * QUARTER + (k + 1) * COLS] = mixed[
                q * ROWS : (q + 1) * ROWS
            ].astype(BF16)


def per_device(
    hidden_rows,
    queries,
    keys,
    values,
    slab_start,
    out_weight,
    norm_gain,
    route_ids,
    route_weights,
    flight_experts,
    gate_weight,
    up_weight,
    down_weight,
):
    xl, xh = lax.axis_index("xl"), lax.axis_index("xh")
    tensor_idx = lax.axis_index(TENSOR)
    place = jnp.stack([lax.axis_index(a) for a in DP + TENSOR]).astype(jnp.int32)

    def transposed(block, shift):
        return lax.ppermute(
            block,
            ("y", "z"),
            [(a * RING + b, (b + shift) % RING * RING + a) for a in range(RING) for b in range(RING)],
        )

    top = transposed(out_weight[: HEADS_WIDE // 2], 0)
    bottom = transposed(out_weight[HEADS_WIDE // 2 :], RING // 2)

    columns = hidden_rows.reshape(ROWS, 2, 1, RING, COLS).transpose(1, 2, 3, 0, 4)
    hidden_out = jnp.broadcast_to(columns, (2, 2, RING, ROWS, COLS)).reshape(2 * BLOCKS, ROWS, COLS)
    hidden_in = lax.all_to_all(
        hidden_out, PAIR_TENSOR, split_axis=0, concat_axis=0, tiled=True
    ).reshape(2 * SLAB, COLS)

    matches = route_ids[:, None, :] == flight_experts[None, :, None]
    hits = jnp.sum(matches.astype(jnp.int32), axis=2, dtype=jnp.int32)
    units = jnp.sum(jnp.where(matches, route_weights[:, None, :], 0), axis=2, dtype=jnp.int32)

    hit_rows = jnp.pad(hits.T.astype(BF16), ((0, TABLE - FLIGHT), (0, HEADS_WIDE - SLAB)))
    (extended,) = kernel_call(
        attend_kernel,
        [((SLAB + TABLE, HEADS_WIDE), BF16)],
        (slab_start, queries, keys, values, hit_rows),
        "svvvv",
        4 * 512 * 1152 * 128,
        1 << 20,
        "attend",
    )
    top, bottom, hidden_in, _ = lax.optimization_barrier((top, bottom, hidden_in, extended))
    (packed,) = kernel_call(
        pack_weights_kernel,
        [((128, 2 * HIDDEN + HEADS_WIDE), BF16)],
        (gate_weight, up_weight, top, bottom),
        "vvvv",
        0,
        4 * 128 * 1280,
        "pack_weights",
    )
    weights = lax.all_gather(packed, ("y", "core"), axis=0, tiled=True)
    (packed_down,) = kernel_call(
        pack_down_kernel, [((128, HIDDEN), BF16)], (down_weight,), "v", 0, 4 * 128 * 384, "pack_down"
    )
    packed_down, _ = lax.optimization_barrier((packed_down, packed))
    down_weights = lax.all_gather(packed_down, ("y", "core"), axis=0, tiled=True)

    other = swap(extended, "xl")
    both = jnp.concatenate([extended[:SLAB], other[:SLAB]])
    up1, down1 = along_z(both, 1), along_z(both, -1)
    up2, down2 = along_z(up1, 1), along_z(down1, -1)
    up3, down3 = along_z(up2, 1), along_z(down2, -1)
    up4, down4 = along_z(up3[:SLAB], 1), along_z(down3[SLAB:], -1)

    hits_both = jnp.where(
        xl == 0, jnp.stack([extended[SLAB:], other[SLAB:]]), jnp.stack([other[SLAB:], extended[SLAB:]])
    )
    hits_here = lax.dynamic_slice(
        hits_both, (0, xh * (FLIGHT // 2), 0), (2, FLIGHT // 2, SLAB)
    )
    hits_here = hits_here.astype(jnp.int32).reshape(2, FLIGHT // 2, BLOCKS, ROWS)
    slot_here = jnp.cumsum(hits_here, axis=3) - 1
    here = jnp.logical_and(
        hits_here[:, :, :, None, :] == 1,
        slot_here[:, :, :, None, :] == jnp.arange(CAP, dtype=jnp.int32)[:, None],
    ).astype(BF16)
    same = jnp.eye(BLOCKS, dtype=BF16)
    pickers = (here[:, :, :, :, None, :] * same[None, None, :, None, :, None]).reshape(
        2 * (FLIGHT // 2) * BLOCKS * CAP, SLAB
    )
    hits_mine = lax.dynamic_slice_in_dim(hits, tensor_idx * ROWS, ROWS, 0)
    coef = lax.dynamic_slice_in_dim(units, tensor_idx * ROWS, ROWS, 0).astype(F32) / 65536.0
    slot_mine = jnp.cumsum(hits_mine, axis=0) - 1
    mine = jnp.where(
        jnp.logical_and(
            hits_mine[..., None] == 1, slot_mine[..., None] == jnp.arange(CAP, dtype=jnp.int32)
        ),
        coef[..., None],
        0.0,
    )
    two = jnp.eye(2, dtype=F32)
    coefs = (
        mine[None, None, :, None, :, None, None, :]
        * two[:, None, None, :, None, None, None, None]
        * two[None, :, None, None, None, None, :, None]
    )
    coefs = jnp.broadcast_to(coefs, (2, 2, ROWS, 2, FLIGHT, GROUP, 2, CAP)).reshape(
        4 * ROWS, 2 * BLOCKS * 2 * CAP
    )
    gain = lax.dynamic_slice(norm_gain, (xl * HALF,), (HALF,)).reshape(1, HALF)
    weights, pickers, coefs, gain = lax.optimization_barrier((weights, pickers, coefs, gain))

    keep, send = kernel_call(
        project_kernel,
        [((2 * SLAB, COLS), F32), ((2 * SLAB, COLS), BF16)],
        (place, both, up1, down1, up2, down2, up3, down3, up4, down4, weights),
        "s" + "v" * 9 + "h",
        2 * 256 * 4096 * 256,
        2 * 2048 * 1024,
        "project",
        [pltpu.VMEM((HALF, HEADS_WIDE), BF16), pltpu.SemaphoreType.DMA((RING,))],
    )
    residual, rows_out = kernel_call(
        residual_kernel,
        [((SLAB, COLS), BF16), ((RING * 2 * BLOCKS * CAP, COLS), BF16)],
        (place, keep, swap(send, "xh"), hidden_in, pickers),
        "svvvv",
        2 * 256 * 128 * 256,
        1 << 20,
        "residual",
    )
    rows_in = lax.all_to_all(
        rows_out.reshape(RING, 2 * BLOCKS * CAP, COLS), "z", split_axis=0, concat_axis=0, tiled=True
    ).reshape(RING * 2 * BLOCKS * CAP, COLS)
    own, part = kernel_call(
        gate_up_kernel,
        [((2 * BLOCKS * CAP, 2 * HIDDEN + 128), F32), ((2 * BLOCKS * CAP, 2 * HIDDEN + 128), BF16)],
        (rows_in, gain, weights),
        "vvh",
        2 * 128 * 2048 * 768,
        3 << 20,
        "gate_up",
        [pltpu.VMEM((HALF, 2 * HIDDEN), BF16), pltpu.SemaphoreType.DMA((RING,))],
    )
    (outward,) = kernel_call(
        down_kernel,
        [((4 * BLOCKS * CAP, QUARTER + COLS), BF16)],
        (place, own, swap(part, "xl"), residual, down_weights),
        "svvvh",
        2 * 256 * 384 * 2048,
        2 << 20,
        "down",
        [pltpu.VMEM((HALF, HIDDEN), BF16), pltpu.SemaphoreType.DMA],
    )
    returned = lax.all_to_all(
        outward.reshape(2 * BLOCKS, 2 * CAP, QUARTER + COLS),
        PAIR_TENSOR,
        split_axis=0,
        concat_axis=0,
        tiled=True,
    ).reshape(4 * BLOCKS * CAP, QUARTER + COLS)
    (mixed,) = kernel_call(
        combine_kernel,
        [((ROWS, 2 * HALF), BF16)],
        (place, coefs, returned),
        "svv",
        2 * 128 * 256 * 1024,
        1 << 20,
        "combine",
    )
    return mixed


def solution(mesh):
    fine = Mesh(mesh.devices.reshape(2, RING, 2, 2, RING), DP + TENSOR)
    placed = (
        P(DP + TENSOR, None),
        P(DP, TENSOR),
        P(DP, TENSOR),
        P(DP, TENSOR),
        P(DP),
        P(TENSOR, DP),
        P(),
        P(DP, None),
        P(DP, None),
        P(),
        P(DP, TENSOR),
        P(DP, TENSOR),
        P(TENSOR, DP),
    )
    return jax.shard_map(
        per_device, mesh=fine, in_specs=placed, out_specs=P(DP + TENSOR, None), check_vma=False
    )
```

```python
import jax
import jax.numpy as jnp
from jax import lax
from jax.experimental import pallas as pl
from jax.experimental.pallas import tpu as pltpu
from jax.sharding import Mesh
from jax.sharding import PartitionSpec as P

DP = ("xl", "y", "core")
TENSOR = ("xh", "z")
PAIR_TENSOR = ("xl",) + TENSOR
RING = 8
STEPS = (0, -1, 1, -2, 2, -3, 3)
SLAB = 128
HALF = 2048
QUARTER = 1024
COLS = 256
HIDDEN = 384
HEADS_WIDE = 512
CAP = 4
FLIGHT = 4
GROUP = 4
BLOCKS = 16
ROWS = 8
TABLE = 16
VMEM_BYTES = 48 * 1024 * 1024
ALL_VMEM_BYTES = 63400000
F32, BF16 = jnp.float32, jnp.bfloat16


def attend_kernel(
    start_ref, flight_ref, ids_hbm, queries_hbm, keys_hbm, values_hbm, out_ref, ids_ref, queries_ref, keys_ref, values_ref, sems
):
    copies = [
        pltpu.make_async_copy(source, target, sems.at[i])
        for i, (source, target) in enumerate(
            ((keys_hbm, keys_ref), (queries_hbm, queries_ref), (values_hbm, values_ref), (ids_hbm, ids_ref))
        )
    ]
    for copy in copies:
        copy.start()
    for copy in copies:
        copy.wait()
    keys, values = keys_ref[...], values_ref[...]
    size = keys.shape[1]
    shape = (2 * SLAB, keys.shape[0])
    position = start_ref[0] + (lax.broadcasted_iota(jnp.int32, shape, 0) & (SLAB - 1))
    visible = lax.broadcasted_iota(jnp.int32, shape, 1) <= position
    for pair in range(HEADS_WIDE // size // 2):
        first, second = (slice((2 * pair + i) * size, (2 * pair + i + 1) * size) for i in range(2))
        block = jnp.concatenate([queries_ref[:, first], queries_ref[:, second]])
        scores = lax.dot_general(
            block, keys, (((1,), (1,)), ((), ())), preferred_element_type=F32
        ) * size ** (-0.5)
        scores = jnp.where(visible, scores, -1e30)
        exp_scores = jnp.exp(scores - jnp.max(scores, axis=1, keepdims=True))
        totals = jnp.sum(exp_scores, axis=1, keepdims=True)
        context = (jnp.dot(exp_scores.astype(BF16), values, preferred_element_type=F32) / totals).astype(BF16)
        out_ref[:SLAB, first] = context[:SLAB]
        out_ref[:SLAB, second] = context[SLAB:]
    line = lax.broadcasted_iota(jnp.int32, (TABLE, SLAB), 0)
    table = jnp.zeros((TABLE, SLAB), F32)
    for f in range(FLIGHT):
        named = jnp.max(jnp.where(ids_ref[...] == flight_ref[f], 1.0, 0.0), axis=0, keepdims=True)
        table = jnp.where(line == f, named, table)
    out_ref[SLAB:, :SLAB] = table.astype(BF16)
    out_ref[SLAB:, SLAB:] = jnp.zeros((TABLE, HEADS_WIDE - SLAB), BF16)


def swap(block, axis):
    return lax.ppermute(block, axis, [(0, 1), (1, 0)])


def along_z(block, step):
    return lax.ppermute(block, "z", [(i, (i + step) % RING) for i in range(RING)])


def kernel_call(body, out_shapes, operands, spaces, flops, moved, name, scratch=(), out_space="v", vmem=VMEM_BYTES):
    kinds = {
        "v": pl.BlockSpec(memory_space=pltpu.VMEM),
        "s": pl.BlockSpec(memory_space=pltpu.SMEM),
        "h": pl.BlockSpec(memory_space=pl.ANY),
    }
    return pl.pallas_call(
        body,
        out_shape=[jax.ShapeDtypeStruct(shape, dtype) for shape, dtype in out_shapes],
        in_specs=[kinds[s] for s in spaces],
        out_specs=[kinds[out_space]] * len(out_shapes),
        scratch_shapes=list(scratch),
        compiler_params=pltpu.CompilerParams(vmem_limit_bytes=vmem),
        cost_estimate=pl.CostEstimate(flops=flops, bytes_accessed=moved, transcendentals=0),
        name=name,
    )(*operands)


def pack_weights_kernel(gate_ref, up_ref, down_ref, swapped_ref, packed_ref, sems):
    pieces = [(gate_ref, HIDDEN), (up_ref, HIDDEN)] + [
        (ref.at[pl.ds(j * 128, 128)], 128)
        for ref in (down_ref, swapped_ref)
        for j in range(ref.shape[0] // 128)
    ]
    copies, at = [], 0
    for i, (piece, lanes) in enumerate(pieces):
        copies.append(pltpu.make_async_copy(piece, packed_ref.at[:, pl.ds(at, lanes)], sems.at[i]))
        at += lanes
    for copy in copies:
        copy.start()
    for copy in copies:
        copy.wait()


def project_kernel(place_ref, hidden_ref, *refs):
    contexts, (weights_hbm, keep_ref, send_ref, weights, sems) = refs[:9], refs[9:]
    xl, xh, z = place_ref[0], place_ref[3], place_ref[4]

    def copy(k):
        at = pl.ds(k * 2 * 128, 2 * 128)
        return pltpu.make_async_copy(
            weights_hbm.at[at, pl.ds(3 * HIDDEN, HEADS_WIDE)], weights.at[at], sems.at[k]
        )

    for k in range(RING):
        copy(k).start()
    for k in range(RING):
        copy(k).wait()
    total = jnp.zeros((2 * SLAB, COLS), F32)
    for k in range(RING):
        if k < len(STEPS):
            step, context = STEPS[k], contexts[k][...]
        else:
            step, context = 4, jnp.concatenate([contexts[k][...], contexts[k + 1][...]])
        first = pl.multiple_of(((z + (step + RING)) & (RING - 1)) * 256, 256)
        for half in range(2):
            lanes = slice(half * 256, half * 256 + 256)
            block = weights[pl.ds(first, 256), lanes]
            rhs = jnp.concatenate(
                [
                    jnp.concatenate([block[:128, q * 128 : (q + 1) * 128], block[128:, q * 128 : (q + 1) * 128]], axis=1)
                    for q in range(2)
                ]
            )
            total += jnp.dot(context[:, lanes], rhs, preferred_element_type=F32)
    hidden = hidden_ref[...].astype(F32)
    rows = SLAB // 2
    own = jnp.where(xl == 0, hidden[:rows], hidden[rows:])
    other = jnp.where(xl == 0, hidden[rows:], hidden[:rows])
    total += jnp.concatenate(
        [jnp.where(xh == at, block, 0.0) for block in (own, other) for at in range(2)]
    )
    keep_ref[...] = total
    send_ref[...] = total.astype(BF16)


def residual_kernel(place_ref, keep_ref, recv_ref, pickers_ref, residual_ref, rows_ref):
    xl, xh = place_ref[0], place_ref[3]
    summed = keep_ref[...] + recv_ref[...].astype(F32)
    own, other = summed[:SLAB], summed[SLAB:]
    per_expert = BLOCKS * CAP
    held = jnp.zeros((SLAB, COLS), F32)
    for slab in range(2):
        at = slice(slab * SLAB, (slab + 1) * SLAB)
        residual = jnp.where(xl == slab, own, other).astype(BF16)
        held = jnp.where(xh == slab, residual.astype(F32), held)
        picked = jnp.dot(pickers_ref[at, :], residual, preferred_element_type=F32).astype(BF16)
        for f in range(FLIGHT // 2):
            for j in range(GROUP):
                to = ((f * GROUP + j) * 2 + slab) * per_expert
                rows_ref[to : to + per_expert, :] = picked[f * per_expert : (f + 1) * per_expert]
    residual_ref[...] = held.astype(BF16)


def gate_up_kernel(rows_ref, gain_ref, weights_hbm, own_ref, send_ref, weights, sems):
    part = HALF // RING

    def copy(k):
        at = pl.ds(k * part, part)
        return pltpu.make_async_copy(
            weights_hbm.at[at, pl.ds(0, 2 * HIDDEN)], weights.at[at], sems.at[k]
        )

    for k in range(RING):
        copy(k).start()
    slots = BLOCKS * CAP
    total = jnp.zeros((2 * slots, 2 * HIDDEN), F32)
    squares = jnp.zeros((2 * slots, 1), F32)
    for k in range(RING):
        rows = rows_ref[2 * k * slots : 2 * (k + 1) * slots, :].astype(F32)
        squares += jnp.sum(rows * rows, axis=1, keepdims=True)
        scaled = (rows * gain_ref[:, k * part : (k + 1) * part].astype(F32)).astype(BF16)
        copy(k).wait()
        total += jnp.dot(scaled, weights[k * part : (k + 1) * part, :], preferred_element_type=F32)
    own_ref[:, : 2 * HIDDEN] = total
    own_ref[:, 2 * HIDDEN :] = jnp.broadcast_to(squares, (2 * slots, 128))
    send_ref[:, : 2 * HIDDEN] = total.astype(BF16)
    high = squares.astype(BF16)
    rest = squares - high.astype(F32)
    middle = rest.astype(BF16)
    low = (rest - middle.astype(F32)).astype(BF16)
    lane = lax.broadcasted_iota(jnp.int32, (2 * slots, 128), 1)
    tail = jnp.where(lane == 0, high.astype(F32), 0.0)
    tail = jnp.where(lane == 1, middle.astype(F32), tail)
    tail = jnp.where(lane == 2, low.astype(F32), tail)
    send_ref[:, 2 * HIDDEN :] = tail.astype(BF16)


def down_kernel(place_ref, own_ref, recv_ref, residual_ref, weights_hbm, out_ref, weights, sem):
    copy = pltpu.make_async_copy(weights_hbm.at[:, pl.ds(2 * HIDDEN, HIDDEN)], weights, sem)
    copy.start()
    xh = place_ref[3]
    slots = 2 * BLOCKS * CAP
    other = recv_ref[:, 2 * HIDDEN :].astype(F32)
    squares = own_ref[:, 2 * HIDDEN : 2 * HIDDEN + 1] + jnp.sum(other, axis=1, keepdims=True)
    inverse = lax.rsqrt(squares / (2 * HALF) + 1e-06)
    total = (own_ref[:, : 2 * HIDDEN] + recv_ref[:, : 2 * HIDDEN].astype(F32)) * inverse
    gate, up = total[:, :HIDDEN], total[:, HIDDEN:]
    activated = (gate / (1.0 + jnp.exp(-gate)) * up).astype(BF16)
    to = lax.broadcasted_iota(jnp.int32, (2 * slots, slots), 0)
    source = lax.broadcasted_iota(jnp.int32, (2 * slots, slots), 1)
    twice = jnp.where(source == (to >> 3) * CAP + (to & 3), 1.0, 0.0).astype(BF16)
    activated = jnp.dot(twice, activated, preferred_element_type=F32).astype(BF16)
    first = (lax.broadcasted_iota(jnp.int32, (2 * slots, COLS), 0) & 4) == 0

    def columns(d):
        rhs = jnp.concatenate(
            [
                jnp.concatenate(
                    [
                        weights[(2 * d + e) * 128 : (2 * d + e + 1) * 128, j * 128 : (j + 1) * 128]
                        for j in range(HIDDEN // 128)
                    ]
                )
                for e in range(2)
            ],
            axis=1,
        )
        return jnp.dot(activated, rhs, preferred_element_type=F32)

    copy.wait()
    chunks = QUARTER // COLS
    for d in range(chunks):
        out_ref[:, d * COLS : (d + 1) * COLS] = jnp.where(first, columns(d), columns(d + chunks)).astype(BF16)
    residual = residual_ref[...].astype(F32)
    out_ref[:SLAB, QUARTER:] = jnp.where(xh == 0, residual, 0.0).astype(BF16)
    out_ref[SLAB:, QUARTER:] = jnp.where(xh == 1, residual, 0.0).astype(BF16)


def combine_kernel(place_ref, coefs_ref, returned_ref, out_ref):
    xl = place_ref[0]
    coefs = coefs_ref[...]
    high = coefs.astype(BF16)
    rest = coefs - high.astype(F32)
    middle = rest.astype(BF16)
    low = (rest - middle.astype(F32)).astype(BF16)
    rows, slots = 4 * ROWS, 2 * BLOCKS * ROWS
    to = lax.broadcasted_iota(jnp.int32, (rows, slots), 0)
    source = lax.broadcasted_iota(jnp.int32, (rows, slots), 1)
    half, quarter, row = to >> 4, (to >> 3) & 1, to & 7
    for k in range(QUARTER // COLS):
        at = slice(k * COLS, (k + 1) * COLS)
        wanted = (half * BLOCKS + xl * RING + quarter * (RING // 2) + k) * ROWS + row
        picker = jnp.where(source == wanted, 1.0, 0.0).astype(BF16)
        parts = returned_ref[:, at]
        mixed = (
            jnp.dot(picker, returned_ref[:, QUARTER:], preferred_element_type=F32)
            + jnp.dot(high, parts, preferred_element_type=F32)
            + (
                jnp.dot(middle, parts, preferred_element_type=F32)
                + jnp.dot(low, parts, preferred_element_type=F32)
            )
        )
        for q in range(4):
            out_ref[:, q * QUARTER + k * COLS : q * QUARTER + (k + 1) * COLS] = mixed[
                q * ROWS : (q + 1) * ROWS
            ].astype(BF16)


def per_device(
    hidden_rows,
    queries,
    keys,
    values,
    slab_start,
    out_weight,
    norm_gain,
    route_ids,
    route_weights,
    flight_experts,
    gate_weight,
    up_weight,
    down_weight,
):
    xl, xh = lax.axis_index("xl"), lax.axis_index("xh")
    tensor_idx = lax.axis_index(TENSOR)
    place = jnp.stack([lax.axis_index(a) for a in DP + TENSOR]).astype(jnp.int32)

    swapped = lax.ppermute(
        out_weight, ("y", "z"), [(a * RING + b, b * RING + a) for a in range(RING) for b in range(RING)]
    )
    hidden_in = lax.all_to_all(
        hidden_rows.reshape(ROWS, BLOCKS, COLS).transpose(1, 0, 2),
        ("xl", "z"),
        split_axis=0,
        concat_axis=0,
        tiled=True,
    ).reshape(SLAB, COLS)
    (extended,) = kernel_call(
        attend_kernel,
        [((SLAB + TABLE, HEADS_WIDE), BF16)],
        (slab_start, flight_experts, route_ids.T, queries, keys, values),
        "sshhhh",
        4 * 512 * 1152 * 128,
        1 << 20,
        "attend",
        [
            pltpu.VMEM((8, SLAB), jnp.int32),
            pltpu.VMEM(queries.shape, BF16),
            pltpu.VMEM(keys.shape, BF16),
            pltpu.VMEM(values.shape, BF16),
            pltpu.SemaphoreType.DMA((4,)),
        ],
        vmem=ALL_VMEM_BYTES,
    )
    swapped, hidden_in, _ = lax.optimization_barrier((swapped, hidden_in, extended))
    (packed,) = kernel_call(
        pack_weights_kernel,
        [((128, 3 * HIDDEN + HEADS_WIDE), BF16)],
        (gate_weight, up_weight, down_weight, swapped),
        "hhhh",
        0,
        4 * 128 * 1664,
        "pack_weights",
        [pltpu.SemaphoreType.DMA((2 + HIDDEN // 128 + HEADS_WIDE // 128,))],
        "h",
        ALL_VMEM_BYTES,
    )
    weights = lax.all_gather(packed, ("y", "core"), axis=0, tiled=True)
    other = swap(extended, "xl")
    both = jnp.concatenate([extended[:SLAB], other[:SLAB]])
    up1, down1 = along_z(both, 1), along_z(both, -1)
    up2, down2 = along_z(up1, 1), along_z(down1, -1)
    up3, down3 = along_z(up2, 1), along_z(down2, -1)
    up4, down4 = along_z(up3[:SLAB], 1), along_z(down3[SLAB:], -1)

    matches = route_ids[:, None, :] == flight_experts[None, :, None]
    hits = jnp.sum(matches.astype(jnp.int32), axis=2, dtype=jnp.int32)
    units = jnp.sum(jnp.where(matches, route_weights[:, None, :], 0), axis=2, dtype=jnp.int32)
    hits_both = jnp.where(
        xl == 0, jnp.stack([extended[SLAB:], other[SLAB:]]), jnp.stack([other[SLAB:], extended[SLAB:]])
    )
    hits_here = lax.dynamic_slice(
        hits_both, (0, xh * (FLIGHT // 2), 0), (2, FLIGHT // 2, SLAB)
    )
    hits_here = hits_here.astype(jnp.int32).reshape(2, FLIGHT // 2, BLOCKS, ROWS)
    slot_here = jnp.cumsum(hits_here, axis=3) - 1
    here = jnp.logical_and(
        hits_here[:, :, :, None, :] == 1,
        slot_here[:, :, :, None, :] == jnp.arange(CAP, dtype=jnp.int32)[:, None],
    ).astype(BF16)
    same = jnp.eye(BLOCKS, dtype=BF16)
    pickers = (here[:, :, :, :, None, :] * same[None, None, :, None, :, None]).reshape(
        2 * (FLIGHT // 2) * BLOCKS * CAP, SLAB
    )
    hits_mine = lax.dynamic_slice_in_dim(hits, tensor_idx * ROWS, ROWS, 0)
    coef = lax.dynamic_slice_in_dim(units, tensor_idx * ROWS, ROWS, 0).astype(F32) / 65536.0
    slot_mine = jnp.cumsum(hits_mine, axis=0) - 1
    mine = jnp.where(
        jnp.logical_and(
            hits_mine[..., None] == 1, slot_mine[..., None] == jnp.arange(CAP, dtype=jnp.int32)
        ),
        coef[..., None],
        0.0,
    )
    two = jnp.eye(2, dtype=F32)
    coefs = (
        mine[None, None, :, None, :, None, None, :]
        * two[:, None, None, :, None, None, None, None]
        * two[None, :, None, None, None, None, :, None]
    )
    coefs = jnp.broadcast_to(coefs, (2, 2, ROWS, 2, FLIGHT, GROUP, 2, CAP)).reshape(
        4 * ROWS, 2 * BLOCKS * 2 * CAP
    )
    gain = lax.dynamic_slice(norm_gain, (xl * HALF,), (HALF,)).reshape(1, HALF)
    weights, pickers, coefs, gain = lax.optimization_barrier((weights, pickers, coefs, gain))

    keep, send = kernel_call(
        project_kernel,
        [((2 * SLAB, COLS), F32), ((2 * SLAB, COLS), BF16)],
        (place, hidden_in, both, up1, down1, up2, down2, up3, down3, up4, down4, weights),
        "s" + "v" * 10 + "h",
        2 * 256 * 4096 * 256,
        2 * 2048 * 1024,
        "project",
        [pltpu.VMEM((HALF, HEADS_WIDE), BF16), pltpu.SemaphoreType.DMA((RING,))],
    )
    residual, rows_out = kernel_call(
        residual_kernel,
        [((SLAB, COLS), BF16), ((RING * 2 * BLOCKS * CAP, COLS), BF16)],
        (place, keep, swap(send, "xh"), pickers),
        "svvv",
        2 * 256 * 128 * 256,
        1 << 20,
        "residual",
    )
    rows_in = lax.all_to_all(
        rows_out.reshape(RING, 2 * BLOCKS * CAP, COLS), "z", split_axis=0, concat_axis=0, tiled=True
    ).reshape(RING * 2 * BLOCKS * CAP, COLS)
    own, part = kernel_call(
        gate_up_kernel,
        [((2 * BLOCKS * CAP, 2 * HIDDEN + 128), F32), ((2 * BLOCKS * CAP, 2 * HIDDEN + 128), BF16)],
        (rows_in, gain, weights),
        "vvh",
        2 * 128 * 2048 * 768,
        3 << 20,
        "gate_up",
        [pltpu.VMEM((HALF, 2 * HIDDEN), BF16), pltpu.SemaphoreType.DMA((RING,))],
    )
    (outward,) = kernel_call(
        down_kernel,
        [((4 * BLOCKS * CAP, QUARTER + COLS), BF16)],
        (place, own, swap(part, "xl"), residual, weights),
        "svvvh",
        2 * 256 * 384 * 2048,
        2 << 20,
        "down",
        [pltpu.VMEM((HALF, HIDDEN), BF16), pltpu.SemaphoreType.DMA],
    )
    returned = lax.all_to_all(
        outward.reshape(2 * BLOCKS, 2 * CAP, QUARTER + COLS),
        PAIR_TENSOR,
        split_axis=0,
        concat_axis=0,
        tiled=True,
    ).reshape(4 * BLOCKS * CAP, QUARTER + COLS)
    (mixed,) = kernel_call(
        combine_kernel,
        [((ROWS, 2 * HALF), BF16)],
        (place, coefs, returned),
        "svv",
        2 * 128 * 256 * 1024,
        1 << 20,
        "combine",
    )
    return mixed


def solution(mesh):
    fine = Mesh(mesh.devices.reshape(2, RING, 2, 2, RING), DP + TENSOR)
    placed = (
        P(DP + TENSOR, None),
        P(DP, TENSOR),
        P(DP, TENSOR),
        P(DP, TENSOR),
        P(DP),
        P(TENSOR, DP),
        P(),
        P(DP, None),
        P(DP, None),
        P(),
        P(DP, TENSOR),
        P(DP, TENSOR),
        P(TENSOR, DP),
    )
    return jax.shard_map(
        per_device, mesh=fine, in_specs=placed, out_specs=P(DP + TENSOR, None), check_vma=False
    )
```

```python
import jax
import jax.numpy as jnp
from jax import lax
from jax.experimental import pallas as pl
from jax.experimental.pallas import tpu as pltpu
from jax.sharding import Mesh
from jax.sharding import PartitionSpec as P

DP = ("xl", "y", "core")
TENSOR = ("xh", "z")
PAIR_TENSOR = ("xl",) + TENSOR
RING = 8
STEPS = (0, -1, 1, -2, 2, -3, 3, 4)
SLAB = 128
HALF = 2048
QUARTER = 1024
COLS = 256
HIDDEN = 384
HEADS_WIDE = 512
CAP = 4
FLIGHT = 4
GROUP = 4
BLOCKS = 16
ROWS = 8
TABLE = 16
SPARE = 80
VMEM_BYTES = 48 * 1024 * 1024
ALL_VMEM_BYTES = 63400000
F32, BF16 = jnp.float32, jnp.bfloat16


def attend_kernel(
    start_ref, flight_ref, ids_hbm, queries_hbm, keys_hbm, values_hbm, out_ref, ids_ref, queries_ref, keys_ref, values_ref, sems
):
    copies = [
        pltpu.make_async_copy(source, target, sems.at[i])
        for i, (source, target) in enumerate(
            ((keys_hbm, keys_ref), (queries_hbm, queries_ref), (values_hbm, values_ref), (ids_hbm, ids_ref))
        )
    ]
    for copy in copies:
        copy.start()
    for copy in copies:
        copy.wait()
    keys, values = keys_ref[...], values_ref[...]
    size = keys.shape[1]
    shape = (2 * SLAB, keys.shape[0])
    position = start_ref[0] + (lax.broadcasted_iota(jnp.int32, shape, 0) & (SLAB - 1))
    visible = lax.broadcasted_iota(jnp.int32, shape, 1) <= position
    for pair in range(HEADS_WIDE // size // 2):
        first, second = (slice((2 * pair + i) * size, (2 * pair + i + 1) * size) for i in range(2))
        block = jnp.concatenate([queries_ref[:, first], queries_ref[:, second]])
        scores = lax.dot_general(
            block, keys, (((1,), (1,)), ((), ())), preferred_element_type=F32
        ) * size ** (-0.5)
        scores = jnp.where(visible, scores, -1e30)
        exp_scores = jnp.exp(scores - jnp.max(scores, axis=1, keepdims=True))
        totals = jnp.sum(exp_scores, axis=1, keepdims=True)
        context = (jnp.dot(exp_scores.astype(BF16), values, preferred_element_type=F32) / totals).astype(BF16)
        out_ref[:SLAB, first] = context[:SLAB]
        out_ref[:SLAB, second] = context[SLAB:]
    line = lax.broadcasted_iota(jnp.int32, (TABLE, SLAB), 0)
    table = jnp.zeros((TABLE, SLAB), F32)
    for f in range(FLIGHT):
        named = jnp.max(jnp.where(ids_ref[...] == flight_ref[f], 1.0, 0.0), axis=0, keepdims=True)
        table = jnp.where(line == f, named, table)
    out_ref[SLAB:, :SLAB] = table.astype(BF16)
    out_ref[SLAB:, SLAB:] = jnp.zeros((TABLE, HEADS_WIDE - SLAB), BF16)


def swap(block, axis):
    return lax.ppermute(block, axis, [(0, 1), (1, 0)])


def along_z(block, step):
    return lax.ppermute(block, "z", [(i, (i + step) % RING) for i in range(RING)])


def kernel_call(body, out_shapes, operands, spaces, flops, moved, name, scratch=(), out_space="v", vmem=VMEM_BYTES):
    kinds = {
        "v": pl.BlockSpec(memory_space=pltpu.VMEM),
        "s": pl.BlockSpec(memory_space=pltpu.SMEM),
        "h": pl.BlockSpec(memory_space=pl.ANY),
    }
    return pl.pallas_call(
        body,
        out_shape=[jax.ShapeDtypeStruct(shape, dtype) for shape, dtype in out_shapes],
        in_specs=[kinds[s] for s in spaces],
        out_specs=[kinds[out_space]] * len(out_shapes),
        scratch_shapes=list(scratch),
        compiler_params=pltpu.CompilerParams(vmem_limit_bytes=vmem),
        cost_estimate=pl.CostEstimate(flops=flops, bytes_accessed=moved, transcendentals=0),
        name=name,
    )(*operands)


def pack_weights_kernel(gate_ref, up_ref, swapped_ref, packed_ref):
    packed_ref[:, :HIDDEN] = gate_ref[...]
    packed_ref[:, HIDDEN : 2 * HIDDEN] = up_ref[...]
    for j in range(HEADS_WIDE // 128):
        at = 2 * HIDDEN + j * 128
        packed_ref[:, at : at + 128] = swapped_ref[j * 128 : (j + 1) * 128, :]


def pack_down_kernel(down_ref, packed_ref):
    for j in range(HIDDEN // 128):
        packed_ref[:, j * 128 : (j + 1) * 128] = down_ref[j * 128 : (j + 1) * 128, :]


def project_kernel(place_ref, *refs):
    contexts, (weights_hbm, keep_ref, send_ref, weights, sems) = refs[:RING], refs[RING:]
    z = place_ref[4]

    def copy(k):
        at = pl.ds(k * 2 * 128, 2 * 128)
        return pltpu.make_async_copy(
            weights_hbm.at[at, pl.ds(2 * HIDDEN, HEADS_WIDE)], weights.at[at], sems.at[k]
        )

    for k in range(RING):
        copy(k).start()
    for k in range(RING):
        copy(k).wait()
    total = jnp.zeros((2 * SLAB, COLS), F32)
    for k in range(RING):
        context = contexts[k][...]
        first = pl.multiple_of(((z + (STEPS[k] + RING + RING // 2)) & (RING - 1)) * 256, 256)
        for half in range(2):
            lanes = slice(half * 256, half * 256 + 256)
            block = weights[pl.ds(first, 256), lanes]
            rhs = jnp.concatenate(
                [
                    jnp.concatenate([block[:128, q * 128 : (q + 1) * 128], block[128:, q * 128 : (q + 1) * 128]], axis=1)
                    for q in range(2)
                ]
            )
            total += jnp.dot(context[:, lanes], rhs, preferred_element_type=F32)
    keep_ref[...] = total
    send_ref[...] = total.astype(BF16)


def residual_kernel(place_ref, keep_ref, recv_ref, hidden_ref, pickers_ref, residual_ref, rows_ref):
    xl, xh = place_ref[0], place_ref[3]
    summed = keep_ref[...] + recv_ref[...].astype(F32)
    own, other = summed[:SLAB], summed[SLAB:]
    per_expert = BLOCKS * CAP
    held = jnp.zeros((SLAB, COLS), F32)
    for slab in range(2):
        at = slice(slab * SLAB, (slab + 1) * SLAB)
        residual = (jnp.where(xl == slab, own, other) + hidden_ref[at, :].astype(F32)).astype(BF16)
        held = jnp.where(xh == slab, residual.astype(F32), held)
        picked = jnp.dot(pickers_ref[at, :], residual, preferred_element_type=F32).astype(BF16)
        for f in range(FLIGHT // 2):
            for j in range(GROUP):
                to = ((f * GROUP + j) * 2 + slab) * per_expert
                rows_ref[to : to + per_expert, :] = picked[f * per_expert : (f + 1) * per_expert]
    residual_ref[...] = held.astype(BF16)


def gate_up_kernel(rows_ref, gain_ref, weights_hbm, own_ref, send_ref, weights, sems):
    part = HALF // RING

    def copy(k):
        at = pl.ds(k * part, part)
        return pltpu.make_async_copy(
            weights_hbm.at[at, pl.ds(0, 2 * HIDDEN)], weights.at[at], sems.at[k]
        )

    for k in range(RING):
        copy(k).start()
    slots = BLOCKS * CAP
    total = jnp.zeros((2 * slots, 2 * HIDDEN), F32)
    squares = jnp.zeros((2 * slots, 1), F32)
    for k in range(RING):
        rows = rows_ref[2 * k * slots : 2 * (k + 1) * slots, :].astype(F32)
        squares += jnp.sum(rows * rows, axis=1, keepdims=True)
        scaled = (rows * gain_ref[:, k * part : (k + 1) * part].astype(F32)).astype(BF16)
        copy(k).wait()
        total += jnp.dot(scaled, weights[k * part : (k + 1) * part, :], preferred_element_type=F32)
    own_ref[:, : 2 * HIDDEN] = total
    own_ref[:, 2 * HIDDEN :] = jnp.broadcast_to(squares, (2 * slots, 128))
    send_ref[:, : 2 * HIDDEN] = total.astype(BF16)
    high = squares.astype(BF16)
    rest = squares - high.astype(F32)
    middle = rest.astype(BF16)
    low = (rest - middle.astype(F32)).astype(BF16)
    lane = lax.broadcasted_iota(jnp.int32, (2 * slots, 128), 1)
    tail = jnp.where(lane == 0, high.astype(F32), 0.0)
    tail = jnp.where(lane == 1, middle.astype(F32), tail)
    tail = jnp.where(lane == 2, low.astype(F32), tail)
    send_ref[:, 2 * HIDDEN :] = tail.astype(BF16)


def down_kernel(place_ref, own_ref, recv_ref, residual_ref, weights_hbm, out_ref, weights, sem):
    copy = pltpu.make_async_copy(weights_hbm, weights, sem)
    copy.start()
    xh = place_ref[3]
    slots = 2 * BLOCKS * CAP
    other = recv_ref[:, 2 * HIDDEN :].astype(F32)
    squares = own_ref[:, 2 * HIDDEN : 2 * HIDDEN + 1] + jnp.sum(other, axis=1, keepdims=True)
    inverse = lax.rsqrt(squares / (2 * HALF) + 1e-06)
    total = (own_ref[:, : 2 * HIDDEN] + recv_ref[:, : 2 * HIDDEN].astype(F32)) * inverse
    gate, up = total[:, :HIDDEN], total[:, HIDDEN:]
    activated = (gate / (1.0 + jnp.exp(-gate)) * up).astype(BF16)
    to = lax.broadcasted_iota(jnp.int32, (2 * slots, slots), 0)
    source = lax.broadcasted_iota(jnp.int32, (2 * slots, slots), 1)
    twice = jnp.where(source == (to >> 3) * CAP + (to & 3), 1.0, 0.0).astype(BF16)
    activated = jnp.dot(twice, activated, preferred_element_type=F32).astype(BF16)
    first = (lax.broadcasted_iota(jnp.int32, (2 * slots, COLS), 0) & 4) == 0

    def columns(d):
        rhs = jnp.concatenate(
            [
                jnp.concatenate(
                    [
                        weights[(2 * d + e) * 128 : (2 * d + e + 1) * 128, j * 128 : (j + 1) * 128]
                        for j in range(HIDDEN // 128)
                    ]
                )
                for e in range(2)
            ],
            axis=1,
        )
        return jnp.dot(activated, rhs, preferred_element_type=F32)

    copy.wait()
    chunks = QUARTER // COLS
    for d in range(chunks):
        out_ref[:, d * COLS : (d + 1) * COLS] = jnp.where(first, columns(d), columns(d + chunks)).astype(BF16)
    residual = residual_ref[...].astype(F32)
    out_ref[:SLAB, QUARTER:] = jnp.where(xh == 0, residual, 0.0).astype(BF16)
    out_ref[SLAB:, QUARTER:] = jnp.where(xh == 1, residual, 0.0).astype(BF16)


def combine_kernel(place_ref, coefs_ref, returned_ref, out_ref):
    xl = place_ref[0]
    coefs = coefs_ref[...]
    high = coefs.astype(BF16)
    rest = coefs - high.astype(F32)
    middle = rest.astype(BF16)
    low = (rest - middle.astype(F32)).astype(BF16)
    rows, slots = 4 * ROWS, 2 * BLOCKS * ROWS
    to = lax.broadcasted_iota(jnp.int32, (rows, slots), 0)
    source = lax.broadcasted_iota(jnp.int32, (rows, slots), 1)
    half, quarter, row = to >> 4, (to >> 3) & 1, to & 7
    for k in range(QUARTER // COLS):
        at = slice(k * COLS, (k + 1) * COLS)
        wanted = (half * BLOCKS + xl * RING + quarter * (RING // 2) + k) * ROWS + row
        picker = jnp.where(source == wanted, 1.0, 0.0).astype(BF16)
        parts = returned_ref[:, at]
        mixed = (
            jnp.dot(picker, returned_ref[:, QUARTER:], preferred_element_type=F32)
            + jnp.dot(high, parts, preferred_element_type=F32)
            + (
                jnp.dot(middle, parts, preferred_element_type=F32)
                + jnp.dot(low, parts, preferred_element_type=F32)
            )
        )
        for q in range(4):
            out_ref[:, q * QUARTER + k * COLS : q * QUARTER + (k + 1) * COLS] = mixed[
                q * ROWS : (q + 1) * ROWS
            ].astype(BF16)


def per_device(
    hidden_rows,
    queries,
    keys,
    values,
    slab_start,
    out_weight,
    norm_gain,
    route_ids,
    route_weights,
    flight_experts,
    gate_weight,
    up_weight,
    down_weight,
):
    xl, xh = lax.axis_index("xl"), lax.axis_index("xh")
    tensor_idx = lax.axis_index(TENSOR)
    place = jnp.stack([lax.axis_index(a) for a in DP + TENSOR]).astype(jnp.int32)

    swapped = lax.ppermute(
        jnp.pad(out_weight, ((0, SPARE), (0, 0))),
        ("y", "z"),
        [(a * RING + b, (b + RING // 2) % RING * RING + a) for a in range(RING) for b in range(RING)],
    )
    (extended,) = kernel_call(
        attend_kernel,
        [((SLAB + TABLE, HEADS_WIDE), BF16)],
        (slab_start, flight_experts, route_ids.T, queries, keys, values),
        "sshhhh",
        4 * 512 * 1152 * 128,
        1 << 20,
        "attend",
        [
            pltpu.VMEM((8, SLAB), jnp.int32),
            pltpu.VMEM(queries.shape, BF16),
            pltpu.VMEM(keys.shape, BF16),
            pltpu.VMEM(values.shape, BF16),
            pltpu.SemaphoreType.DMA((4,)),
        ],
        vmem=ALL_VMEM_BYTES,
    )
    other = swap(extended, "xl")
    swapped, _ = lax.optimization_barrier((swapped, other))
    (packed,) = kernel_call(
        pack_weights_kernel,
        [((128, 2 * HIDDEN + HEADS_WIDE), BF16)],
        (gate_weight, up_weight, swapped),
        "vvv",
        0,
        4 * 128 * 1280,
        "pack_weights",
    )
    weights = lax.all_gather(packed, ("y", "core"), axis=0, tiled=True)
    (packed_down,) = kernel_call(
        pack_down_kernel, [((128, HIDDEN), BF16)], (down_weight,), "v", 0, 4 * 128 * 384, "pack_down"
    )
    packed_down, _ = lax.optimization_barrier((packed_down, packed))
    down_weights = lax.all_gather(packed_down, ("y", "core"), axis=0, tiled=True)
    both = jnp.concatenate([extended[:SLAB], other[:SLAB]])
    up1, down1 = along_z(both, 1), along_z(both, -1)
    up2, down2 = along_z(up1, 1), along_z(down1, -1)
    up3, down3 = along_z(up2, 1), along_z(down2, -1)
    up4 = along_z(up3, 1)

    hidden_later, _, _ = lax.optimization_barrier((hidden_rows, up4, down3))
    columns = hidden_later.reshape(ROWS, 2, 1, RING, COLS).transpose(1, 2, 3, 0, 4)
    hidden_in = lax.all_to_all(
        jnp.broadcast_to(columns, (2, 2, RING, ROWS, COLS)).reshape(2 * BLOCKS, ROWS, COLS),
        PAIR_TENSOR,
        split_axis=0,
        concat_axis=0,
        tiled=True,
    ).reshape(2 * SLAB, COLS)

    matches = route_ids[:, None, :] == flight_experts[None, :, None]
    hits = jnp.sum(matches.astype(jnp.int32), axis=2, dtype=jnp.int32)
    units = jnp.sum(jnp.where(matches, route_weights[:, None, :], 0), axis=2, dtype=jnp.int32)
    hits_both = jnp.where(
        xl == 0, jnp.stack([extended[SLAB:], other[SLAB:]]), jnp.stack([other[SLAB:], extended[SLAB:]])
    )
    hits_here = lax.dynamic_slice(
        hits_both, (0, xh * (FLIGHT // 2), 0), (2, FLIGHT // 2, SLAB)
    )
    hits_here = hits_here.astype(jnp.int32).reshape(2, FLIGHT // 2, BLOCKS, ROWS)
    slot_here = jnp.cumsum(hits_here, axis=3) - 1
    here = jnp.logical_and(
        hits_here[:, :, :, None, :] == 1,
        slot_here[:, :, :, None, :] == jnp.arange(CAP, dtype=jnp.int32)[:, None],
    ).astype(BF16)
    same = jnp.eye(BLOCKS, dtype=BF16)
    pickers = (here[:, :, :, :, None, :] * same[None, None, :, None, :, None]).reshape(
        2 * (FLIGHT // 2) * BLOCKS * CAP, SLAB
    )
    hits_mine = lax.dynamic_slice_in_dim(hits, tensor_idx * ROWS, ROWS, 0)
    coef = lax.dynamic_slice_in_dim(units, tensor_idx * ROWS, ROWS, 0).astype(F32) / 65536.0
    slot_mine = jnp.cumsum(hits_mine, axis=0) - 1
    mine = jnp.where(
        jnp.logical_and(
            hits_mine[..., None] == 1, slot_mine[..., None] == jnp.arange(CAP, dtype=jnp.int32)
        ),
        coef[..., None],
        0.0,
    )
    two = jnp.eye(2, dtype=F32)
    coefs = (
        mine[None, None, :, None, :, None, None, :]
        * two[:, None, None, :, None, None, None, None]
        * two[None, :, None, None, None, None, :, None]
    )
    coefs = jnp.broadcast_to(coefs, (2, 2, ROWS, 2, FLIGHT, GROUP, 2, CAP)).reshape(
        4 * ROWS, 2 * BLOCKS * 2 * CAP
    )
    gain = lax.dynamic_slice(norm_gain, (xl * HALF,), (HALF,)).reshape(1, HALF)
    weights, pickers, coefs, gain = lax.optimization_barrier((weights, pickers, coefs, gain))

    keep, send = kernel_call(
        project_kernel,
        [((2 * SLAB, COLS), F32), ((2 * SLAB, COLS), BF16)],
        (place, both, up1, down1, up2, down2, up3, down3, up4, weights),
        "s" + "v" * RING + "h",
        2 * 256 * 4096 * 256,
        2 * 2048 * 1024,
        "project",
        [pltpu.VMEM((HALF, HEADS_WIDE), BF16), pltpu.SemaphoreType.DMA((RING,))],
    )
    residual, rows_out = kernel_call(
        residual_kernel,
        [((SLAB, COLS), BF16), ((RING * 2 * BLOCKS * CAP, COLS), BF16)],
        (place, keep, swap(send, "xh"), hidden_in, pickers),
        "svvvv",
        2 * 256 * 128 * 256,
        1 << 20,
        "residual",
    )
    rows_in = lax.all_to_all(
        rows_out.reshape(RING, 2 * BLOCKS * CAP, COLS), "z", split_axis=0, concat_axis=0, tiled=True
    ).reshape(RING * 2 * BLOCKS * CAP, COLS)
    own, part = kernel_call(
        gate_up_kernel,
        [((2 * BLOCKS * CAP, 2 * HIDDEN + 128), F32), ((2 * BLOCKS * CAP, 2 * HIDDEN + 128), BF16)],
        (rows_in, gain, weights),
        "vvh",
        2 * 128 * 2048 * 768,
        3 << 20,
        "gate_up",
        [pltpu.VMEM((HALF, 2 * HIDDEN), BF16), pltpu.SemaphoreType.DMA((RING,))],
    )
    (outward,) = kernel_call(
        down_kernel,
        [((4 * BLOCKS * CAP, QUARTER + COLS), BF16)],
        (place, own, swap(part, "xl"), residual, down_weights),
        "svvvh",
        2 * 256 * 384 * 2048,
        2 << 20,
        "down",
        [pltpu.VMEM((HALF, HIDDEN), BF16), pltpu.SemaphoreType.DMA],
    )
    returned = lax.all_to_all(
        outward.reshape(2 * BLOCKS, 2 * CAP, QUARTER + COLS),
        PAIR_TENSOR,
        split_axis=0,
        concat_axis=0,
        tiled=True,
    ).reshape(4 * BLOCKS * CAP, QUARTER + COLS)
    (mixed,) = kernel_call(
        combine_kernel,
        [((ROWS, 2 * HALF), BF16)],
        (place, coefs, returned),
        "svv",
        2 * 128 * 256 * 1024,
        1 << 20,
        "combine",
    )
    return mixed


def solution(mesh):
    fine = Mesh(mesh.devices.reshape(2, RING, 2, 2, RING), DP + TENSOR)
    placed = (
        P(DP + TENSOR, None),
        P(DP, TENSOR),
        P(DP, TENSOR),
        P(DP, TENSOR),
        P(DP),
        P(TENSOR, DP),
        P(),
        P(DP, None),
        P(DP, None),
        P(),
        P(DP, TENSOR),
        P(DP, TENSOR),
        P(TENSOR, DP),
    )
    return jax.shard_map(
        per_device, mesh=fine, in_specs=placed, out_specs=P(DP + TENSOR, None), check_vma=False
    )
```

```python
import jax
import jax.numpy as jnp
from jax import lax
from jax.experimental import pallas as pl
from jax.experimental.pallas import tpu as pltpu
from jax.sharding import Mesh
from jax.sharding import PartitionSpec as P

DP = ("xl", "y", "core")
TENSOR = ("xh", "z")
PAIR_TENSOR = ("xl",) + TENSOR
RING = 8
STEPS = (0, -1, 1, -2, 2, -3, 3, 4)
SLAB = 128
HALF = 2048
QUARTER = 1024
COLS = 256
HIDDEN = 384
HEADS_WIDE = 512
CAP = 4
FLIGHT = 4
GROUP = 4
BLOCKS = 16
ROWS = 8
VMEM_BYTES = 48 * 1024 * 1024
ALL_VMEM_BYTES = 63400000
F32, BF16 = jnp.float32, jnp.bfloat16


def attend_kernel(
    start_ref, queries_hbm, keys_hbm, values_hbm, out_ref, queries_ref, keys_ref, values_ref, sems
):
    copies = [
        pltpu.make_async_copy(source, target, sems.at[i])
        for i, (source, target) in enumerate(
            ((keys_hbm, keys_ref), (queries_hbm, queries_ref), (values_hbm, values_ref))
        )
    ]
    for copy in copies:
        copy.start()
    for copy in copies:
        copy.wait()
    keys, values = keys_ref[...], values_ref[...]
    size = keys.shape[1]
    shape = (2 * SLAB, keys.shape[0])
    position = start_ref[0] + (lax.broadcasted_iota(jnp.int32, shape, 0) & (SLAB - 1))
    visible = lax.broadcasted_iota(jnp.int32, shape, 1) <= position
    for pair in range(HEADS_WIDE // size // 2):
        first, second = (slice((2 * pair + i) * size, (2 * pair + i + 1) * size) for i in range(2))
        block = jnp.concatenate([queries_ref[:, first], queries_ref[:, second]])
        scores = lax.dot_general(
            block, keys, (((1,), (1,)), ((), ())), preferred_element_type=F32
        ) * size ** (-0.5)
        scores = jnp.where(visible, scores, -1e30)
        exp_scores = jnp.exp(scores - jnp.max(scores, axis=1, keepdims=True))
        totals = jnp.sum(exp_scores, axis=1, keepdims=True)
        context = (jnp.dot(exp_scores.astype(BF16), values, preferred_element_type=F32) / totals).astype(BF16)
        out_ref[:, first] = context[:SLAB]
        out_ref[:, second] = context[SLAB:]


def swap(block, axis):
    return lax.ppermute(block, axis, [(0, 1), (1, 0)])


def along_z(block, step):
    return lax.ppermute(block, "z", [(i, (i + step) % RING) for i in range(RING)])


def kernel_call(body, out_shapes, operands, spaces, flops, moved, name, scratch=(), out_space="v", vmem=VMEM_BYTES):
    kinds = {
        "v": pl.BlockSpec(memory_space=pltpu.VMEM),
        "s": pl.BlockSpec(memory_space=pltpu.SMEM),
        "h": pl.BlockSpec(memory_space=pl.ANY),
    }
    return pl.pallas_call(
        body,
        out_shape=[jax.ShapeDtypeStruct(shape, dtype) for shape, dtype in out_shapes],
        in_specs=[kinds[s] for s in spaces],
        out_specs=[kinds[out_space]] * len(out_shapes),
        scratch_shapes=list(scratch),
        compiler_params=pltpu.CompilerParams(vmem_limit_bytes=vmem),
        cost_estimate=pl.CostEstimate(flops=flops, bytes_accessed=moved, transcendentals=0),
        name=name,
    )(*operands)


def pack_weights_kernel(gate_ref, up_ref, swapped_ref, packed_ref):
    packed_ref[:, :HIDDEN] = gate_ref[...]
    packed_ref[:, HIDDEN : 2 * HIDDEN] = up_ref[...]
    for j in range(HEADS_WIDE // 128):
        at = 2 * HIDDEN + j * 128
        packed_ref[:, at : at + 128] = swapped_ref[j * 128 : (j + 1) * 128, :]


def pack_down_kernel(down_ref, packed_ref):
    for j in range(HIDDEN // 128):
        packed_ref[:, j * 128 : (j + 1) * 128] = down_ref[j * 128 : (j + 1) * 128, :]


def unpack_kernel(place_ref, incoming_ref, hidden_ref, pickers_ref):
    xh = place_ref[3]
    shape = (SLAB, 2 * SLAB)
    to, source = (lax.broadcasted_iota(jnp.int32, shape, d) for d in range(2))
    taken = jnp.where(source == (to >> 3) * 2 * ROWS + (to & 7), 1.0, 0.0).astype(BF16)
    hidden_ref[...] = jnp.dot(taken, incoming_ref[...], preferred_element_type=F32).astype(BF16)
    line = lax.broadcasted_iota(jnp.int32, (2 * ROWS, COLS), 0)
    hits = []
    for slab in range(2):
        rows = incoming_ref[slab * SLAB : slab * SLAB + 2 * ROWS, :].astype(F32)
        both = jnp.sum(jnp.where(line == ROWS + xh, rows, 0.0), axis=0, keepdims=True)
        hits += [both[:, :SLAB], both[:, SLAB:]]
    above, row = (lax.broadcasted_iota(jnp.int32, (SLAB, SLAB), d) for d in range(2))
    earlier = jnp.where(jnp.logical_and(above >> 3 == row >> 3, above <= row), 1.0, 0.0).astype(BF16)
    slots = BLOCKS * CAP
    shape = (slots, SLAB)
    place, row = (lax.broadcasted_iota(jnp.int32, shape, d) for d in range(2))
    number = ((place & (CAP - 1)) + 1).astype(F32)
    for i, hit in enumerate(hits):
        count = jnp.dot(
            jnp.broadcast_to(hit, (ROWS, SLAB)).astype(BF16), earlier, preferred_element_type=F32
        )[:1]
        count = jnp.where(hit > 0.5, count, 0.0)
        named = jnp.logical_and(place >> 2 == row >> 3, count == number)
        pickers_ref[i * slots : (i + 1) * slots, :] = jnp.where(named, 1.0, 0.0).astype(BF16)


def project_kernel(place_ref, hidden_ref, *refs):
    contexts, (weights_hbm, keep_ref, send_ref, weights, sems) = refs[:RING], refs[RING:]
    xl, xh, z = place_ref[0], place_ref[3], place_ref[4]

    def copy(k):
        at = pl.ds(k * 2 * 128, 2 * 128)
        return pltpu.make_async_copy(
            weights_hbm.at[at, pl.ds(2 * HIDDEN, HEADS_WIDE)], weights.at[at], sems.at[k]
        )

    for k in range(RING):
        copy(k).start()
    for k in range(RING):
        copy(k).wait()
    total = jnp.zeros((2 * SLAB, COLS), F32)
    for k in range(RING):
        context = contexts[k][...]
        first = pl.multiple_of(((z + (RING + RING // 2 - STEPS[k])) & (RING - 1)) * 256, 256)
        for half in range(2):
            lanes = slice(half * 256, half * 256 + 256)
            block = weights[pl.ds(first, 256), lanes]
            rhs = jnp.concatenate(
                [
                    jnp.concatenate([block[:128, q * 128 : (q + 1) * 128], block[128:, q * 128 : (q + 1) * 128]], axis=1)
                    for q in range(2)
                ]
            )
            total += jnp.dot(context[:, lanes], rhs, preferred_element_type=F32)
    hidden = hidden_ref[...].astype(F32)
    rows = SLAB // 2
    own = jnp.where(xl == 0, hidden[:rows], hidden[rows:])
    other = jnp.where(xl == 0, hidden[rows:], hidden[:rows])
    total += jnp.concatenate(
        [jnp.where(xh == at, block, 0.0) for block in (own, other) for at in range(2)]
    )
    keep_ref[...] = total
    send_ref[...] = total.astype(BF16)


def residual_kernel(place_ref, keep_ref, recv_ref, pickers_ref, residual_ref, rows_ref):
    xl, xh = place_ref[0], place_ref[3]
    summed = keep_ref[...] + recv_ref[...].astype(F32)
    own, other = summed[:SLAB], summed[SLAB:]
    per_expert = BLOCKS * CAP
    held = jnp.zeros((SLAB, COLS), F32)
    for slab in range(2):
        at = slice(slab * SLAB, (slab + 1) * SLAB)
        residual = jnp.where(xl == slab, own, other).astype(BF16)
        held = jnp.where(xh == slab, residual.astype(F32), held)
        picked = jnp.dot(pickers_ref[at, :], residual, preferred_element_type=F32).astype(BF16)
        for f in range(FLIGHT // 2):
            for j in range(GROUP):
                to = ((f * GROUP + j) * 2 + slab) * per_expert
                rows_ref[to : to + per_expert, :] = picked[f * per_expert : (f + 1) * per_expert]
    residual_ref[...] = held.astype(BF16)


def gate_up_kernel(rows_ref, gain_ref, weights_hbm, own_ref, send_ref, weights, sems):
    part = HALF // RING

    def copy(k):
        at = pl.ds(k * part, part)
        return pltpu.make_async_copy(
            weights_hbm.at[at, pl.ds(0, 2 * HIDDEN)], weights.at[at], sems.at[k]
        )

    for k in range(RING):
        copy(k).start()
    slots = BLOCKS * CAP
    total = jnp.zeros((2 * slots, 2 * HIDDEN), F32)
    squares = jnp.zeros((2 * slots, 1), F32)
    for k in range(RING):
        rows = rows_ref[2 * k * slots : 2 * (k + 1) * slots, :].astype(F32)
        squares += jnp.sum(rows * rows, axis=1, keepdims=True)
        scaled = (rows * gain_ref[:, k * part : (k + 1) * part].astype(F32)).astype(BF16)
        copy(k).wait()
        total += jnp.dot(scaled, weights[k * part : (k + 1) * part, :], preferred_element_type=F32)
    own_ref[:, : 2 * HIDDEN] = total
    own_ref[:, 2 * HIDDEN :] = jnp.broadcast_to(squares, (2 * slots, 128))
    send_ref[:, : 2 * HIDDEN] = total.astype(BF16)
    high = squares.astype(BF16)
    rest = squares - high.astype(F32)
    middle = rest.astype(BF16)
    low = (rest - middle.astype(F32)).astype(BF16)
    lane = lax.broadcasted_iota(jnp.int32, (2 * slots, 128), 1)
    tail = jnp.where(lane == 0, high.astype(F32), 0.0)
    tail = jnp.where(lane == 1, middle.astype(F32), tail)
    tail = jnp.where(lane == 2, low.astype(F32), tail)
    send_ref[:, 2 * HIDDEN :] = tail.astype(BF16)


def down_kernel(place_ref, own_ref, recv_ref, residual_ref, weights_hbm, out_ref, weights, sem):
    copy = pltpu.make_async_copy(weights_hbm, weights, sem)
    copy.start()
    xh = place_ref[3]
    slots = 2 * BLOCKS * CAP
    other = recv_ref[:, 2 * HIDDEN :].astype(F32)
    squares = own_ref[:, 2 * HIDDEN : 2 * HIDDEN + 1] + jnp.sum(other, axis=1, keepdims=True)
    inverse = lax.rsqrt(squares / (2 * HALF) + 1e-06)
    total = (own_ref[:, : 2 * HIDDEN] + recv_ref[:, : 2 * HIDDEN].astype(F32)) * inverse
    gate, up = total[:, :HIDDEN], total[:, HIDDEN:]
    activated = (gate / (1.0 + jnp.exp(-gate)) * up).astype(BF16)
    to = lax.broadcasted_iota(jnp.int32, (2 * slots, slots), 0)
    source = lax.broadcasted_iota(jnp.int32, (2 * slots, slots), 1)
    twice = jnp.where(source == (to >> 3) * CAP + (to & 3), 1.0, 0.0).astype(BF16)
    activated = jnp.dot(twice, activated, preferred_element_type=F32).astype(BF16)
    first = (lax.broadcasted_iota(jnp.int32, (2 * slots, COLS), 0) & 4) == 0

    def columns(d):
        rhs = jnp.concatenate(
            [
                jnp.concatenate(
                    [
                        weights[(2 * d + e) * 128 : (2 * d + e + 1) * 128, j * 128 : (j + 1) * 128]
                        for j in range(HIDDEN // 128)
                    ]
                )
                for e in range(2)
            ],
            axis=1,
        )
        return jnp.dot(activated, rhs, preferred_element_type=F32)

    copy.wait()
    chunks = QUARTER // COLS
    for d in range(chunks):
        out_ref[:, d * COLS : (d + 1) * COLS] = jnp.where(first, columns(d), columns(d + chunks)).astype(BF16)
    residual = residual_ref[...].astype(F32)
    out_ref[:SLAB, QUARTER:] = jnp.where(xh == 0, residual, 0.0).astype(BF16)
    out_ref[SLAB:, QUARTER:] = jnp.where(xh == 1, residual, 0.0).astype(BF16)


def combine_kernel(place_ref, coefs_ref, returned_ref, out_ref):
    xl = place_ref[0]
    coefs = coefs_ref[...]
    high = coefs.astype(BF16)
    rest = coefs - high.astype(F32)
    middle = rest.astype(BF16)
    low = (rest - middle.astype(F32)).astype(BF16)
    rows, slots = 4 * ROWS, 2 * BLOCKS * ROWS
    to = lax.broadcasted_iota(jnp.int32, (rows, slots), 0)
    source = lax.broadcasted_iota(jnp.int32, (rows, slots), 1)
    half, quarter, row = to >> 4, (to >> 3) & 1, to & 7
    for k in range(QUARTER // COLS):
        at = slice(k * COLS, (k + 1) * COLS)
        wanted = (half * BLOCKS + xl * RING + quarter * (RING // 2) + k) * ROWS + row
        picker = jnp.where(source == wanted, 1.0, 0.0).astype(BF16)
        parts = returned_ref[:, at]
        mixed = (
            jnp.dot(picker, returned_ref[:, QUARTER:], preferred_element_type=F32)
            + jnp.dot(high, parts, preferred_element_type=F32)
            + (
                jnp.dot(middle, parts, preferred_element_type=F32)
                + jnp.dot(low, parts, preferred_element_type=F32)
            )
        )
        for q in range(4):
            out_ref[:, q * QUARTER + k * COLS : q * QUARTER + (k + 1) * COLS] = mixed[
                q * ROWS : (q + 1) * ROWS
            ].astype(BF16)


def per_device(
    hidden_rows,
    queries,
    keys,
    values,
    slab_start,
    out_weight,
    norm_gain,
    route_ids,
    route_weights,
    flight_experts,
    gate_weight,
    up_weight,
    down_weight,
):
    xl, xh = lax.axis_index("xl"), lax.axis_index("xh")
    tensor_idx = lax.axis_index(TENSOR)
    place = jnp.stack([lax.axis_index(a) for a in DP + TENSOR]).astype(jnp.int32)

    swapped = lax.ppermute(
        out_weight,
        ("y", "z"),
        [
            (a * RING + b, (2 * a - b + RING // 2) % RING * RING + a)
            for a in range(RING)
            for b in range(RING)
        ],
    )
    (context,) = kernel_call(
        attend_kernel,
        [((SLAB, HEADS_WIDE), BF16)],
        (slab_start, queries, keys, values),
        "shhh",
        4 * 512 * 1152 * 128,
        1 << 20,
        "attend",
        [
            pltpu.VMEM(queries.shape, BF16),
            pltpu.VMEM(keys.shape, BF16),
            pltpu.VMEM(values.shape, BF16),
            pltpu.SemaphoreType.DMA((3,)),
        ],
        vmem=ALL_VMEM_BYTES,
    )
    other = swap(context, "xl")
    both = jnp.concatenate([context, other])
    matches = route_ids[:, None, :] == flight_experts[None, :, None]
    hits = jnp.sum(matches.astype(jnp.int32), axis=2, dtype=jnp.int32)
    units = jnp.sum(jnp.where(matches, route_weights[:, None, :], 0), axis=2, dtype=jnp.int32)

    table = jnp.pad(hits.T.astype(BF16).reshape(2, COLS), ((0, ROWS - 2), (0, 0)))
    outgoing = jnp.concatenate(
        [hidden_rows.reshape(ROWS, BLOCKS, COLS).transpose(1, 0, 2), jnp.broadcast_to(table, (BLOCKS, ROWS, COLS))],
        axis=1,
    )
    gain = lax.dynamic_slice(norm_gain, (xl * HALF,), (HALF,)).reshape(1, HALF)
    (packed_down,) = kernel_call(
        pack_down_kernel, [((128, HIDDEN), BF16)], (down_weight,), "v", 0, 4 * 128 * 384, "pack_down"
    )
    swapped, outgoing, gain, packed_down, _ = lax.optimization_barrier(
        (swapped, outgoing, gain, packed_down, other)
    )
    (packed,) = kernel_call(
        pack_weights_kernel,
        [((128, 2 * HIDDEN + HEADS_WIDE), BF16)],
        (gate_weight, up_weight, swapped),
        "vvv",
        0,
        4 * 128 * 1280,
        "pack_weights",
    )
    weights = lax.all_gather(packed, ("y", "core"), axis=0, tiled=True)
    packed_down, _ = lax.optimization_barrier((packed_down, packed))
    down_weights = lax.all_gather(packed_down, ("y", "core"), axis=0, tiled=True)
    up1, down1 = along_z(both, 1), along_z(both, -1)
    up2, down2 = along_z(up1, 1), along_z(down1, -1)
    up3, down3 = along_z(up2, 1), along_z(down2, -1)
    up4 = along_z(up3, 1)

    outgoing, _ = lax.optimization_barrier((outgoing, up1))
    incoming = lax.all_to_all(outgoing, ("xl", "z"), split_axis=0, concat_axis=0, tiled=True)
    hidden_in, pickers = kernel_call(
        unpack_kernel,
        [((SLAB, COLS), BF16), ((2 * (FLIGHT // 2) * BLOCKS * CAP, SLAB), BF16)],
        (place, incoming.reshape(2 * SLAB, COLS)),
        "sv",
        0,
        1 << 18,
        "unpack",
    )
    hits_mine = lax.dynamic_slice_in_dim(hits, tensor_idx * ROWS, ROWS, 0)
    coef = lax.dynamic_slice_in_dim(units, tensor_idx * ROWS, ROWS, 0).astype(F32) / 65536.0
    slot_mine = jnp.cumsum(hits_mine, axis=0) - 1
    mine = jnp.where(
        jnp.logical_and(
            hits_mine[..., None] == 1, slot_mine[..., None] == jnp.arange(CAP, dtype=jnp.int32)
        ),
        coef[..., None],
        0.0,
    )
    two = jnp.eye(2, dtype=F32)
    coefs = (
        mine[None, None, :, None, :, None, None, :]
        * two[:, None, None, :, None, None, None, None]
        * two[None, :, None, None, None, None, :, None]
    )
    coefs = jnp.broadcast_to(coefs, (2, 2, ROWS, 2, FLIGHT, GROUP, 2, CAP)).reshape(
        4 * ROWS, 2 * BLOCKS * 2 * CAP
    )
    weights, pickers, coefs, gain = lax.optimization_barrier((weights, pickers, coefs, gain))

    keep, send = kernel_call(
        project_kernel,
        [((2 * SLAB, COLS), F32), ((2 * SLAB, COLS), BF16)],
        (place, hidden_in, both, up1, down1, up2, down2, up3, down3, up4, weights),
        "sv" + "v" * RING + "h",
        2 * 256 * 4096 * 256,
        2 * 2048 * 1024,
        "project",
        [pltpu.VMEM((HALF, HEADS_WIDE), BF16), pltpu.SemaphoreType.DMA((RING,))],
    )
    residual, rows_out = kernel_call(
        residual_kernel,
        [((SLAB, COLS), BF16), ((RING * 2 * BLOCKS * CAP, COLS), BF16)],
        (place, keep, swap(send, "xh"), pickers),
        "svvv",
        2 * 256 * 128 * 256,
        1 << 20,
        "residual",
    )
    rows_in = lax.all_to_all(
        rows_out.reshape(RING, 2 * BLOCKS * CAP, COLS), "z", split_axis=0, concat_axis=0, tiled=True
    ).reshape(RING * 2 * BLOCKS * CAP, COLS)
    own, part = kernel_call(
        gate_up_kernel,
        [((2 * BLOCKS * CAP, 2 * HIDDEN + 128), F32), ((2 * BLOCKS * CAP, 2 * HIDDEN + 128), BF16)],
        (rows_in, gain, weights),
        "vvh",
        2 * 128 * 2048 * 768,
        3 << 20,
        "gate_up",
        [pltpu.VMEM((HALF, 2 * HIDDEN), BF16), pltpu.SemaphoreType.DMA((RING,))],
    )
    (outward,) = kernel_call(
        down_kernel,
        [((4 * BLOCKS * CAP, QUARTER + COLS), BF16)],
        (place, own, swap(part, "xl"), residual, down_weights),
        "svvvh",
        2 * 256 * 384 * 2048,
        2 << 20,
        "down",
        [pltpu.VMEM((HALF, HIDDEN), BF16), pltpu.SemaphoreType.DMA],
    )
    returned = lax.all_to_all(
        outward.reshape(2 * BLOCKS, 2 * CAP, QUARTER + COLS),
        PAIR_TENSOR,
        split_axis=0,
        concat_axis=0,
        tiled=True,
    ).reshape(4 * BLOCKS * CAP, QUARTER + COLS)
    (mixed,) = kernel_call(
        combine_kernel,
        [((ROWS, 2 * HALF), BF16)],
        (place, coefs, returned),
        "svv",
        2 * 128 * 256 * 1024,
        1 << 20,
        "combine",
    )
    return mixed


def solution(mesh):
    fine = Mesh(mesh.devices.reshape(2, RING, 2, 2, RING), DP + TENSOR)
    placed = (
        P(DP + TENSOR, None),
        P(DP, TENSOR),
        P(DP, TENSOR),
        P(DP, TENSOR),
        P(DP),
        P(TENSOR, DP),
        P(),
        P(DP, None),
        P(DP, None),
        P(),
        P(DP, TENSOR),
        P(DP, TENSOR),
        P(TENSOR, DP),
    )
    return jax.shard_map(
        per_device, mesh=fine, in_specs=placed, out_specs=P(DP + TENSOR, None), check_vma=False
    )
```

```python
import jax
import jax.numpy as jnp
from jax import lax
from jax.experimental import pallas as pl
from jax.experimental.pallas import tpu as pltpu
from jax.sharding import Mesh
from jax.sharding import PartitionSpec as P

DP = ("xl", "y", "core")
TENSOR = ("xh", "z")
PAIR_TENSOR = ("xl",) + TENSOR
RING = 8
STEPS = (0, -1, 1, -2, 2, -3, 3, 4)
SLAB = 128
HALF = 2048
QUARTER = 1024
COLS = 256
HIDDEN = 384
HEADS_WIDE = 512
CAP = 4
FLIGHT = 4
GROUP = 4
BLOCKS = 16
ROWS = 8
VMEM_BYTES = 48 * 1024 * 1024
ALL_VMEM_BYTES = 63400000
MOST_VMEM_BYTES = 57000000
DOWN_VMEM_BYTES = 55000000
F32, BF16 = jnp.float32, jnp.bfloat16


def attend_kernel(
    start_ref, queries_hbm, keys_hbm, values_hbm, out_ref, queries_ref, keys_ref, values_ref, sems
):
    copies = [
        pltpu.make_async_copy(source, target, sems.at[i])
        for i, (source, target) in enumerate(
            ((keys_hbm, keys_ref), (queries_hbm, queries_ref), (values_hbm, values_ref))
        )
    ]
    for copy in copies:
        copy.start()
    for copy in copies:
        copy.wait()
    keys, values = keys_ref[...], values_ref[...]
    size = keys.shape[1]
    shape = (2 * SLAB, keys.shape[0])
    position = start_ref[0] + (lax.broadcasted_iota(jnp.int32, shape, 0) & (SLAB - 1))
    visible = lax.broadcasted_iota(jnp.int32, shape, 1) <= position
    for pair in range(HEADS_WIDE // size // 2):
        first, second = (slice((2 * pair + i) * size, (2 * pair + i + 1) * size) for i in range(2))
        block = jnp.concatenate([queries_ref[:, first], queries_ref[:, second]])
        scores = lax.dot_general(
            block, keys, (((1,), (1,)), ((), ())), preferred_element_type=F32
        ) * size ** (-0.5)
        scores = jnp.where(visible, scores, -1e30)
        exp_scores = jnp.exp(scores - jnp.max(scores, axis=1, keepdims=True))
        totals = jnp.sum(exp_scores, axis=1, keepdims=True)
        context = (jnp.dot(exp_scores.astype(BF16), values, preferred_element_type=F32) / totals).astype(BF16)
        out_ref[:, first] = context[:SLAB]
        out_ref[:, second] = context[SLAB:]


def swap(block, axis):
    return lax.ppermute(block, axis, [(0, 1), (1, 0)])


def along_z(block, step):
    return lax.ppermute(block, "z", [(i, (i + step) % RING) for i in range(RING)])


def kernel_call(body, out_shapes, operands, spaces, flops, moved, name, scratch=(), out_space="v", vmem=VMEM_BYTES, aliases=None):
    kinds = {
        "v": pl.BlockSpec(memory_space=pltpu.VMEM),
        "s": pl.BlockSpec(memory_space=pltpu.SMEM),
        "h": pl.BlockSpec(memory_space=pl.ANY),
    }
    return pl.pallas_call(
        body,
        out_shape=[jax.ShapeDtypeStruct(shape, dtype) for shape, dtype in out_shapes],
        in_specs=[kinds[s] for s in spaces],
        out_specs=[kinds[out_space]] * len(out_shapes),
        scratch_shapes=list(scratch),
        input_output_aliases=aliases or {},
        compiler_params=pltpu.CompilerParams(vmem_limit_bytes=vmem),
        cost_estimate=pl.CostEstimate(flops=flops, bytes_accessed=moved, transcendentals=0),
        name=name,
    )(*operands)


def pack_gate_up_kernel(gate_hbm, up_hbm, packed_hbm, held, sems):
    copies = [
        pltpu.make_async_copy(source, held.at[:, pl.ds(i * HIDDEN, HIDDEN)], sems.at[i])
        for i, source in enumerate((gate_hbm, up_hbm))
    ]
    for copy in copies:
        copy.start()
    for copy in copies:
        copy.wait()
    whole = pltpu.make_async_copy(held, packed_hbm.at[:, pl.ds(0, 2 * HIDDEN)], sems.at[2])
    whole.start()
    whole.wait()


def pack_out_kernel(swapped_ref, started_hbm, packed_hbm, sems):
    copies = [
        pltpu.make_async_copy(
            swapped_ref.at[pl.ds(j * 128, 128)],
            packed_hbm.at[:, pl.ds(2 * HIDDEN + j * 128, 128)],
            sems.at[j],
        )
        for j in range(HEADS_WIDE // 128)
    ]
    for copy in copies:
        copy.start()
    for copy in copies:
        copy.wait()


def pack_down_kernel(down_ref, packed_ref):
    for j in range(HIDDEN // 128):
        packed_ref[:, j * 128 : (j + 1) * 128] = down_ref[j * 128 : (j + 1) * 128, :]


def unpack_kernel(place_ref, incoming_ref, hidden_ref, pickers_ref):
    xh = place_ref[3]
    shape = (SLAB, 2 * SLAB)
    to, source = (lax.broadcasted_iota(jnp.int32, shape, d) for d in range(2))
    taken = jnp.where(source == (to >> 3) * 2 * ROWS + (to & 7), 1.0, 0.0).astype(BF16)
    hidden_ref[...] = jnp.dot(taken, incoming_ref[...], preferred_element_type=F32).astype(BF16)
    line = lax.broadcasted_iota(jnp.int32, (2 * ROWS, COLS), 0)
    hits = []
    for slab in range(2):
        rows = incoming_ref[slab * SLAB : slab * SLAB + 2 * ROWS, :].astype(F32)
        both = jnp.sum(jnp.where(line == ROWS + xh, rows, 0.0), axis=0, keepdims=True)
        hits += [both[:, :SLAB], both[:, SLAB:]]
    above, row = (lax.broadcasted_iota(jnp.int32, (SLAB, SLAB), d) for d in range(2))
    earlier = jnp.where(jnp.logical_and(above >> 3 == row >> 3, above <= row), 1.0, 0.0).astype(BF16)
    slots = BLOCKS * CAP
    shape = (slots, SLAB)
    place, row = (lax.broadcasted_iota(jnp.int32, shape, d) for d in range(2))
    number = ((place & (CAP - 1)) + 1).astype(F32)
    for i, hit in enumerate(hits):
        count = jnp.dot(
            jnp.broadcast_to(hit, (ROWS, SLAB)).astype(BF16), earlier, preferred_element_type=F32
        )[:1]
        count = jnp.where(hit > 0.5, count, 0.0)
        named = jnp.logical_and(place >> 2 == row >> 3, count == number)
        pickers_ref[i * slots : (i + 1) * slots, :] = jnp.where(named, 1.0, 0.0).astype(BF16)


def project_kernel(place_ref, hidden_ref, *refs):
    contexts, (weights_hbm, keep_ref, send_ref, weights, sems) = refs[:RING], refs[RING:]
    xl, xh, z = place_ref[0], place_ref[3], place_ref[4]

    def copy(k):
        at = pl.ds(pl.multiple_of(k * 2 * 128, 2 * 128), 2 * 128)
        return pltpu.make_async_copy(
            weights_hbm.at[at, pl.ds(2 * HIDDEN, HEADS_WIDE)], weights.at[at], sems.at[k]
        )

    blocks = [(z + (RING + RING // 2 - step)) & (RING - 1) for step in STEPS]
    for block in blocks:
        copy(block).start()
    for block in blocks:
        copy(block).wait()
    total = jnp.zeros((2 * SLAB, COLS), F32)
    for k in range(RING):
        context = contexts[k][...]
        first = pl.multiple_of(blocks[k] * 256, 256)
        for half in range(2):
            lanes = slice(half * 256, half * 256 + 256)
            block = weights[pl.ds(first, 256), lanes]
            rhs = jnp.concatenate(
                [
                    jnp.concatenate([block[:128, q * 128 : (q + 1) * 128], block[128:, q * 128 : (q + 1) * 128]], axis=1)
                    for q in range(2)
                ]
            )
            total += jnp.dot(context[:, lanes], rhs, preferred_element_type=F32)
    hidden = hidden_ref[...].astype(F32)
    rows = SLAB // 2
    own = jnp.where(xl == 0, hidden[:rows], hidden[rows:])
    other = jnp.where(xl == 0, hidden[rows:], hidden[:rows])
    total += jnp.concatenate(
        [jnp.where(xh == at, block, 0.0) for block in (own, other) for at in range(2)]
    )
    keep_ref[...] = total
    send_ref[...] = total.astype(BF16)


def residual_kernel(place_ref, keep_ref, recv_ref, pickers_ref, residual_ref, rows_ref):
    xl, xh = place_ref[0], place_ref[3]
    summed = keep_ref[...] + recv_ref[...].astype(F32)
    own, other = summed[:SLAB], summed[SLAB:]
    per_expert = BLOCKS * CAP
    held = jnp.zeros((SLAB, COLS), F32)
    for slab in range(2):
        at = slice(slab * SLAB, (slab + 1) * SLAB)
        residual = jnp.where(xl == slab, own, other).astype(BF16)
        held = jnp.where(xh == slab, residual.astype(F32), held)
        picked = jnp.dot(pickers_ref[at, :], residual, preferred_element_type=F32).astype(BF16)
        for f in range(FLIGHT // 2):
            for j in range(GROUP):
                to = ((f * GROUP + j) * 2 + slab) * per_expert
                rows_ref[to : to + per_expert, :] = picked[f * per_expert : (f + 1) * per_expert]
    residual_ref[...] = held.astype(BF16)


def gate_up_kernel(rows_ref, gain_ref, weights_hbm, own_ref, send_ref, weights, sems):
    part = HALF // RING

    def copy(k):
        at = pl.ds(k * part, part)
        return pltpu.make_async_copy(
            weights_hbm.at[at, pl.ds(0, 2 * HIDDEN)], weights.at[at], sems.at[k]
        )

    for k in range(RING):
        copy(k).start()
    slots = BLOCKS * CAP
    total = jnp.zeros((2 * slots, 2 * HIDDEN), F32)
    squares = jnp.zeros((2 * slots, 1), F32)
    for k in range(RING):
        rows = rows_ref[2 * k * slots : 2 * (k + 1) * slots, :].astype(F32)
        squares += jnp.sum(rows * rows, axis=1, keepdims=True)
        scaled = (rows * gain_ref[:, k * part : (k + 1) * part].astype(F32)).astype(BF16)
        copy(k).wait()
        total += jnp.dot(scaled, weights[k * part : (k + 1) * part, :], preferred_element_type=F32)
    own_ref[:, : 2 * HIDDEN] = total
    own_ref[:, 2 * HIDDEN :] = jnp.broadcast_to(squares, (2 * slots, 128))
    send_ref[:, : 2 * HIDDEN] = total.astype(BF16)
    high = squares.astype(BF16)
    rest = squares - high.astype(F32)
    middle = rest.astype(BF16)
    low = (rest - middle.astype(F32)).astype(BF16)
    lane = lax.broadcasted_iota(jnp.int32, (2 * slots, 128), 1)
    tail = jnp.where(lane == 0, high.astype(F32), 0.0)
    tail = jnp.where(lane == 1, middle.astype(F32), tail)
    tail = jnp.where(lane == 2, low.astype(F32), tail)
    send_ref[:, 2 * HIDDEN :] = tail.astype(BF16)


def down_kernel(place_ref, own_ref, recv_ref, residual_ref, weights_hbm, out_ref, weights, sem):
    copy = pltpu.make_async_copy(weights_hbm, weights, sem)
    copy.start()
    xh = place_ref[3]
    slots = 2 * BLOCKS * CAP
    other = recv_ref[:, 2 * HIDDEN :].astype(F32)
    squares = own_ref[:, 2 * HIDDEN : 2 * HIDDEN + 1] + jnp.sum(other, axis=1, keepdims=True)
    inverse = lax.rsqrt(squares / (2 * HALF) + 1e-06)
    total = (own_ref[:, : 2 * HIDDEN] + recv_ref[:, : 2 * HIDDEN].astype(F32)) * inverse
    gate, up = total[:, :HIDDEN], total[:, HIDDEN:]
    activated = (gate / (1.0 + jnp.exp(-gate)) * up).astype(BF16)
    to = lax.broadcasted_iota(jnp.int32, (2 * slots, slots), 0)
    source = lax.broadcasted_iota(jnp.int32, (2 * slots, slots), 1)
    twice = jnp.where(source == (to >> 3) * CAP + (to & 3), 1.0, 0.0).astype(BF16)
    activated = jnp.dot(twice, activated, preferred_element_type=F32).astype(BF16)
    first = (lax.broadcasted_iota(jnp.int32, (2 * slots, COLS), 0) & 4) == 0

    def columns(d):
        rhs = jnp.concatenate(
            [
                jnp.concatenate(
                    [
                        weights[(2 * d + e) * 128 : (2 * d + e + 1) * 128, j * 128 : (j + 1) * 128]
                        for j in range(HIDDEN // 128)
                    ]
                )
                for e in range(2)
            ],
            axis=1,
        )
        return jnp.dot(activated, rhs, preferred_element_type=F32)

    copy.wait()
    chunks = QUARTER // COLS
    for d in range(chunks):
        out_ref[:, d * COLS : (d + 1) * COLS] = jnp.where(first, columns(d), columns(d + chunks)).astype(BF16)
    residual = residual_ref[...].astype(F32)
    out_ref[:SLAB, QUARTER:] = jnp.where(xh == 0, residual, 0.0).astype(BF16)
    out_ref[SLAB:, QUARTER:] = jnp.where(xh == 1, residual, 0.0).astype(BF16)


def combine_kernel(place_ref, coefs_ref, returned_ref, out_ref):
    xl = place_ref[0]
    coefs = coefs_ref[...]
    high = coefs.astype(BF16)
    rest = coefs - high.astype(F32)
    middle = rest.astype(BF16)
    low = (rest - middle.astype(F32)).astype(BF16)
    rows, slots = 4 * ROWS, 2 * BLOCKS * ROWS
    to = lax.broadcasted_iota(jnp.int32, (rows, slots), 0)
    source = lax.broadcasted_iota(jnp.int32, (rows, slots), 1)
    half, quarter, row = to >> 4, (to >> 3) & 1, to & 7
    for k in range(QUARTER // COLS):
        at = slice(k * COLS, (k + 1) * COLS)
        wanted = (half * BLOCKS + xl * RING + quarter * (RING // 2) + k) * ROWS + row
        picker = jnp.where(source == wanted, 1.0, 0.0).astype(BF16)
        parts = returned_ref[:, at]
        mixed = (
            jnp.dot(picker, returned_ref[:, QUARTER:], preferred_element_type=F32)
            + jnp.dot(high, parts, preferred_element_type=F32)
            + (
                jnp.dot(middle, parts, preferred_element_type=F32)
                + jnp.dot(low, parts, preferred_element_type=F32)
            )
        )
        for q in range(4):
            out_ref[:, q * QUARTER + k * COLS : q * QUARTER + (k + 1) * COLS] = mixed[
                q * ROWS : (q + 1) * ROWS
            ].astype(BF16)


def per_device(
    hidden_rows,
    queries,
    keys,
    values,
    slab_start,
    out_weight,
    norm_gain,
    route_ids,
    route_weights,
    flight_experts,
    gate_weight,
    up_weight,
    down_weight,
):
    xl, xh = lax.axis_index("xl"), lax.axis_index("xh")
    tensor_idx = lax.axis_index(TENSOR)
    place = jnp.stack([lax.axis_index(a) for a in DP + TENSOR]).astype(jnp.int32)

    swapped = lax.ppermute(
        out_weight,
        ("y", "z"),
        [
            (a * RING + b, (2 * a - b + RING // 2) % RING * RING + a)
            for a in range(RING)
            for b in range(RING)
        ],
    )
    (context,) = kernel_call(
        attend_kernel,
        [((SLAB, HEADS_WIDE), BF16)],
        (slab_start, queries, keys, values),
        "shhh",
        4 * 512 * 1152 * 128,
        1 << 20,
        "attend",
        [
            pltpu.VMEM(queries.shape, BF16),
            pltpu.VMEM(keys.shape, BF16),
            pltpu.VMEM(values.shape, BF16),
            pltpu.SemaphoreType.DMA((3,)),
        ],
        vmem=ALL_VMEM_BYTES,
    )
    other = swap(context, "xl")
    both = jnp.concatenate([context, other])
    matches = route_ids[:, None, :] == flight_experts[None, :, None]
    hits = jnp.sum(matches.astype(jnp.int32), axis=2, dtype=jnp.int32)
    units = jnp.sum(jnp.where(matches, route_weights[:, None, :], 0), axis=2, dtype=jnp.int32)

    table = jnp.pad(hits.T.astype(BF16).reshape(2, COLS), ((0, ROWS - 2), (0, 0)))
    outgoing = jnp.concatenate(
        [hidden_rows.reshape(ROWS, BLOCKS, COLS).transpose(1, 0, 2), jnp.broadcast_to(table, (BLOCKS, ROWS, COLS))],
        axis=1,
    )
    gain = lax.dynamic_slice(norm_gain, (xl * HALF,), (HALF,)).reshape(1, HALF)
    (packed_down,) = kernel_call(
        pack_down_kernel, [((128, HIDDEN), BF16)], (down_weight,), "v", 0, 4 * 128 * 384, "pack_down"
    )
    (started,) = kernel_call(
        pack_gate_up_kernel,
        [((128, 2 * HIDDEN + HEADS_WIDE), BF16)],
        (gate_weight, up_weight),
        "hh",
        0,
        4 * 128 * 768,
        "pack_gate_up",
        [pltpu.VMEM((128, 2 * HIDDEN), BF16), pltpu.SemaphoreType.DMA((3,))],
        "h",
        MOST_VMEM_BYTES,
    )
    swapped, started, _ = lax.optimization_barrier((swapped, started, other))
    (packed,) = kernel_call(
        pack_out_kernel,
        [((128, 2 * HIDDEN + HEADS_WIDE), BF16)],
        (swapped, started),
        "vh",
        0,
        4 * 128 * 512,
        "pack_out",
        [pltpu.SemaphoreType.DMA((HEADS_WIDE // 128,))],
        "h",
        vmem=MOST_VMEM_BYTES,
        aliases={1: 0},
    )
    weights = lax.all_gather(packed, ("y", "core"), axis=0, tiled=True)
    packed_down, _ = lax.optimization_barrier((packed_down, packed))
    down_weights = lax.all_gather(packed_down, ("y", "core"), axis=0, tiled=True)
    up1, down1 = along_z(both, 1), along_z(both, -1)
    up2, down2 = along_z(up1, 1), along_z(down1, -1)
    up3, down3 = along_z(up2, 1), along_z(down2, -1)
    up4 = along_z(up3, 1)

    outgoing, _ = lax.optimization_barrier((outgoing, up1))
    incoming = lax.all_to_all(outgoing, ("xl", "z"), split_axis=0, concat_axis=0, tiled=True)
    hidden_in, pickers = kernel_call(
        unpack_kernel,
        [((SLAB, COLS), BF16), ((2 * (FLIGHT // 2) * BLOCKS * CAP, SLAB), BF16)],
        (place, incoming.reshape(2 * SLAB, COLS)),
        "sv",
        0,
        1 << 18,
        "unpack",
    )
    hits_mine = lax.dynamic_slice_in_dim(hits, tensor_idx * ROWS, ROWS, 0)
    coef = lax.dynamic_slice_in_dim(units, tensor_idx * ROWS, ROWS, 0).astype(F32) / 65536.0
    slot_mine = jnp.cumsum(hits_mine, axis=0) - 1
    mine = jnp.where(
        jnp.logical_and(
            hits_mine[..., None] == 1, slot_mine[..., None] == jnp.arange(CAP, dtype=jnp.int32)
        ),
        coef[..., None],
        0.0,
    )
    two = jnp.eye(2, dtype=F32)
    coefs = (
        mine[None, None, :, None, :, None, None, :]
        * two[:, None, None, :, None, None, None, None]
        * two[None, :, None, None, None, None, :, None]
    )
    coefs = jnp.broadcast_to(coefs, (2, 2, ROWS, 2, FLIGHT, GROUP, 2, CAP)).reshape(
        4 * ROWS, 2 * BLOCKS * 2 * CAP
    )
    weights, pickers, coefs, gain = lax.optimization_barrier((weights, pickers, coefs, gain))

    keep, send = kernel_call(
        project_kernel,
        [((2 * SLAB, COLS), F32), ((2 * SLAB, COLS), BF16)],
        (place, hidden_in, both, up1, down1, up2, down2, up3, down3, up4, weights),
        "sv" + "v" * RING + "h",
        2 * 256 * 4096 * 256,
        2 * 2048 * 1024,
        "project",
        [pltpu.VMEM((HALF, HEADS_WIDE), BF16), pltpu.SemaphoreType.DMA((RING,))],
    )
    residual, rows_out = kernel_call(
        residual_kernel,
        [((SLAB, COLS), BF16), ((RING * 2 * BLOCKS * CAP, COLS), BF16)],
        (place, keep, swap(send, "xh"), pickers),
        "svvv",
        2 * 256 * 128 * 256,
        1 << 20,
        "residual",
    )
    rows_in = lax.all_to_all(
        rows_out.reshape(RING, 2 * BLOCKS * CAP, COLS), "z", split_axis=0, concat_axis=0, tiled=True
    ).reshape(RING * 2 * BLOCKS * CAP, COLS)
    own, part = kernel_call(
        gate_up_kernel,
        [((2 * BLOCKS * CAP, 2 * HIDDEN + 128), F32), ((2 * BLOCKS * CAP, 2 * HIDDEN + 128), BF16)],
        (rows_in, gain, weights),
        "vvh",
        2 * 128 * 2048 * 768,
        3 << 20,
        "gate_up",
        [pltpu.VMEM((HALF, 2 * HIDDEN), BF16), pltpu.SemaphoreType.DMA((RING,))],
    )
    (outward,) = kernel_call(
        down_kernel,
        [((4 * BLOCKS * CAP, QUARTER + COLS), BF16)],
        (place, own, swap(part, "xl"), residual, down_weights),
        "svvvh",
        2 * 256 * 384 * 2048,
        2 << 20,
        "down",
        [pltpu.VMEM((HALF, HIDDEN), BF16), pltpu.SemaphoreType.DMA],
        vmem=DOWN_VMEM_BYTES,
    )
    returned = lax.all_to_all(
        outward.reshape(2 * BLOCKS, 2 * CAP, QUARTER + COLS),
        PAIR_TENSOR,
        split_axis=0,
        concat_axis=0,
        tiled=True,
    ).reshape(4 * BLOCKS * CAP, QUARTER + COLS)
    (mixed,) = kernel_call(
        combine_kernel,
        [((ROWS, 2 * HALF), BF16)],
        (place, coefs, returned),
        "svv",
        2 * 128 * 256 * 1024,
        1 << 20,
        "combine",
    )
    return mixed


def solution(mesh):
    fine = Mesh(mesh.devices.reshape(2, RING, 2, 2, RING), DP + TENSOR)
    placed = (
        P(DP + TENSOR, None),
        P(DP, TENSOR),
        P(DP, TENSOR),
        P(DP, TENSOR),
        P(DP),
        P(TENSOR, DP),
        P(),
        P(DP, None),
        P(DP, None),
        P(),
        P(DP, TENSOR),
        P(DP, TENSOR),
        P(TENSOR, DP),
    )
    return jax.shard_map(
        per_device, mesh=fine, in_specs=placed, out_specs=P(DP + TENSOR, None), check_vma=False
    )
```

```python
import jax
import jax.numpy as jnp
from jax import lax
from jax.experimental import pallas as pl
from jax.experimental.pallas import tpu as pltpu
from jax.sharding import Mesh
from jax.sharding import PartitionSpec as P

DP = ("xl", "y", "core")
TENSOR = ("xh", "z")
PAIR_TENSOR = ("xl",) + TENSOR
RING = 8
STEPS = (0, -1, 1, -2, 2, -3, 3, 4)
SLAB = 128
HALF = 2048
QUARTER = 1024
COLS = 256
HIDDEN = 384
HEADS_WIDE = 512
CAP = 4
FLIGHT = 4
GROUP = 4
BLOCKS = 16
ROWS = 8
VMEM_BYTES = 48 * 1024 * 1024
ALL_VMEM_BYTES = 63400000
MOST_VMEM_BYTES = 57000000
DOWN_VMEM_BYTES = 55000000
F32, BF16 = jnp.float32, jnp.bfloat16


def attend_kernel(
    start_ref, queries_hbm, keys_hbm, values_hbm, out_ref, queries_ref, keys_ref, values_ref, sems
):
    copies = [
        pltpu.make_async_copy(source, target, sems.at[i])
        for i, (source, target) in enumerate(
            ((keys_hbm, keys_ref), (queries_hbm, queries_ref), (values_hbm, values_ref))
        )
    ]
    for copy in copies:
        copy.start()
    for copy in copies:
        copy.wait()
    keys, values = keys_ref[...], values_ref[...]
    size = keys.shape[1]
    shape = (2 * SLAB, keys.shape[0])
    position = start_ref[0] + (lax.broadcasted_iota(jnp.int32, shape, 0) & (SLAB - 1))
    visible = lax.broadcasted_iota(jnp.int32, shape, 1) <= position
    for pair in range(HEADS_WIDE // size // 2):
        first, second = (slice((2 * pair + i) * size, (2 * pair + i + 1) * size) for i in range(2))
        block = jnp.concatenate([queries_ref[:, first], queries_ref[:, second]])
        scores = lax.dot_general(
            block, keys, (((1,), (1,)), ((), ())), preferred_element_type=F32
        ) * size ** (-0.5)
        scores = jnp.where(visible, scores, -1e30)
        exp_scores = jnp.exp(scores - jnp.max(scores, axis=1, keepdims=True))
        totals = jnp.sum(exp_scores, axis=1, keepdims=True)
        context = (jnp.dot(exp_scores.astype(BF16), values, preferred_element_type=F32) / totals).astype(BF16)
        out_ref[:, first] = context[:SLAB]
        out_ref[:, second] = context[SLAB:]


def swap(block, axis):
    return lax.ppermute(block, axis, [(0, 1), (1, 0)])


def along_z(block, step):
    return lax.ppermute(block, "z", [(i, (i + step) % RING) for i in range(RING)])


def kernel_call(body, out_shapes, operands, spaces, flops, moved, name, scratch=(), out_space="v", vmem=VMEM_BYTES, aliases=None):
    kinds = {
        "v": pl.BlockSpec(memory_space=pltpu.VMEM),
        "s": pl.BlockSpec(memory_space=pltpu.SMEM),
        "h": pl.BlockSpec(memory_space=pl.ANY),
    }
    return pl.pallas_call(
        body,
        out_shape=[jax.ShapeDtypeStruct(shape, dtype) for shape, dtype in out_shapes],
        in_specs=[kinds[s] for s in spaces],
        out_specs=[kinds[out_space]] * len(out_shapes),
        scratch_shapes=list(scratch),
        input_output_aliases=aliases or {},
        compiler_params=pltpu.CompilerParams(vmem_limit_bytes=vmem),
        cost_estimate=pl.CostEstimate(flops=flops, bytes_accessed=moved, transcendentals=0),
        name=name,
    )(*operands)


def pack_gate_up_kernel(gate_hbm, up_hbm, packed_hbm, held, sems):
    copies = [
        pltpu.make_async_copy(source, held.at[:, pl.ds(i * HIDDEN, HIDDEN)], sems.at[i])
        for i, source in enumerate((gate_hbm, up_hbm))
    ]
    for copy in copies:
        copy.start()
    for copy in copies:
        copy.wait()
    whole = pltpu.make_async_copy(held, packed_hbm.at[:, pl.ds(0, 2 * HIDDEN)], sems.at[2])
    whole.start()
    whole.wait()


def pack_out_kernel(swapped_ref, started_hbm, packed_hbm, sems):
    copies = [
        pltpu.make_async_copy(
            swapped_ref.at[pl.ds(j * 128, 128)],
            packed_hbm.at[:, pl.ds(2 * HIDDEN + j * 128, 128)],
            sems.at[j],
        )
        for j in range(HEADS_WIDE // 128)
    ]
    for copy in copies:
        copy.start()
    for copy in copies:
        copy.wait()


def pack_down_kernel(down_ref, packed_ref):
    for j in range(HIDDEN // 128):
        packed_ref[:, j * 128 : (j + 1) * 128] = down_ref[j * 128 : (j + 1) * 128, :]


def unpack_kernel(place_ref, incoming_ref, hidden_ref, pickers_ref):
    xh = place_ref[3]
    shape = (SLAB, 2 * SLAB)
    to, source = (lax.broadcasted_iota(jnp.int32, shape, d) for d in range(2))
    taken = jnp.where(source == (to >> 3) * 2 * ROWS + (to & 7), 1.0, 0.0).astype(BF16)
    hidden_ref[...] = jnp.dot(taken, incoming_ref[...], preferred_element_type=F32).astype(BF16)
    line = lax.broadcasted_iota(jnp.int32, (2 * ROWS, COLS), 0)
    hits = []
    for slab in range(2):
        rows = incoming_ref[slab * SLAB : slab * SLAB + 2 * ROWS, :].astype(F32)
        both = jnp.sum(jnp.where(line == ROWS + xh, rows, 0.0), axis=0, keepdims=True)
        hits += [both[:, :SLAB], both[:, SLAB:]]
    above, row = (lax.broadcasted_iota(jnp.int32, (SLAB, SLAB), d) for d in range(2))
    earlier = jnp.where(jnp.logical_and(above >> 3 == row >> 3, above <= row), 1.0, 0.0).astype(BF16)
    slots = BLOCKS * CAP
    shape = (slots, SLAB)
    place, row = (lax.broadcasted_iota(jnp.int32, shape, d) for d in range(2))
    number = ((place & (CAP - 1)) + 1).astype(F32)
    for i, hit in enumerate(hits):
        count = jnp.dot(
            jnp.broadcast_to(hit, (ROWS, SLAB)).astype(BF16), earlier, preferred_element_type=F32
        )[:1]
        count = jnp.where(hit > 0.5, count, 0.0)
        named = jnp.logical_and(place >> 2 == row >> 3, count == number)
        pickers_ref[i * slots : (i + 1) * slots, :] = jnp.where(named, 1.0, 0.0).astype(BF16)


def project_kernel(place_ref, hidden_ref, *refs):
    contexts, (weights_hbm, keep_ref, send_ref, weights, sems) = refs[:RING], refs[RING:]
    xl, xh, z = place_ref[0], place_ref[3], place_ref[4]

    def copy(k):
        at = pl.ds(pl.multiple_of(k * 2 * 128, 2 * 128), 2 * 128)
        return pltpu.make_async_copy(
            weights_hbm.at[at, pl.ds(2 * HIDDEN, HEADS_WIDE)], weights.at[at], sems.at[k]
        )

    blocks = [(z + (RING + RING // 2 - step)) & (RING - 1) for step in STEPS]
    for block in blocks:
        copy(block).start()
    for block in blocks:
        copy(block).wait()
    total = jnp.zeros((2 * SLAB, COLS), F32)
    for k in range(RING):
        context = contexts[k][...]
        first = pl.multiple_of(blocks[k] * 256, 256)
        for half in range(2):
            lanes = slice(half * 256, half * 256 + 256)
            block = weights[pl.ds(first, 256), lanes]
            rhs = jnp.concatenate(
                [
                    jnp.concatenate([block[:128, q * 128 : (q + 1) * 128], block[128:, q * 128 : (q + 1) * 128]], axis=1)
                    for q in range(2)
                ]
            )
            total += jnp.dot(context[:, lanes], rhs, preferred_element_type=F32)
    hidden = hidden_ref[...].astype(F32)
    rows = SLAB // 2
    own = jnp.where(xl == 0, hidden[:rows], hidden[rows:])
    other = jnp.where(xl == 0, hidden[rows:], hidden[:rows])
    total += jnp.concatenate(
        [jnp.where(xh == at, block, 0.0) for block in (own, other) for at in range(2)]
    )
    keep_ref[...] = total
    send_ref[...] = total.astype(BF16)


def residual_kernel(place_ref, keep_ref, recv_ref, pickers_ref, residual_ref, rows_ref):
    xl, xh = place_ref[0], place_ref[3]
    summed = keep_ref[...] + recv_ref[...].astype(F32)
    own, other = summed[:SLAB], summed[SLAB:]
    per_expert = BLOCKS * CAP
    held = jnp.zeros((SLAB, COLS), F32)
    for slab in range(2):
        at = slice(slab * SLAB, (slab + 1) * SLAB)
        residual = jnp.where(xl == slab, own, other).astype(BF16)
        held = jnp.where(xh == slab, residual.astype(F32), held)
        picked = jnp.dot(pickers_ref[at, :], residual, preferred_element_type=F32).astype(BF16)
        for f in range(FLIGHT // 2):
            for j in range(GROUP):
                to = ((f * GROUP + j) * 2 + slab) * per_expert
                rows_ref[to : to + per_expert, :] = picked[f * per_expert : (f + 1) * per_expert]
    residual_ref[...] = held.astype(BF16)


def gate_up_kernel(rows_ref, gain_ref, weights_hbm, own_ref, send_ref, weights, sems):
    part = HALF // RING

    def copy(k):
        at = pl.ds(k * part, part)
        return pltpu.make_async_copy(
            weights_hbm.at[at, pl.ds(0, 2 * HIDDEN)], weights.at[at], sems.at[k]
        )

    for k in range(RING):
        copy(k).start()
    slots = BLOCKS * CAP
    total = jnp.zeros((2 * slots, 2 * HIDDEN), F32)
    squares = jnp.zeros((2 * slots, 1), F32)
    for k in range(RING):
        rows = rows_ref[2 * k * slots : 2 * (k + 1) * slots, :].astype(F32)
        squares += jnp.sum(rows * rows, axis=1, keepdims=True)
        scaled = (rows * gain_ref[:, k * part : (k + 1) * part].astype(F32)).astype(BF16)
        copy(k).wait()
        total += jnp.dot(scaled, weights[k * part : (k + 1) * part, :], preferred_element_type=F32)
    own_ref[:, : 2 * HIDDEN] = total
    own_ref[:, 2 * HIDDEN :] = jnp.broadcast_to(squares, (2 * slots, 128))
    send_ref[:, : 2 * HIDDEN] = total.astype(BF16)
    high = squares.astype(BF16)
    rest = squares - high.astype(F32)
    middle = rest.astype(BF16)
    low = (rest - middle.astype(F32)).astype(BF16)
    lane = lax.broadcasted_iota(jnp.int32, (2 * slots, 128), 1)
    tail = jnp.where(lane == 0, high.astype(F32), 0.0)
    tail = jnp.where(lane == 1, middle.astype(F32), tail)
    tail = jnp.where(lane == 2, low.astype(F32), tail)
    send_ref[:, 2 * HIDDEN :] = tail.astype(BF16)


def down_kernel(place_ref, own_ref, recv_ref, residual_ref, weights_hbm, out_ref, weights, sem):
    copy = pltpu.make_async_copy(weights_hbm, weights, sem)
    copy.start()
    xh = place_ref[3]
    slots = 2 * BLOCKS * CAP
    other = recv_ref[:, 2 * HIDDEN :].astype(F32)
    squares = own_ref[:, 2 * HIDDEN : 2 * HIDDEN + 1] + jnp.sum(other, axis=1, keepdims=True)
    inverse = lax.rsqrt(squares / (2 * HALF) + 1e-06)
    total = (own_ref[:, : 2 * HIDDEN] + recv_ref[:, : 2 * HIDDEN].astype(F32)) * inverse
    gate, up = total[:, :HIDDEN], total[:, HIDDEN:]
    activated = (gate / (1.0 + jnp.exp(-gate)) * up).astype(BF16)
    to = lax.broadcasted_iota(jnp.int32, (2 * slots, 2 * slots), 0)
    source = lax.broadcasted_iota(jnp.int32, (2 * slots, 2 * slots), 1)
    wanted = ((to >> 2) & 1) * slots + (to >> 3) * CAP + (to & 3)
    spread = jnp.where(source == wanted, 1.0, 0.0).astype(BF16)

    def columns(d):
        rhs = jnp.concatenate(
            [
                jnp.concatenate(
                    [
                        weights[(2 * d + e) * 128 : (2 * d + e + 1) * 128, j * 128 : (j + 1) * 128]
                        for j in range(HIDDEN // 128)
                    ]
                )
                for e in range(2)
            ],
            axis=1,
        )
        return jnp.dot(activated, rhs, preferred_element_type=F32).astype(BF16)

    copy.wait()
    chunks = QUARTER // COLS
    for d in range(chunks):
        both = jnp.concatenate([columns(d), columns(d + chunks)])
        out_ref[:, d * COLS : (d + 1) * COLS] = jnp.dot(spread, both, preferred_element_type=F32).astype(BF16)
    residual = residual_ref[...].astype(F32)
    out_ref[:SLAB, QUARTER:] = jnp.where(xh == 0, residual, 0.0).astype(BF16)
    out_ref[SLAB:, QUARTER:] = jnp.where(xh == 1, residual, 0.0).astype(BF16)


def combine_kernel(place_ref, coefs_ref, returned_ref, out_ref):
    xl = place_ref[0]
    coefs = coefs_ref[...]
    high = coefs.astype(BF16)
    rest = coefs - high.astype(F32)
    middle = rest.astype(BF16)
    low = (rest - middle.astype(F32)).astype(BF16)
    parts = jnp.concatenate([high, middle, low])
    rows, slots = 4 * ROWS, 2 * BLOCKS * ROWS
    chunks = QUARTER // COLS
    to = lax.broadcasted_iota(jnp.int32, (chunks * rows, slots), 0)
    source = lax.broadcasted_iota(jnp.int32, (chunks * rows, slots), 1)
    chunk, half, quarter, row = to >> 5, (to >> 4) & 1, (to >> 3) & 1, to & 7
    wanted = (half * BLOCKS + xl * RING + quarter * (RING // 2) + chunk) * ROWS + row
    picker = jnp.where(source == wanted, 1.0, 0.0).astype(BF16)
    residual = jnp.dot(picker, returned_ref[:, QUARTER:], preferred_element_type=F32)
    for k in range(chunks):
        sums = jnp.dot(parts, returned_ref[:, k * COLS : (k + 1) * COLS], preferred_element_type=F32)
        mixed = residual[k * rows : (k + 1) * rows] + sums[:rows] + (sums[rows : 2 * rows] + sums[2 * rows :])
        for q in range(4):
            out_ref[:, q * QUARTER + k * COLS : q * QUARTER + (k + 1) * COLS] = mixed[
                q * ROWS : (q + 1) * ROWS
            ].astype(BF16)


def per_device(
    hidden_rows,
    queries,
    keys,
    values,
    slab_start,
    out_weight,
    norm_gain,
    route_ids,
    route_weights,
    flight_experts,
    gate_weight,
    up_weight,
    down_weight,
):
    xl, xh = lax.axis_index("xl"), lax.axis_index("xh")
    tensor_idx = lax.axis_index(TENSOR)
    place = jnp.stack([lax.axis_index(a) for a in DP + TENSOR]).astype(jnp.int32)

    swapped = lax.ppermute(
        out_weight,
        ("y", "z"),
        [
            (a * RING + b, (2 * a - b + RING // 2) % RING * RING + a)
            for a in range(RING)
            for b in range(RING)
        ],
    )
    (context,) = kernel_call(
        attend_kernel,
        [((SLAB, HEADS_WIDE), BF16)],
        (slab_start, queries, keys, values),
        "shhh",
        4 * 512 * 1152 * 128,
        1 << 20,
        "attend",
        [
            pltpu.VMEM(queries.shape, BF16),
            pltpu.VMEM(keys.shape, BF16),
            pltpu.VMEM(values.shape, BF16),
            pltpu.SemaphoreType.DMA((3,)),
        ],
        vmem=ALL_VMEM_BYTES,
    )
    other = swap(context, "xl")
    both = jnp.concatenate([context, other])
    matches = route_ids[:, None, :] == flight_experts[None, :, None]
    hits = jnp.sum(matches.astype(jnp.int32), axis=2, dtype=jnp.int32)
    units = jnp.sum(jnp.where(matches, route_weights[:, None, :], 0), axis=2, dtype=jnp.int32)

    table = jnp.pad(hits.T.astype(BF16).reshape(2, COLS), ((0, ROWS - 2), (0, 0)))
    outgoing = jnp.concatenate(
        [hidden_rows.reshape(ROWS, BLOCKS, COLS).transpose(1, 0, 2), jnp.broadcast_to(table, (BLOCKS, ROWS, COLS))],
        axis=1,
    )
    gain = lax.dynamic_slice(norm_gain, (xl * HALF,), (HALF,)).reshape(1, HALF)
    (packed_down,) = kernel_call(
        pack_down_kernel, [((128, HIDDEN), BF16)], (down_weight,), "v", 0, 4 * 128 * 384, "pack_down"
    )
    (started,) = kernel_call(
        pack_gate_up_kernel,
        [((128, 2 * HIDDEN + HEADS_WIDE), BF16)],
        (gate_weight, up_weight),
        "hh",
        0,
        4 * 128 * 768,
        "pack_gate_up",
        [pltpu.VMEM((128, 2 * HIDDEN), BF16), pltpu.SemaphoreType.DMA((3,))],
        "h",
        MOST_VMEM_BYTES,
    )
    swapped, started, _ = lax.optimization_barrier((swapped, started, other))
    (packed,) = kernel_call(
        pack_out_kernel,
        [((128, 2 * HIDDEN + HEADS_WIDE), BF16)],
        (swapped, started),
        "vh",
        0,
        4 * 128 * 512,
        "pack_out",
        [pltpu.SemaphoreType.DMA((HEADS_WIDE // 128,))],
        "h",
        vmem=MOST_VMEM_BYTES,
        aliases={1: 0},
    )
    weights = lax.all_gather(packed, ("y", "core"), axis=0, tiled=True)
    packed_down, _ = lax.optimization_barrier((packed_down, packed))
    down_weights = lax.all_gather(packed_down, ("y", "core"), axis=0, tiled=True)
    up1, down1 = along_z(both, 1), along_z(both, -1)
    up2, down2 = along_z(up1, 1), along_z(down1, -1)
    up3, down3 = along_z(up2, 1), along_z(down2, -1)
    up4 = along_z(up3, 1)

    outgoing, _ = lax.optimization_barrier((outgoing, up1))
    incoming = lax.all_to_all(outgoing, ("xl", "z"), split_axis=0, concat_axis=0, tiled=True)
    hidden_in, pickers = kernel_call(
        unpack_kernel,
        [((SLAB, COLS), BF16), ((2 * (FLIGHT // 2) * BLOCKS * CAP, SLAB), BF16)],
        (place, incoming.reshape(2 * SLAB, COLS)),
        "sv",
        0,
        1 << 18,
        "unpack",
    )
    hits_mine = lax.dynamic_slice_in_dim(hits, tensor_idx * ROWS, ROWS, 0)
    coef = lax.dynamic_slice_in_dim(units, tensor_idx * ROWS, ROWS, 0).astype(F32) / 65536.0
    slot_mine = jnp.cumsum(hits_mine, axis=0) - 1
    mine = jnp.where(
        jnp.logical_and(
            hits_mine[..., None] == 1, slot_mine[..., None] == jnp.arange(CAP, dtype=jnp.int32)
        ),
        coef[..., None],
        0.0,
    )
    two = jnp.eye(2, dtype=F32)
    coefs = (
        mine[None, None, :, None, :, None, None, :]
        * two[:, None, None, :, None, None, None, None]
        * two[None, :, None, None, None, None, :, None]
    )
    coefs = jnp.broadcast_to(coefs, (2, 2, ROWS, 2, FLIGHT, GROUP, 2, CAP)).reshape(
        4 * ROWS, 2 * BLOCKS * 2 * CAP
    )
    weights, pickers, coefs, gain = lax.optimization_barrier((weights, pickers, coefs, gain))

    keep, send = kernel_call(
        project_kernel,
        [((2 * SLAB, COLS), F32), ((2 * SLAB, COLS), BF16)],
        (place, hidden_in, both, up1, down1, up2, down2, up3, down3, up4, weights),
        "sv" + "v" * RING + "h",
        2 * 256 * 4096 * 256,
        2 * 2048 * 1024,
        "project",
        [pltpu.VMEM((HALF, HEADS_WIDE), BF16), pltpu.SemaphoreType.DMA((RING,))],
    )
    residual, rows_out = kernel_call(
        residual_kernel,
        [((SLAB, COLS), BF16), ((RING * 2 * BLOCKS * CAP, COLS), BF16)],
        (place, keep, swap(send, "xh"), pickers),
        "svvv",
        2 * 256 * 128 * 256,
        1 << 20,
        "residual",
    )
    rows_in = lax.all_to_all(
        rows_out.reshape(RING, 2 * BLOCKS * CAP, COLS), "z", split_axis=0, concat_axis=0, tiled=True
    ).reshape(RING * 2 * BLOCKS * CAP, COLS)
    own, part = kernel_call(
        gate_up_kernel,
        [((2 * BLOCKS * CAP, 2 * HIDDEN + 128), F32), ((2 * BLOCKS * CAP, 2 * HIDDEN + 128), BF16)],
        (rows_in, gain, weights),
        "vvh",
        2 * 128 * 2048 * 768,
        3 << 20,
        "gate_up",
        [pltpu.VMEM((HALF, 2 * HIDDEN), BF16), pltpu.SemaphoreType.DMA((RING,))],
    )
    (outward,) = kernel_call(
        down_kernel,
        [((4 * BLOCKS * CAP, QUARTER + COLS), BF16)],
        (place, own, swap(part, "xl"), residual, down_weights),
        "svvvh",
        2 * 256 * 384 * 2048,
        2 << 20,
        "down",
        [pltpu.VMEM((HALF, HIDDEN), BF16), pltpu.SemaphoreType.DMA],
        vmem=DOWN_VMEM_BYTES,
    )
    returned = lax.all_to_all(
        outward.reshape(2 * BLOCKS, 2 * CAP, QUARTER + COLS),
        PAIR_TENSOR,
        split_axis=0,
        concat_axis=0,
        tiled=True,
    ).reshape(4 * BLOCKS * CAP, QUARTER + COLS)
    (mixed,) = kernel_call(
        combine_kernel,
        [((ROWS, 2 * HALF), BF16)],
        (place, coefs, returned),
        "svv",
        2 * 128 * 256 * 1024,
        1 << 20,
        "combine",
    )
    return mixed


def solution(mesh):
    fine = Mesh(mesh.devices.reshape(2, RING, 2, 2, RING), DP + TENSOR)
    placed = (
        P(DP + TENSOR, None),
        P(DP, TENSOR),
        P(DP, TENSOR),
        P(DP, TENSOR),
        P(DP),
        P(TENSOR, DP),
        P(),
        P(DP, None),
        P(DP, None),
        P(),
        P(DP, TENSOR),
        P(DP, TENSOR),
        P(TENSOR, DP),
    )
    return jax.shard_map(
        per_device, mesh=fine, in_specs=placed, out_specs=P(DP + TENSOR, None), check_vma=False
    )
```

```python
import jax
import jax.numpy as jnp
from jax import lax
from jax.experimental import pallas as pl
from jax.experimental.pallas import tpu as pltpu
from jax.sharding import Mesh
from jax.sharding import PartitionSpec as P

DP = ("xl", "y", "core")
TENSOR = ("xh", "z")
PAIR_TENSOR = ("xl",) + TENSOR
RING = 8
STEPS = (0, -1, 1, -2, 2, -3, 3, 4)
SLAB = 128
HALF = 2048
QUARTER = 1024
COLS = 256
HIDDEN = 384
HEADS_WIDE = 512
CAP = 4
FLIGHT = 4
GROUP = 4
BLOCKS = 16
ROWS = 8
VMEM_BYTES = 48 * 1024 * 1024
ALL_VMEM_BYTES = 63400000
MOST_VMEM_BYTES = 57000000
DOWN_VMEM_BYTES = 55000000
F32, BF16 = jnp.float32, jnp.bfloat16


def attend_kernel(
    start_ref, queries_hbm, keys_hbm, values_hbm, out_ref, queries_ref, keys_ref, values_ref, sems
):
    copies = [
        pltpu.make_async_copy(source, target, sems.at[i])
        for i, (source, target) in enumerate(
            ((keys_hbm, keys_ref), (queries_hbm, queries_ref), (values_hbm, values_ref))
        )
    ]
    for copy in copies:
        copy.start()
    for copy in copies[:2]:
        copy.wait()
    keys = keys_ref[...]
    size = keys.shape[1]
    shape = (2 * SLAB, keys.shape[0])
    position = start_ref[0] + (lax.broadcasted_iota(jnp.int32, shape, 0) & (SLAB - 1))
    visible = lax.broadcasted_iota(jnp.int32, shape, 1) <= position
    for pair in range(HEADS_WIDE // size // 2):
        first, second = (slice((2 * pair + i) * size, (2 * pair + i + 1) * size) for i in range(2))
        block = jnp.concatenate([queries_ref[:, first], queries_ref[:, second]])
        scores = lax.dot_general(
            block, keys, (((1,), (1,)), ((), ())), preferred_element_type=F32
        ) * size ** (-0.5)
        scores = jnp.where(visible, scores, -1e30)
        exp_scores = jnp.exp(scores - jnp.max(scores, axis=1, keepdims=True))
        totals = jnp.sum(exp_scores, axis=1, keepdims=True)
        if pair == 0:
            copies[2].wait()
        values = values_ref[...]
        context = (jnp.dot(exp_scores.astype(BF16), values, preferred_element_type=F32) / totals).astype(BF16)
        out_ref[:, first] = context[:SLAB]
        out_ref[:, second] = context[SLAB:]


def swap(block, axis):
    return lax.ppermute(block, axis, [(0, 1), (1, 0)])


def along_z(block, step):
    return lax.ppermute(block, "z", [(i, (i + step) % RING) for i in range(RING)])


def kernel_call(body, out_shapes, operands, spaces, flops, moved, name, scratch=(), out_space="v", vmem=VMEM_BYTES, aliases=None):
    kinds = {
        "v": pl.BlockSpec(memory_space=pltpu.VMEM),
        "s": pl.BlockSpec(memory_space=pltpu.SMEM),
        "h": pl.BlockSpec(memory_space=pl.ANY),
    }
    return pl.pallas_call(
        body,
        out_shape=[jax.ShapeDtypeStruct(shape, dtype) for shape, dtype in out_shapes],
        in_specs=[kinds[s] for s in spaces],
        out_specs=[kinds[out_space]] * len(out_shapes),
        scratch_shapes=list(scratch),
        input_output_aliases=aliases or {},
        compiler_params=pltpu.CompilerParams(vmem_limit_bytes=vmem),
        cost_estimate=pl.CostEstimate(flops=flops, bytes_accessed=moved, transcendentals=0),
        name=name,
    )(*operands)


def pack_gate_up_kernel(gate_hbm, up_hbm, packed_hbm, held, sems):
    copies = [
        pltpu.make_async_copy(source, held.at[:, pl.ds(i * HIDDEN, HIDDEN)], sems.at[i])
        for i, source in enumerate((gate_hbm, up_hbm))
    ]
    for copy in copies:
        copy.start()
    for copy in copies:
        copy.wait()
    whole = pltpu.make_async_copy(held, packed_hbm.at[:, pl.ds(0, 2 * HIDDEN)], sems.at[2])
    whole.start()
    whole.wait()


def pack_out_kernel(swapped_hbm, started_hbm, packed_hbm, held, in_sems, out_sems):
    arriving, leaving = [], []
    for j in range(HEADS_WIDE // 128):
        at = pl.ds(j * 128, 128)
        to = packed_hbm.at[:, pl.ds(2 * HIDDEN + j * 128, 128)]
        arriving.append(pltpu.make_async_copy(swapped_hbm.at[at], held.at[at], in_sems.at[j]))
        leaving.append(pltpu.make_async_copy(held.at[at], to, out_sems.at[j]))
    for copy in arriving:
        copy.start()
    for arrived, copy in zip(arriving, leaving):
        arrived.wait()
        copy.start()
    for copy in leaving:
        copy.wait()


def pack_down_kernel(down_ref, packed_ref):
    for j in range(HIDDEN // 128):
        packed_ref[:, j * 128 : (j + 1) * 128] = down_ref[j * 128 : (j + 1) * 128, :]


def unpack_kernel(place_ref, incoming_ref, hidden_ref, pickers_ref):
    xh = place_ref[3]
    shape = (SLAB, 2 * SLAB)
    to, source = (lax.broadcasted_iota(jnp.int32, shape, d) for d in range(2))
    taken = jnp.where(source == (to >> 3) * 2 * ROWS + (to & 7), 1.0, 0.0).astype(BF16)
    hidden_ref[...] = jnp.dot(taken, incoming_ref[...], preferred_element_type=F32).astype(BF16)
    line = lax.broadcasted_iota(jnp.int32, (2 * ROWS, COLS), 0)
    hits = []
    for slab in range(2):
        rows = incoming_ref[slab * SLAB : slab * SLAB + 2 * ROWS, :].astype(F32)
        both = jnp.sum(jnp.where(line == ROWS + xh, rows, 0.0), axis=0, keepdims=True)
        hits += [both[:, :SLAB], both[:, SLAB:]]
    above, row = (lax.broadcasted_iota(jnp.int32, (SLAB, SLAB), d) for d in range(2))
    earlier = jnp.where(jnp.logical_and(above >> 3 == row >> 3, above <= row), 1.0, 0.0).astype(BF16)
    slots = BLOCKS * CAP
    shape = (slots, SLAB)
    place, row = (lax.broadcasted_iota(jnp.int32, shape, d) for d in range(2))
    number = ((place & (CAP - 1)) + 1).astype(F32)
    for i, hit in enumerate(hits):
        count = jnp.dot(
            jnp.broadcast_to(hit, (ROWS, SLAB)).astype(BF16), earlier, preferred_element_type=F32
        )[:1]
        count = jnp.where(hit > 0.5, count, 0.0)
        named = jnp.logical_and(place >> 2 == row >> 3, count == number)
        pickers_ref[i * slots : (i + 1) * slots, :] = jnp.where(named, 1.0, 0.0).astype(BF16)


def project_kernel(place_ref, hidden_ref, *refs):
    contexts, (weights_hbm, keep_ref, send_ref, weights, sems) = refs[:RING], refs[RING:]
    xl, xh, z = place_ref[0], place_ref[3], place_ref[4]

    def copy(k):
        at = pl.ds(pl.multiple_of(k * 2 * 128, 2 * 128), 2 * 128)
        return pltpu.make_async_copy(
            weights_hbm.at[at, pl.ds(2 * HIDDEN, HEADS_WIDE)], weights.at[at], sems.at[k]
        )

    blocks = [(z + (RING + RING // 2 - step)) & (RING - 1) for step in STEPS]
    for block in blocks:
        copy(block).start()
    for block in blocks:
        copy(block).wait()
    total = jnp.zeros((2 * SLAB, COLS), F32)
    for k in range(RING):
        context = contexts[k][...]
        first = pl.multiple_of(blocks[k] * 256, 256)
        for half in range(2):
            lanes = slice(half * 256, half * 256 + 256)
            block = weights[pl.ds(first, 256), lanes]
            rhs = jnp.concatenate(
                [
                    jnp.concatenate([block[:128, q * 128 : (q + 1) * 128], block[128:, q * 128 : (q + 1) * 128]], axis=1)
                    for q in range(2)
                ]
            )
            total += jnp.dot(context[:, lanes], rhs, preferred_element_type=F32)
    hidden = hidden_ref[...].astype(F32)
    rows = SLAB // 2
    own = jnp.where(xl == 0, hidden[:rows], hidden[rows:])
    other = jnp.where(xl == 0, hidden[rows:], hidden[:rows])
    total += jnp.concatenate(
        [jnp.where(xh == at, block, 0.0) for block in (own, other) for at in range(2)]
    )
    keep_ref[...] = total
    send_ref[...] = total.astype(BF16)


def residual_kernel(place_ref, keep_ref, recv_ref, pickers_ref, residual_ref, rows_ref):
    xl, xh = place_ref[0], place_ref[3]
    summed = keep_ref[...] + recv_ref[...].astype(F32)
    own, other = summed[:SLAB], summed[SLAB:]
    per_expert = BLOCKS * CAP
    held = jnp.zeros((SLAB, COLS), F32)
    for slab in range(2):
        at = slice(slab * SLAB, (slab + 1) * SLAB)
        residual = jnp.where(xl == slab, own, other).astype(BF16)
        held = jnp.where(xh == slab, residual.astype(F32), held)
        picked = jnp.dot(pickers_ref[at, :], residual, preferred_element_type=F32).astype(BF16)
        for f in range(FLIGHT // 2):
            for j in range(GROUP):
                to = ((f * GROUP + j) * 2 + slab) * per_expert
                rows_ref[to : to + per_expert, :] = picked[f * per_expert : (f + 1) * per_expert]
    residual_ref[...] = held.astype(BF16)


def gate_up_kernel(rows_ref, gain_ref, weights_hbm, own_ref, send_ref, weights, sems):
    part = HALF // RING

    def copy(k):
        at = pl.ds(k * part, part)
        return pltpu.make_async_copy(
            weights_hbm.at[at, pl.ds(0, 2 * HIDDEN)], weights.at[at], sems.at[k]
        )

    for k in range(RING):
        copy(k).start()
    slots = BLOCKS * CAP
    total = jnp.zeros((2 * slots, 2 * HIDDEN), F32)
    squares = jnp.zeros((2 * slots, 1), F32)
    for k in range(RING):
        rows = rows_ref[2 * k * slots : 2 * (k + 1) * slots, :].astype(F32)
        squares += jnp.sum(rows * rows, axis=1, keepdims=True)
        scaled = (rows * gain_ref[:, k * part : (k + 1) * part].astype(F32)).astype(BF16)
        copy(k).wait()
        total += jnp.dot(scaled, weights[k * part : (k + 1) * part, :], preferred_element_type=F32)
    own_ref[:, : 2 * HIDDEN] = total
    own_ref[:, 2 * HIDDEN :] = jnp.broadcast_to(squares, (2 * slots, 128))
    send_ref[:, : 2 * HIDDEN] = total.astype(BF16)
    high = squares.astype(BF16)
    rest = squares - high.astype(F32)
    middle = rest.astype(BF16)
    low = (rest - middle.astype(F32)).astype(BF16)
    lane = lax.broadcasted_iota(jnp.int32, (2 * slots, 128), 1)
    tail = jnp.where(lane == 0, high.astype(F32), 0.0)
    tail = jnp.where(lane == 1, middle.astype(F32), tail)
    tail = jnp.where(lane == 2, low.astype(F32), tail)
    send_ref[:, 2 * HIDDEN :] = tail.astype(BF16)


def down_kernel(place_ref, own_ref, recv_ref, residual_ref, weights_hbm, out_ref, weights, sem):
    copy = pltpu.make_async_copy(weights_hbm, weights, sem)
    copy.start()
    xh = place_ref[3]
    slots = 2 * BLOCKS * CAP
    other = recv_ref[:, 2 * HIDDEN :].astype(F32)
    squares = own_ref[:, 2 * HIDDEN : 2 * HIDDEN + 1] + jnp.sum(other, axis=1, keepdims=True)
    inverse = lax.rsqrt(squares / (2 * HALF) + 1e-06)
    total = (own_ref[:, : 2 * HIDDEN] + recv_ref[:, : 2 * HIDDEN].astype(F32)) * inverse
    gate, up = total[:, :HIDDEN], total[:, HIDDEN:]
    activated = (gate / (1.0 + jnp.exp(-gate)) * up).astype(BF16)
    to = lax.broadcasted_iota(jnp.int32, (2 * slots, slots), 0)
    source = lax.broadcasted_iota(jnp.int32, (2 * slots, slots), 1)
    twice = jnp.where(source == (to >> 3) * CAP + (to & 3), 1.0, 0.0).astype(BF16)
    activated = jnp.dot(twice, activated, preferred_element_type=F32).astype(BF16)
    first = (lax.broadcasted_iota(jnp.int32, (2 * slots, COLS), 0) & 4) == 0

    def columns(d):
        rhs = jnp.concatenate(
            [
                jnp.concatenate(
                    [
                        weights[(2 * d + e) * 128 : (2 * d + e + 1) * 128, j * 128 : (j + 1) * 128]
                        for j in range(HIDDEN // 128)
                    ]
                )
                for e in range(2)
            ],
            axis=1,
        )
        return jnp.dot(activated, rhs, preferred_element_type=F32)

    copy.wait()
    chunks = QUARTER // COLS
    for d in range(chunks):
        out_ref[:, d * COLS : (d + 1) * COLS] = jnp.where(first, columns(d), columns(d + chunks)).astype(BF16)
    residual = residual_ref[...].astype(F32)
    out_ref[:SLAB, QUARTER:] = jnp.where(xh == 0, residual, 0.0).astype(BF16)
    out_ref[SLAB:, QUARTER:] = jnp.where(xh == 1, residual, 0.0).astype(BF16)


def combine_kernel(place_ref, coefs_ref, returned_ref, out_ref):
    xl = place_ref[0]
    coefs = coefs_ref[...]
    high = coefs.astype(BF16)
    rest = coefs - high.astype(F32)
    middle = rest.astype(BF16)
    low = (rest - middle.astype(F32)).astype(BF16)
    parts = jnp.concatenate([high, middle, low])
    rows, slots = 4 * ROWS, 2 * BLOCKS * ROWS
    chunks = QUARTER // COLS
    to = lax.broadcasted_iota(jnp.int32, (chunks * rows, slots), 0)
    source = lax.broadcasted_iota(jnp.int32, (chunks * rows, slots), 1)
    chunk, half, quarter, row = to >> 5, (to >> 4) & 1, (to >> 3) & 1, to & 7
    wanted = (half * BLOCKS + xl * RING + quarter * (RING // 2) + chunk) * ROWS + row
    picker = jnp.where(source == wanted, 1.0, 0.0).astype(BF16)
    residual = jnp.dot(picker, returned_ref[:, QUARTER:], preferred_element_type=F32)
    for k in range(chunks):
        sums = jnp.dot(parts, returned_ref[:, k * COLS : (k + 1) * COLS], preferred_element_type=F32)
        mixed = residual[k * rows : (k + 1) * rows] + sums[:rows] + (sums[rows : 2 * rows] + sums[2 * rows :])
        for q in range(4):
            out_ref[:, q * QUARTER + k * COLS : q * QUARTER + (k + 1) * COLS] = mixed[
                q * ROWS : (q + 1) * ROWS
            ].astype(BF16)


def per_device(
    hidden_rows,
    queries,
    keys,
    values,
    slab_start,
    out_weight,
    norm_gain,
    route_ids,
    route_weights,
    flight_experts,
    gate_weight,
    up_weight,
    down_weight,
):
    xl, xh = lax.axis_index("xl"), lax.axis_index("xh")
    tensor_idx = lax.axis_index(TENSOR)
    place = jnp.stack([lax.axis_index(a) for a in DP + TENSOR]).astype(jnp.int32)

    swapped = lax.ppermute(
        out_weight,
        ("y", "z"),
        [
            (a * RING + b, (2 * a - b + RING // 2) % RING * RING + a)
            for a in range(RING)
            for b in range(RING)
        ],
    )
    (context,) = kernel_call(
        attend_kernel,
        [((SLAB, HEADS_WIDE), BF16)],
        (slab_start, queries, keys, values),
        "shhh",
        4 * 512 * 1152 * 128,
        1 << 20,
        "attend",
        [
            pltpu.VMEM(queries.shape, BF16),
            pltpu.VMEM(keys.shape, BF16),
            pltpu.VMEM(values.shape, BF16),
            pltpu.SemaphoreType.DMA((3,)),
        ],
        vmem=ALL_VMEM_BYTES,
    )
    other = swap(context, "xl")
    both = jnp.concatenate([context, other])
    matches = route_ids[:, None, :] == flight_experts[None, :, None]
    hits = jnp.sum(matches.astype(jnp.int32), axis=2, dtype=jnp.int32)
    units = jnp.sum(jnp.where(matches, route_weights[:, None, :], 0), axis=2, dtype=jnp.int32)

    table = jnp.pad(hits.T.astype(BF16).reshape(2, COLS), ((0, ROWS - 2), (0, 0)))
    outgoing = jnp.concatenate(
        [hidden_rows.reshape(ROWS, BLOCKS, COLS).transpose(1, 0, 2), jnp.broadcast_to(table, (BLOCKS, ROWS, COLS))],
        axis=1,
    )
    gain = lax.dynamic_slice(norm_gain, (xl * HALF,), (HALF,)).reshape(1, HALF)
    (packed_down,) = kernel_call(
        pack_down_kernel, [((128, HIDDEN), BF16)], (down_weight,), "v", 0, 4 * 128 * 384, "pack_down"
    )
    (started,) = kernel_call(
        pack_gate_up_kernel,
        [((128, 2 * HIDDEN + HEADS_WIDE), BF16)],
        (gate_weight, up_weight),
        "hh",
        0,
        4 * 128 * 768,
        "pack_gate_up",
        [pltpu.VMEM((128, 2 * HIDDEN), BF16), pltpu.SemaphoreType.DMA((3,))],
        "h",
        MOST_VMEM_BYTES,
    )
    swapped, started, _ = lax.optimization_barrier((swapped, started, other))
    (packed,) = kernel_call(
        pack_out_kernel,
        [((128, 2 * HIDDEN + HEADS_WIDE), BF16)],
        (swapped, started),
        "hh",
        0,
        4 * 128 * 512,
        "pack_out",
        [pltpu.VMEM((HEADS_WIDE, 128), BF16)] + [pltpu.SemaphoreType.DMA((HEADS_WIDE // 128,))] * 2,
        "h",
        vmem=MOST_VMEM_BYTES,
        aliases={1: 0},
    )
    weights = lax.all_gather(packed, ("y", "core"), axis=0, tiled=True)
    packed_down, _ = lax.optimization_barrier((packed_down, packed))
    down_weights = lax.all_gather(packed_down, ("y", "core"), axis=0, tiled=True)
    up1, down1 = along_z(both, 1), along_z(both, -1)
    up2, down2 = along_z(up1, 1), along_z(down1, -1)
    up3, down3 = along_z(up2, 1), along_z(down2, -1)
    up4 = along_z(up3, 1)

    outgoing, _ = lax.optimization_barrier((outgoing, up1))
    incoming = lax.all_to_all(outgoing, ("xl", "z"), split_axis=0, concat_axis=0, tiled=True)
    hidden_in, pickers = kernel_call(
        unpack_kernel,
        [((SLAB, COLS), BF16), ((2 * (FLIGHT // 2) * BLOCKS * CAP, SLAB), BF16)],
        (place, incoming.reshape(2 * SLAB, COLS)),
        "sv",
        0,
        1 << 18,
        "unpack",
    )
    hits_mine = lax.dynamic_slice_in_dim(hits, tensor_idx * ROWS, ROWS, 0)
    coef = lax.dynamic_slice_in_dim(units, tensor_idx * ROWS, ROWS, 0).astype(F32) / 65536.0
    slot_mine = jnp.cumsum(hits_mine, axis=0) - 1
    mine = jnp.where(
        jnp.logical_and(
            hits_mine[..., None] == 1, slot_mine[..., None] == jnp.arange(CAP, dtype=jnp.int32)
        ),
        coef[..., None],
        0.0,
    )
    two = jnp.eye(2, dtype=F32)
    coefs = (
        mine[None, None, :, None, :, None, None, :]
        * two[:, None, None, :, None, None, None, None]
        * two[None, :, None, None, None, None, :, None]
    )
    coefs = jnp.broadcast_to(coefs, (2, 2, ROWS, 2, FLIGHT, GROUP, 2, CAP)).reshape(
        4 * ROWS, 2 * BLOCKS * 2 * CAP
    )
    weights, pickers, coefs, gain = lax.optimization_barrier((weights, pickers, coefs, gain))

    keep, send = kernel_call(
        project_kernel,
        [((2 * SLAB, COLS), F32), ((2 * SLAB, COLS), BF16)],
        (place, hidden_in, both, up1, down1, up2, down2, up3, down3, up4, weights),
        "sv" + "v" * RING + "h",
        2 * 256 * 4096 * 256,
        2 * 2048 * 1024,
        "project",
        [pltpu.VMEM((HALF, HEADS_WIDE), BF16), pltpu.SemaphoreType.DMA((RING,))],
    )
    residual, rows_out = kernel_call(
        residual_kernel,
        [((SLAB, COLS), BF16), ((RING * 2 * BLOCKS * CAP, COLS), BF16)],
        (place, keep, swap(send, "xh"), pickers),
        "svvv",
        2 * 256 * 128 * 256,
        1 << 20,
        "residual",
    )
    rows_in = lax.all_to_all(
        rows_out.reshape(RING, 2 * BLOCKS * CAP, COLS), "z", split_axis=0, concat_axis=0, tiled=True
    ).reshape(RING * 2 * BLOCKS * CAP, COLS)
    own, part = kernel_call(
        gate_up_kernel,
        [((2 * BLOCKS * CAP, 2 * HIDDEN + 128), F32), ((2 * BLOCKS * CAP, 2 * HIDDEN + 128), BF16)],
        (rows_in, gain, weights),
        "vvh",
        2 * 128 * 2048 * 768,
        3 << 20,
        "gate_up",
        [pltpu.VMEM((HALF, 2 * HIDDEN), BF16), pltpu.SemaphoreType.DMA((RING,))],
    )
    (outward,) = kernel_call(
        down_kernel,
        [((4 * BLOCKS * CAP, QUARTER + COLS), BF16)],
        (place, own, swap(part, "xl"), residual, down_weights),
        "svvvh",
        2 * 256 * 384 * 2048,
        2 << 20,
        "down",
        [pltpu.VMEM((HALF, HIDDEN), BF16), pltpu.SemaphoreType.DMA],
        vmem=DOWN_VMEM_BYTES,
    )
    returned = lax.all_to_all(
        outward.reshape(2 * BLOCKS, 2 * CAP, QUARTER + COLS),
        PAIR_TENSOR,
        split_axis=0,
        concat_axis=0,
        tiled=True,
    ).reshape(4 * BLOCKS * CAP, QUARTER + COLS)
    (mixed,) = kernel_call(
        combine_kernel,
        [((ROWS, 2 * HALF), BF16)],
        (place, coefs, returned),
        "svv",
        2 * 128 * 256 * 1024,
        1 << 20,
        "combine",
    )
    return mixed


def solution(mesh):
    fine = Mesh(mesh.devices.reshape(2, RING, 2, 2, RING), DP + TENSOR)
    placed = (
        P(DP + TENSOR, None),
        P(DP, TENSOR),
        P(DP, TENSOR),
        P(DP, TENSOR),
        P(DP),
        P(TENSOR, DP),
        P(),
        P(DP, None),
        P(DP, None),
        P(),
        P(DP, TENSOR),
        P(DP, TENSOR),
        P(TENSOR, DP),
    )
    return jax.shard_map(
        per_device, mesh=fine, in_specs=placed, out_specs=P(DP + TENSOR, None), check_vma=False
    )
```

```python
import jax
import jax.numpy as jnp
from jax import lax
from jax.experimental import pallas as pl
from jax.experimental.pallas import tpu as pltpu
from jax.sharding import Mesh
from jax.sharding import PartitionSpec as P

DP = ("xl", "y", "core")
TENSOR = ("xh", "z")
PAIR_TENSOR = ("xl",) + TENSOR
RING = 8
STEPS = (0, -1, 1, -2, 2, -3, 3, 4)
SLAB = 128
HALF = 2048
LEAST_START = 512
QUARTER = 1024
COLS = 256
HIDDEN = 384
HEADS_WIDE = 512
CAP = 4
FLIGHT = 4
GROUP = 4
BLOCKS = 16
ROWS = 8
VMEM_BYTES = 48 * 1024 * 1024
ALL_VMEM_BYTES = 63400000
MOST_VMEM_BYTES = 57000000
DOWN_VMEM_BYTES = 55000000
F32, BF16 = jnp.float32, jnp.bfloat16


def attend_kernel(
    start_ref, queries_hbm, keys_hbm, values_hbm, out_ref, queries_ref, keys_ref, values_ref, sems
):
    copies = [
        pltpu.make_async_copy(source, target, sems.at[i])
        for i, (source, target) in enumerate(
            ((keys_hbm, keys_ref), (queries_hbm, queries_ref), (values_hbm, values_ref))
        )
    ]
    for copy in copies:
        copy.start()
    for copy in copies[:2]:
        copy.wait()
    keys = keys_ref[...]
    size = keys.shape[1]
    heads = HEADS_WIDE // size
    shape = (heads * SLAB, keys.shape[0] - LEAST_START)
    position = start_ref[0] - LEAST_START + (lax.broadcasted_iota(jnp.int32, shape, 0) & (SLAB - 1))
    visible = lax.broadcasted_iota(jnp.int32, shape, 1) <= position
    block = jnp.concatenate([queries_ref[:, h * size : (h + 1) * size] for h in range(heads)])
    scores = lax.dot_general(
        block, keys, (((1,), (1,)), ((), ())), preferred_element_type=F32
    ) * size ** (-0.5)
    scores = jnp.concatenate(
        [scores[:, :LEAST_START], jnp.where(visible, scores[:, LEAST_START:], -1e30)], axis=1
    )
    exp_scores = jnp.exp(scores - jnp.max(scores, axis=1, keepdims=True))
    totals = jnp.sum(exp_scores, axis=1, keepdims=True)
    copies[2].wait()
    context = (jnp.dot(exp_scores.astype(BF16), values_ref[...], preferred_element_type=F32) / totals).astype(BF16)
    for h in range(heads):
        out_ref[:, h * size : (h + 1) * size] = context[h * SLAB : (h + 1) * SLAB]


def swap(block, axis):
    return lax.ppermute(block, axis, [(0, 1), (1, 0)])


def along_z(block, step):
    return lax.ppermute(block, "z", [(i, (i + step) % RING) for i in range(RING)])


def kernel_call(body, out_shapes, operands, spaces, flops, moved, name, scratch=(), out_space="v", vmem=VMEM_BYTES, aliases=None):
    kinds = {
        "v": pl.BlockSpec(memory_space=pltpu.VMEM),
        "s": pl.BlockSpec(memory_space=pltpu.SMEM),
        "h": pl.BlockSpec(memory_space=pl.ANY),
    }
    return pl.pallas_call(
        body,
        out_shape=[jax.ShapeDtypeStruct(shape, dtype) for shape, dtype in out_shapes],
        in_specs=[kinds[s] for s in spaces],
        out_specs=[kinds[out_space]] * len(out_shapes),
        scratch_shapes=list(scratch),
        input_output_aliases=aliases or {},
        compiler_params=pltpu.CompilerParams(vmem_limit_bytes=vmem),
        cost_estimate=pl.CostEstimate(flops=flops, bytes_accessed=moved, transcendentals=0),
        name=name,
    )(*operands)


def pack_gate_up_kernel(gate_hbm, up_hbm, packed_hbm, held, sems):
    copies = [
        pltpu.make_async_copy(source, held.at[:, pl.ds(i * HIDDEN, HIDDEN)], sems.at[i])
        for i, source in enumerate((gate_hbm, up_hbm))
    ]
    for copy in copies:
        copy.start()
    for copy in copies:
        copy.wait()
    whole = pltpu.make_async_copy(held, packed_hbm.at[:, pl.ds(0, 2 * HIDDEN)], sems.at[2])
    whole.start()
    whole.wait()


def pack_out_kernel(swapped_hbm, started_hbm, packed_hbm, held, in_sems, out_sems):
    arriving, leaving = [], []
    for j in range(HEADS_WIDE // 128):
        at = pl.ds(j * 128, 128)
        to = packed_hbm.at[:, pl.ds(2 * HIDDEN + j * 128, 128)]
        arriving.append(pltpu.make_async_copy(swapped_hbm.at[at], held.at[at], in_sems.at[j]))
        leaving.append(pltpu.make_async_copy(held.at[at], to, out_sems.at[j]))
    for copy in arriving:
        copy.start()
    for arrived, copy in zip(arriving, leaving):
        arrived.wait()
        copy.start()
    for copy in leaving:
        copy.wait()


def pack_down_kernel(down_ref, packed_ref):
    for j in range(HIDDEN // 128):
        packed_ref[:, j * 128 : (j + 1) * 128] = down_ref[j * 128 : (j + 1) * 128, :]


def unpack_kernel(place_ref, incoming_ref, hidden_ref, pickers_ref):
    xh = place_ref[3]
    shape = (SLAB, 2 * SLAB)
    to, source = (lax.broadcasted_iota(jnp.int32, shape, d) for d in range(2))
    taken = jnp.where(source == (to >> 3) * 2 * ROWS + (to & 7), 1.0, 0.0).astype(BF16)
    hidden_ref[...] = jnp.dot(taken, incoming_ref[...], preferred_element_type=F32).astype(BF16)
    line = lax.broadcasted_iota(jnp.int32, (2 * ROWS, COLS), 0)
    hits = []
    for slab in range(2):
        rows = incoming_ref[slab * SLAB : slab * SLAB + 2 * ROWS, :].astype(F32)
        both = jnp.sum(jnp.where(line == ROWS + xh, rows, 0.0), axis=0, keepdims=True)
        hits += [both[:, :SLAB], both[:, SLAB:]]
    above, row = (lax.broadcasted_iota(jnp.int32, (SLAB, SLAB), d) for d in range(2))
    earlier = jnp.where(jnp.logical_and(above >> 3 == row >> 3, above <= row), 1.0, 0.0).astype(BF16)
    slots = BLOCKS * CAP
    shape = (slots, SLAB)
    place, row = (lax.broadcasted_iota(jnp.int32, shape, d) for d in range(2))
    number = ((place & (CAP - 1)) + 1).astype(F32)
    for i, hit in enumerate(hits):
        count = jnp.dot(
            jnp.broadcast_to(hit, (ROWS, SLAB)).astype(BF16), earlier, preferred_element_type=F32
        )[:1]
        count = jnp.where(hit > 0.5, count, 0.0)
        named = jnp.logical_and(place >> 2 == row >> 3, count == number)
        pickers_ref[i * slots : (i + 1) * slots, :] = jnp.where(named, 1.0, 0.0).astype(BF16)


def project_kernel(place_ref, hidden_ref, *refs):
    contexts, (weights_hbm, keep_ref, send_ref, weights, sems) = refs[:RING], refs[RING:]
    xl, xh, z = place_ref[0], place_ref[3], place_ref[4]

    def copy(k):
        at = pl.ds(pl.multiple_of(k * 2 * 128, 2 * 128), 2 * 128)
        return pltpu.make_async_copy(
            weights_hbm.at[at, pl.ds(2 * HIDDEN, HEADS_WIDE)], weights.at[at], sems.at[k]
        )

    blocks = [(z + (RING + RING // 2 - step)) & (RING - 1) for step in STEPS]
    for block in blocks:
        copy(block).start()
    for block in blocks:
        copy(block).wait()
    total = jnp.zeros((2 * SLAB, COLS), F32)
    for k in range(RING):
        context = contexts[k][...]
        first = pl.multiple_of(blocks[k] * 256, 256)
        for half in range(2):
            lanes = slice(half * 256, half * 256 + 256)
            block = weights[pl.ds(first, 256), lanes]
            rhs = jnp.concatenate(
                [
                    jnp.concatenate([block[:128, q * 128 : (q + 1) * 128], block[128:, q * 128 : (q + 1) * 128]], axis=1)
                    for q in range(2)
                ]
            )
            total += jnp.dot(context[:, lanes], rhs, preferred_element_type=F32)
    hidden = hidden_ref[...].astype(F32)
    rows = SLAB // 2
    own = jnp.where(xl == 0, hidden[:rows], hidden[rows:])
    other = jnp.where(xl == 0, hidden[rows:], hidden[:rows])
    total += jnp.concatenate(
        [jnp.where(xh == at, block, 0.0) for block in (own, other) for at in range(2)]
    )
    keep_ref[...] = total
    send_ref[...] = total.astype(BF16)


def residual_kernel(place_ref, keep_ref, recv_ref, pickers_ref, residual_ref, rows_ref):
    xl, xh = place_ref[0], place_ref[3]
    summed = keep_ref[...] + recv_ref[...].astype(F32)
    own, other = summed[:SLAB], summed[SLAB:]
    per_expert = BLOCKS * CAP
    held = jnp.zeros((SLAB, COLS), F32)
    for slab in range(2):
        at = slice(slab * SLAB, (slab + 1) * SLAB)
        residual = jnp.where(xl == slab, own, other).astype(BF16)
        held = jnp.where(xh == slab, residual.astype(F32), held)
        picked = jnp.dot(pickers_ref[at, :], residual, preferred_element_type=F32).astype(BF16)
        for f in range(FLIGHT // 2):
            for j in range(GROUP):
                to = ((f * GROUP + j) * 2 + slab) * per_expert
                rows_ref[to : to + per_expert, :] = picked[f * per_expert : (f + 1) * per_expert]
    residual_ref[...] = held.astype(BF16)


def gate_up_kernel(rows_ref, gain_ref, weights_hbm, own_ref, send_ref, weights, sems):
    part = HALF // RING

    def copy(k):
        at = pl.ds(k * part, part)
        return pltpu.make_async_copy(
            weights_hbm.at[at, pl.ds(0, 2 * HIDDEN)], weights.at[at], sems.at[k]
        )

    for k in range(RING):
        copy(k).start()
    slots = BLOCKS * CAP
    total = jnp.zeros((2 * slots, 2 * HIDDEN), F32)
    squares = jnp.zeros((2 * slots, 1), F32)
    for k in range(RING):
        rows = rows_ref[2 * k * slots : 2 * (k + 1) * slots, :].astype(F32)
        squares += jnp.sum(rows * rows, axis=1, keepdims=True)
        scaled = (rows * gain_ref[:, k * part : (k + 1) * part].astype(F32)).astype(BF16)
        copy(k).wait()
        total += jnp.dot(scaled, weights[k * part : (k + 1) * part, :], preferred_element_type=F32)
    own_ref[:, : 2 * HIDDEN] = total
    own_ref[:, 2 * HIDDEN :] = jnp.broadcast_to(squares, (2 * slots, 128))
    send_ref[:, : 2 * HIDDEN] = total.astype(BF16)
    high = squares.astype(BF16)
    rest = squares - high.astype(F32)
    middle = rest.astype(BF16)
    low = (rest - middle.astype(F32)).astype(BF16)
    lane = lax.broadcasted_iota(jnp.int32, (2 * slots, 128), 1)
    tail = jnp.where(lane == 0, high.astype(F32), 0.0)
    tail = jnp.where(lane == 1, middle.astype(F32), tail)
    tail = jnp.where(lane == 2, low.astype(F32), tail)
    send_ref[:, 2 * HIDDEN :] = tail.astype(BF16)


def down_kernel(place_ref, own_ref, recv_ref, residual_ref, weights_hbm, out_ref, weights, sem):
    copy = pltpu.make_async_copy(weights_hbm, weights, sem)
    copy.start()
    xh = place_ref[3]
    slots = 2 * BLOCKS * CAP
    other = recv_ref[:, 2 * HIDDEN :].astype(F32)
    squares = own_ref[:, 2 * HIDDEN : 2 * HIDDEN + 1] + jnp.sum(other, axis=1, keepdims=True)
    inverse = lax.rsqrt(squares / (2 * HALF) + 1e-06)
    total = (own_ref[:, : 2 * HIDDEN] + recv_ref[:, : 2 * HIDDEN].astype(F32)) * inverse
    gate, up = total[:, :HIDDEN], total[:, HIDDEN:]
    activated = (gate / (1.0 + jnp.exp(-gate)) * up).astype(BF16)
    to = lax.broadcasted_iota(jnp.int32, (2 * slots, slots), 0)
    source = lax.broadcasted_iota(jnp.int32, (2 * slots, slots), 1)
    twice = jnp.where(source == (to >> 3) * CAP + (to & 3), 1.0, 0.0).astype(BF16)
    activated = jnp.dot(twice, activated, preferred_element_type=F32).astype(BF16)
    first = (lax.broadcasted_iota(jnp.int32, (2 * slots, COLS), 0) & 4) == 0

    def columns(d):
        rhs = jnp.concatenate(
            [
                jnp.concatenate(
                    [
                        weights[(2 * d + e) * 128 : (2 * d + e + 1) * 128, j * 128 : (j + 1) * 128]
                        for j in range(HIDDEN // 128)
                    ]
                )
                for e in range(2)
            ],
            axis=1,
        )
        return jnp.dot(activated, rhs, preferred_element_type=F32)

    copy.wait()
    chunks = QUARTER // COLS
    for d in range(chunks):
        out_ref[:, d * COLS : (d + 1) * COLS] = jnp.where(first, columns(d), columns(d + chunks)).astype(BF16)
    residual = residual_ref[...].astype(F32)
    out_ref[:SLAB, QUARTER:] = jnp.where(xh == 0, residual, 0.0).astype(BF16)
    out_ref[SLAB:, QUARTER:] = jnp.where(xh == 1, residual, 0.0).astype(BF16)


def combine_kernel(place_ref, coefs_ref, returned_ref, out_ref):
    xl = place_ref[0]
    coefs = coefs_ref[...]
    high = coefs.astype(BF16)
    rest = coefs - high.astype(F32)
    middle = rest.astype(BF16)
    low = (rest - middle.astype(F32)).astype(BF16)
    parts = jnp.concatenate([high, middle, low])
    rows, slots = 4 * ROWS, 2 * BLOCKS * ROWS
    chunks = QUARTER // COLS
    to = lax.broadcasted_iota(jnp.int32, (chunks * rows, slots), 0)
    source = lax.broadcasted_iota(jnp.int32, (chunks * rows, slots), 1)
    chunk, half, quarter, row = to >> 5, (to >> 4) & 1, (to >> 3) & 1, to & 7
    wanted = (half * BLOCKS + xl * RING + quarter * (RING // 2) + chunk) * ROWS + row
    picker = jnp.where(source == wanted, 1.0, 0.0).astype(BF16)
    residual = jnp.dot(picker, returned_ref[:, QUARTER:], preferred_element_type=F32)
    for k in range(chunks):
        sums = jnp.dot(parts, returned_ref[:, k * COLS : (k + 1) * COLS], preferred_element_type=F32)
        mixed = residual[k * rows : (k + 1) * rows] + sums[:rows] + (sums[rows : 2 * rows] + sums[2 * rows :])
        for q in range(4):
            out_ref[:, q * QUARTER + k * COLS : q * QUARTER + (k + 1) * COLS] = mixed[
                q * ROWS : (q + 1) * ROWS
            ].astype(BF16)


def per_device(
    hidden_rows,
    queries,
    keys,
    values,
    slab_start,
    out_weight,
    norm_gain,
    route_ids,
    route_weights,
    flight_experts,
    gate_weight,
    up_weight,
    down_weight,
):
    xl, xh = lax.axis_index("xl"), lax.axis_index("xh")
    tensor_idx = lax.axis_index(TENSOR)
    place = jnp.stack([lax.axis_index(a) for a in DP + TENSOR]).astype(jnp.int32)

    swapped = lax.ppermute(
        out_weight,
        ("y", "z"),
        [
            (a * RING + b, (2 * a - b + RING // 2) % RING * RING + a)
            for a in range(RING)
            for b in range(RING)
        ],
    )
    (context,) = kernel_call(
        attend_kernel,
        [((SLAB, HEADS_WIDE), BF16)],
        (slab_start, queries, keys, values),
        "shhh",
        4 * 512 * 1152 * 128,
        1 << 20,
        "attend",
        [
            pltpu.VMEM(queries.shape, BF16),
            pltpu.VMEM(keys.shape, BF16),
            pltpu.VMEM(values.shape, BF16),
            pltpu.SemaphoreType.DMA((3,)),
        ],
        vmem=ALL_VMEM_BYTES,
    )
    other = swap(context, "xl")
    both = jnp.concatenate([context, other])
    matches = route_ids[:, None, :] == flight_experts[None, :, None]
    hits = jnp.sum(matches.astype(jnp.int32), axis=2, dtype=jnp.int32)
    units = jnp.sum(jnp.where(matches, route_weights[:, None, :], 0), axis=2, dtype=jnp.int32)

    table = jnp.pad(hits.T.astype(BF16).reshape(2, COLS), ((0, ROWS - 2), (0, 0)))
    outgoing = jnp.concatenate(
        [hidden_rows.reshape(ROWS, BLOCKS, COLS).transpose(1, 0, 2), jnp.broadcast_to(table, (BLOCKS, ROWS, COLS))],
        axis=1,
    )
    gain = lax.dynamic_slice(norm_gain, (xl * HALF,), (HALF,)).reshape(1, HALF)
    (packed_down,) = kernel_call(
        pack_down_kernel, [((128, HIDDEN), BF16)], (down_weight,), "v", 0, 4 * 128 * 384, "pack_down"
    )
    (started,) = kernel_call(
        pack_gate_up_kernel,
        [((128, 2 * HIDDEN + HEADS_WIDE), BF16)],
        (gate_weight, up_weight),
        "hh",
        0,
        4 * 128 * 768,
        "pack_gate_up",
        [pltpu.VMEM((128, 2 * HIDDEN), BF16), pltpu.SemaphoreType.DMA((3,))],
        "h",
        MOST_VMEM_BYTES,
    )
    swapped, started, _ = lax.optimization_barrier((swapped, started, other))
    (packed,) = kernel_call(
        pack_out_kernel,
        [((128, 2 * HIDDEN + HEADS_WIDE), BF16)],
        (swapped, started),
        "hh",
        0,
        4 * 128 * 512,
        "pack_out",
        [pltpu.VMEM((HEADS_WIDE, 128), BF16)] + [pltpu.SemaphoreType.DMA((HEADS_WIDE // 128,))] * 2,
        "h",
        vmem=MOST_VMEM_BYTES,
        aliases={1: 0},
    )
    weights = lax.all_gather(packed, ("y", "core"), axis=0, tiled=True)
    packed_down, _ = lax.optimization_barrier((packed_down, packed))
    down_weights = lax.all_gather(packed_down, ("y", "core"), axis=0, tiled=True)
    up1, down1 = along_z(both, 1), along_z(both, -1)
    up2, down2 = along_z(up1, 1), along_z(down1, -1)
    up3, down3 = along_z(up2, 1), along_z(down2, -1)
    up4 = along_z(up3, 1)

    outgoing, _ = lax.optimization_barrier((outgoing, up1))
    incoming = lax.all_to_all(outgoing, ("xl", "z"), split_axis=0, concat_axis=0, tiled=True)
    hidden_in, pickers = kernel_call(
        unpack_kernel,
        [((SLAB, COLS), BF16), ((2 * (FLIGHT // 2) * BLOCKS * CAP, SLAB), BF16)],
        (place, incoming.reshape(2 * SLAB, COLS)),
        "sv",
        0,
        1 << 18,
        "unpack",
    )
    hits_mine = lax.dynamic_slice_in_dim(hits, tensor_idx * ROWS, ROWS, 0)
    coef = lax.dynamic_slice_in_dim(units, tensor_idx * ROWS, ROWS, 0).astype(F32) / 65536.0
    slot_mine = jnp.cumsum(hits_mine, axis=0) - 1
    mine = jnp.where(
        jnp.logical_and(
            hits_mine[..., None] == 1, slot_mine[..., None] == jnp.arange(CAP, dtype=jnp.int32)
        ),
        coef[..., None],
        0.0,
    )
    two = jnp.eye(2, dtype=F32)
    coefs = (
        mine[None, None, :, None, :, None, None, :]
        * two[:, None, None, :, None, None, None, None]
        * two[None, :, None, None, None, None, :, None]
    )
    coefs = jnp.broadcast_to(coefs, (2, 2, ROWS, 2, FLIGHT, GROUP, 2, CAP)).reshape(
        4 * ROWS, 2 * BLOCKS * 2 * CAP
    )
    weights, pickers, coefs, gain = lax.optimization_barrier((weights, pickers, coefs, gain))

    keep, send = kernel_call(
        project_kernel,
        [((2 * SLAB, COLS), F32), ((2 * SLAB, COLS), BF16)],
        (place, hidden_in, both, up1, down1, up2, down2, up3, down3, up4, weights),
        "sv" + "v" * RING + "h",
        2 * 256 * 4096 * 256,
        2 * 2048 * 1024,
        "project",
        [pltpu.VMEM((HALF, HEADS_WIDE), BF16), pltpu.SemaphoreType.DMA((RING,))],
    )
    residual, rows_out = kernel_call(
        residual_kernel,
        [((SLAB, COLS), BF16), ((RING * 2 * BLOCKS * CAP, COLS), BF16)],
        (place, keep, swap(send, "xh"), pickers),
        "svvv",
        2 * 256 * 128 * 256,
        1 << 20,
        "residual",
    )
    rows_in = lax.all_to_all(
        rows_out.reshape(RING, 2 * BLOCKS * CAP, COLS), "z", split_axis=0, concat_axis=0, tiled=True
    ).reshape(RING * 2 * BLOCKS * CAP, COLS)
    own, part = kernel_call(
        gate_up_kernel,
        [((2 * BLOCKS * CAP, 2 * HIDDEN + 128), F32), ((2 * BLOCKS * CAP, 2 * HIDDEN + 128), BF16)],
        (rows_in, gain, weights),
        "vvh",
        2 * 128 * 2048 * 768,
        3 << 20,
        "gate_up",
        [pltpu.VMEM((HALF, 2 * HIDDEN), BF16), pltpu.SemaphoreType.DMA((RING,))],
    )
    (outward,) = kernel_call(
        down_kernel,
        [((4 * BLOCKS * CAP, QUARTER + COLS), BF16)],
        (place, own, swap(part, "xl"), residual, down_weights),
        "svvvh",
        2 * 256 * 384 * 2048,
        2 << 20,
        "down",
        [pltpu.VMEM((HALF, HIDDEN), BF16), pltpu.SemaphoreType.DMA],
        vmem=DOWN_VMEM_BYTES,
    )
    returned = lax.all_to_all(
        outward.reshape(2 * BLOCKS, 2 * CAP, QUARTER + COLS),
        PAIR_TENSOR,
        split_axis=0,
        concat_axis=0,
        tiled=True,
    ).reshape(4 * BLOCKS * CAP, QUARTER + COLS)
    (mixed,) = kernel_call(
        combine_kernel,
        [((ROWS, 2 * HALF), BF16)],
        (place, coefs, returned),
        "svv",
        2 * 128 * 256 * 1024,
        1 << 20,
        "combine",
    )
    return mixed


def solution(mesh):
    fine = Mesh(mesh.devices.reshape(2, RING, 2, 2, RING), DP + TENSOR)
    placed = (
        P(DP + TENSOR, None),
        P(DP, TENSOR),
        P(DP, TENSOR),
        P(DP, TENSOR),
        P(DP),
        P(TENSOR, DP),
        P(),
        P(DP, None),
        P(DP, None),
        P(),
        P(DP, TENSOR),
        P(DP, TENSOR),
        P(TENSOR, DP),
    )
    return jax.shard_map(
        per_device, mesh=fine, in_specs=placed, out_specs=P(DP + TENSOR, None), check_vma=False
    )
```
